32 devices in a mesh: feat: 16 (over z, x, core), dom: 2 (over y).
Axes of the slice: x: 2, y: 2, z: 4, core: 2. Of those that a mesh axis runs over, the one named last changes fastest.
Arguments:
- features: bfloat16 [16384, 1024], P('dom', 'feat'), may hold values from -6 to 6
- self_weight: bfloat16 [1024, 512], P('feat'), may hold values from -0.1875 to 0.1875
- neighbour_weight: bfloat16 [1024, 512], P('feat'), may hold values from -1.5 to 1.5
- cotangent: bfloat16 [16384, 512], P(('dom', 'feat')), may hold values from -0.1875 to 0.1875
- send_rows: int32 [2, 2, 256], replicated, may hold values from 0 to 8191
- send_count: int32 [2, 2], replicated, may hold values from 32 to 256, as said below
- tile_source: int32 [2, 64, 8], P('dom'), may hold values from 0 to 67
- tile_kind: int32 [2, 64, 8], P('dom'), may hold values from 0 to 63
- tile_patterns: bfloat16 [64, 128, 128], replicated, may hold values from 0.0099487305 to 1
Outputs:
- hidden: bfloat16 [16384, 512], P(('dom', 'feat'))
- grad_self: float32 [1024, 512], P('feat')
- grad_neighbour: float32 [1024, 512], P('feat')
The draws below stay inside these ranges and needn't reach their ends.
Inputs may be any that keep to these rules, and one draw needn't show every extreme that they name: `send_count`: one destination has 256 live slots from every owner.
All inputs are finite; a program needn't handle non-finite values.
Results may differ from the reference program's by a relative error of at most 0.005.
Values may be sent and summed in bfloat16 or wider, within the bound.
No kernel may reach another device: no remote copies, remote signals or barrier semaphores. Data moves between devices by JAX's collectives and lax.ppermute only.
A program may use at most 128 MiB of HBM per device.

```python
import math
import jax
import jax.numpy as jnp
from jax import lax

D_IN = 1024
HID = 512
TILE = 128
K = 8
NBANK = 64
CAP = 256
P_SIZE = 8192
NPART = 2
HALO = 512
NODES = 16384


def draw_send_count(key, part):
    base = jax.random.randint(jax.random.fold_in(key, 11), (NPART, NPART), CAP // 8, CAP + 1)
    full_dest = jax.random.randint(jax.random.fold_in(key, 13), (), 0, NPART)
    dests = jnp.arange(NPART, dtype=jnp.int32)
    full = jnp.broadcast_to(dests[None, :] == full_dest, (NPART, NPART))
    return jnp.where(full, CAP, base).astype(jnp.int32)


def with_ends(array, own_key, least, top_value):
    shape = array.shape
    place = [jax.random.randint(jax.random.fold_in(own_key, axis), (), 0, shape[axis]) for axis in range(len(shape))]
    array = array.at[tuple(place)].set(least)
    longest = shape.index(max(shape))
    place[longest] = (place[longest] + 1) % shape[longest]
    return array.at[tuple(place)].set(top_value)


def steps_of(own_key, extent, cuts, smallest, top_value):
    def one(axis_at, parts):
        steps = jax.random.uniform(jax.random.fold_in(jax.random.fold_in(own_key, 6), axis_at), (parts,), jnp.float32, smallest / len(cuts), top_value / len(cuts))
        return jnp.repeat(jnp.exp(steps), extent[axis_at] // parts).reshape((-1,) + (1,) * (len(extent) - axis_at - 1))

    factor_of = one(*cuts[0])
    for cut in cuts[1:]:
        factor_of = factor_of * one(*cut)
    return factor_of


def bell_draw(rng, dims, scale, reach, cuts=(), kind=jnp.bfloat16):
    result = jax.random.normal(rng, dims, jnp.float32) * scale
    if len(cuts) > 0:
        result = steps_of(rng, dims, cuts, -0.22, 0.18) * result
    return jnp.clip(result, min=-reach, max=reach).astype(kind)


def setup_inputs(seed: int = 0) -> dict:
    streams_of = jax.random.split(jax.random.key(seed), 10)
    features = bell_draw(streams_of[0], (NODES, D_IN), 1.0, 6.0, ((0, 2), (1, 16)))
    self_weight = bell_draw(streams_of[1], (D_IN, HID), D_IN ** -0.5, 0.1875, ((0, 16),))
    neighbour_weight = bell_draw(streams_of[2], (D_IN, HID), 0.25, 1.5, ((0, 16),))
    cotangent = bell_draw(streams_of[3], (NODES, HID), (NODES // 16) ** -0.5, 0.1875, ((0, 32),))
    send_rows = with_ends(jax.random.randint(streams_of[4], (NPART, NPART, CAP), 0, P_SIZE), jax.random.fold_in(streams_of[4], 1), 0, P_SIZE - 1).astype(jnp.int32)
    send_count = draw_send_count(jax.random.fold_in(streams_of[9], 71), 0)
    tile_source = with_ends(jax.random.randint(streams_of[6], (NPART, P_SIZE // TILE, K), 0, (P_SIZE + HALO) // TILE), jax.random.fold_in(streams_of[6], 1), 0, ((P_SIZE + HALO) // TILE) - 1).astype(jnp.int32)
    tile_kind = with_ends(jax.random.randint(streams_of[7], (NPART, P_SIZE // TILE, K), 0, NBANK), jax.random.fold_in(streams_of[7], 1), 0, NBANK - 1).astype(jnp.int32)
    tile_patterns = jnp.clip(jnp.exp(jax.random.uniform(streams_of[8], (NBANK, TILE, TILE), jnp.float32, math.log(0.0099487305), math.log(1.0))), 0.0099487305, 1.0).astype(jnp.bfloat16)
    return dict(features=features, self_weight=self_weight, neighbour_weight=neighbour_weight, cotangent=cotangent, send_rows=send_rows, send_count=send_count, tile_source=tile_source, tile_kind=tile_kind, tile_patterns=tile_patterns)


inv_root_two = 0.7071067811865476
inv_root_two_pi = 0.3989422804014327


def gelu_pair(linear):
    normal_cdf = 0.5 * (1.0 + jax.scipy.special.erf(linear * inv_root_two))
    density = jnp.exp(-0.5 * linear * linear) * inv_root_two_pi
    return linear * normal_cdf, normal_cdf + linear * density


def partition_mean(features, send_rows, send_count, tile_source, tile_kind, tile_patterns, part_index):
    owners = jnp.arange(NPART, dtype=jnp.int32)
    wanted = send_rows[:, part_index, :]
    flat_ids = (owners[:, None] * P_SIZE + wanted).reshape(-1).astype(jnp.int32)
    live_mask = (jnp.arange(CAP, dtype=jnp.int32)[None, :] < send_count[:, part_index][:, None]).reshape(-1)
    halo = jnp.where(live_mask[:, None], features[flat_ids], jnp.zeros((), jnp.bfloat16))
    local_rows = lax.dynamic_slice_in_dim(features, part_index * P_SIZE, P_SIZE, 0)
    extended = jnp.concatenate([local_rows, halo], 0).reshape(-1, TILE, D_IN)
    tile_mats = tile_patterns[tile_kind[part_index]].astype(jnp.float32)
    sources = extended[tile_source[part_index]].astype(jnp.float32)
    summed = jnp.einsum("tkab,tkbf->taf", tile_mats, sources)
    degree = jnp.sum(tile_mats, axis=(1, 3))
    return (summed / degree[:, :, None]).reshape(P_SIZE, D_IN).astype(jnp.bfloat16)


def reference(features, self_weight, neighbour_weight, cotangent, send_rows, send_count, tile_source, tile_kind, tile_patterns):
    pieces = []
    for part_index in range(NPART):
        pieces.append(partition_mean(features, send_rows, send_count, tile_source, tile_kind, tile_patterns, part_index))
    neighbour_mean = jnp.concatenate(pieces, 0)
    linear = jnp.dot(features, self_weight, preferred_element_type=jnp.float32) + jnp.dot(neighbour_mean, neighbour_weight, preferred_element_type=jnp.float32)
    gelu_value, gelu_slope = gelu_pair(linear)
    hidden = gelu_value.astype(jnp.bfloat16)
    grad_linear = (cotangent.astype(jnp.float32) * gelu_slope).astype(jnp.bfloat16)
    grad_self = jnp.dot(features.T, grad_linear, preferred_element_type=jnp.float32)
    grad_neighbour = jnp.dot(neighbour_mean.T, grad_linear, preferred_element_type=jnp.float32)
    return hidden, grad_self, grad_neighbour
```

```python
import functools

import jax
import jax.numpy as jnp
from jax import lax
from jax.experimental import pallas as pl
from jax.experimental.pallas import tpu as pltpu
from jax.sharding import PartitionSpec as P

inv_root_two = 0.7071067811865476
inv_root_two_pi = 0.3989422804014327
bf16 = jnp.bfloat16
f32 = jnp.float32
vmem_bytes = 48 * 2**20
whole_vmem = pl.BlockSpec(memory_space=pltpu.VMEM)
whole_smem = pl.BlockSpec(memory_space=pltpu.SMEM)
last_with_last = (((1,), (1,)), ((), ()))
first_with_first = (((0,), (0,)), ((), ()))


def gelu_pair(linear):
    normal_cdf = 0.5 * (1.0 + lax.erf(linear * inv_root_two))
    density = jnp.exp(-0.5 * linear * linear) * inv_root_two_pi
    return (linear * normal_cdf, normal_cdf + linear * density)


def flip(axis, bit):
    size = lax.axis_size(axis)
    return functools.partial(
        lax.ppermute, axis_name=axis, perm=[(i, i ^ bit) for i in range(size)]
    )


def bits_of(size):
    return [1 << i for i in range(size.bit_length() - 1)]


def pick_kernel(step, columns_ref, rows_ref, picked_ref):
    total = jnp.zeros(picked_ref.shape, f32)
    for at in range(0, columns_ref.shape[1], step):
        ids = lax.broadcasted_iota(jnp.int32, (step, rows_ref.shape[1]), 0) + at
        one_hot = jnp.where(ids == rows_ref[...], 1.0, 0.0).astype(bf16)
        total = total + jnp.dot(
            columns_ref[:, at : at + step], one_hot, preferred_element_type=f32
        )
    picked_ref[...] = total.astype(bf16)


def pick_rows(columns, rows):
    depth, width = columns.shape[0], rows.shape[1]
    return pl.pallas_call(
        functools.partial(pick_kernel, min(256, columns.shape[1])),
        out_shape=jax.ShapeDtypeStruct((depth, width), bf16),
        in_specs=[whole_vmem, whole_vmem],
        out_specs=whole_vmem,
        cost_estimate=pl.CostEstimate(
            flops=2 * columns.size * width, bytes_accessed=2 * columns.size, transcendentals=0
        ),
        compiler_params=pltpu.CompilerParams(vmem_limit_bytes=vmem_bytes),
        name="pick_rows",
    )(columns, rows)


def mean_kernel(unroll, source_ref, kind_ref, local_ref, halo_ref, pattern_ref, mean_ref, tiles):
    depth = local_ref.shape[0]
    side = pattern_ref.shape[1]
    local_tiles, halo_tiles = local_ref.shape[1] // side, halo_ref.shape[1] // side
    for i in range(local_tiles):
        tiles[i, 0:depth, :] = local_ref[:, i * side : (i + 1) * side]
    for i in range(halo_tiles):
        tiles[local_tiles + i, 0:depth, :] = halo_ref[:, i * side : (i + 1) * side]
    tiles[:, depth:, :] = jnp.ones((tiles.shape[0], tiles.shape[1] - depth, side), bf16)
    per_block = mean_ref.shape[2] // side

    def one(t):
        rows = [tiles[source_ref[k, t]] for k in range(source_ref.shape[0])]
        weights = [pattern_ref[kind_ref[k, t]] for k in range(source_ref.shape[0])]
        summed = lax.dot_general(
            jnp.concatenate(rows, 1),
            jnp.concatenate(weights, 1),
            last_with_last,
            preferred_element_type=f32,
        )
        mean = (summed[0:depth] / summed[depth : depth + 1]).astype(bf16)
        at = lax.rem(t, per_block) * side
        mean_ref[lax.div(t, per_block), :, pl.ds(pl.multiple_of(at, side), side)] = mean

    @pl.loop(0, source_ref.shape[1] // unroll)
    def _(step):
        for u in range(unroll):
            one(step * unroll + u)


def neighbour_means(source, kind, local, halo, patterns, blocks):
    depth, count = local.shape
    side = patterns.shape[1]
    tile_count = (count + halo.shape[1]) // side
    dest = source.shape[1]
    flops = 2 * source.size * side * side * depth
    return pl.pallas_call(
        functools.partial(mean_kernel, 4 if dest % 4 == 0 else 1),
        out_shape=jax.ShapeDtypeStruct((blocks, depth, count // blocks), bf16),
        in_specs=[whole_smem, whole_smem, whole_vmem, whole_vmem, whole_vmem],
        out_specs=whole_vmem,
        scratch_shapes=[pltpu.VMEM((tile_count, depth + 16, side), bf16)],
        cost_estimate=pl.CostEstimate(
            flops=8 * flops, bytes_accessed=2 * (patterns.size + 2 * local.size), transcendentals=0
        ),
        compiler_params=pltpu.CompilerParams(vmem_limit_bytes=vmem_bytes),
        name="neighbour_means",
    )(source, kind, local, halo, patterns)


def gather_weights(weights):
    size = lax.axis_size("feat")
    me = lax.axis_index("feat")
    held = weights
    for place, bit in enumerate(reversed(bits_of(size))):
        other = flip("feat", bit)(held)
        upper = (me & bit) != 0
        held = jnp.stack(
            [jnp.where(upper, other, held), jnp.where(upper, held, other)], axis=place
        )
    return held.reshape((size,) + weights.shape)


def halve(parts, axis_name, bit, axis):
    mine = (lax.axis_index(axis_name) & bit) // bit
    sent = lax.dynamic_index_in_dim(parts, 1 - mine, axis, keepdims=False)
    kept = lax.dynamic_index_in_dim(parts, mine, axis, keepdims=False)
    return kept.astype(f32) + flip(axis_name, bit)(sent.astype(bf16)).astype(f32)


def reduce_gradients(parts):
    feat, dom = lax.axis_size("feat"), lax.axis_size("dom")
    rows, cols = parts.shape[2:]
    cores, rest = 2, feat // 2
    near = min(4, rest)
    far = rest // near
    parts = halve(parts.reshape(rest, cores, dom, rows, cols), "feat", 1, 1)
    parts = parts.astype(bf16).reshape(far, near, dom, rows, cols)
    blocks = jnp.transpose(parts, (2, 1, 0, 3, 4)).reshape(dom * near, far, rows, cols)
    groups = [
        [d * feat + (h * near + n) * cores + c for d in range(dom) for n in range(near)]
        for h in range(far)
        for c in range(cores)
    ]
    blocks = lax.all_to_all(
        blocks, ("dom", "feat"), 0, 0, axis_index_groups=groups, tiled=True
    )
    total = jnp.sum(blocks.astype(f32), axis=0)
    for place, bit in enumerate(reversed(bits_of(far))):
        total = halve(
            total.reshape((2, -1) + total.shape[1:]), "feat", bit * near * cores, 0
        )
    total = total.reshape(rows, cols)
    me = lax.axis_index("dom")
    if dom == 2:
        other = flip("dom", 1)(total)
        return jnp.stack([jnp.where(me == 0, total, other), jnp.where(me == 0, other, total)])
    return lax.all_gather(total, "dom", axis=0)


def on_device(
    features,
    self_weight,
    neighbour_weight,
    cotangent,
    send_rows,
    send_count,
    tile_source,
    tile_kind,
    tile_patterns,
):
    feat, dom = lax.axis_size("feat"), lax.axis_size("dom")
    my_part = lax.axis_index("dom")
    count, depth = features.shape
    rows = count // feat
    hid = self_weight.shape[1]
    slots = send_rows.shape[2]
    columns = features.T
    own_features = lax.all_to_all(
        jnp.transpose(columns.reshape(depth, feat, rows), (1, 0, 2)), "feat", 0, 0, tiled=True
    )
    outgoing = lax.dynamic_index_in_dim(send_rows, my_part, 0, keepdims=False)
    live = lax.dynamic_index_in_dim(send_count, my_part, 0, keepdims=False)
    slot_ids = jnp.arange(slots, dtype=jnp.int32)
    outgoing = jnp.where(slot_ids[None, :] < live[:, None], outgoing, -1)
    picked = pick_rows(columns, outgoing.reshape(1, dom * slots))
    if dom == 2:
        to_me = lax.dynamic_slice_in_dim(picked, my_part * slots, slots, 1)
        to_other = lax.dynamic_slice_in_dim(picked, (1 - my_part) * slots, slots, 1)
        got = flip("dom", 1)(to_other)
        first = my_part == 0
        halo = jnp.concatenate(
            [jnp.where(first, to_me, got), jnp.where(first, got, to_me)], axis=1
        )
    else:
        halo = lax.all_to_all(picked, "dom", 1, 1, tiled=True)
    own_mean = lax.all_to_all(
        neighbour_means(tile_source[0].T, tile_kind[0].T, columns, halo, tile_patterns, feat),
        "feat",
        0,
        0,
        tiled=True,
    )
    weights = gather_weights(jnp.stack([self_weight, neighbour_weight]))
    own_features = own_features.reshape(feat * depth, rows)
    own_mean = own_mean.reshape(feat * depth, rows)
    linear = lax.dot_general(
        own_features,
        weights[:, 0].reshape(feat * depth, hid),
        first_with_first,
        preferred_element_type=f32,
    ) + lax.dot_general(
        own_mean,
        weights[:, 1].reshape(feat * depth, hid),
        first_with_first,
        preferred_element_type=f32,
    )
    gelu_value, gelu_slope = gelu_pair(linear)
    hidden = gelu_value.astype(bf16)
    grad_linear = (cotangent.astype(f32) * gelu_slope).astype(bf16)
    self_part = jnp.dot(own_features, grad_linear, preferred_element_type=f32)
    neigh_part = jnp.dot(own_mean, grad_linear, preferred_element_type=f32)
    both = jnp.stack(
        [self_part.reshape(feat, depth, hid), neigh_part.reshape(feat, depth, hid)], axis=1
    )
    split = dom // 2 if dom > 2 else 1
    both = both.reshape(feat, 2 * split, depth // split, hid)
    grads = reduce_gradients(both).reshape(2, depth, hid)
    return (hidden, grads[0], grads[1])


def solution(mesh):
    placed = (
        P("dom", "feat"),
        P("feat", None),
        P("feat", None),
        P(("dom", "feat"), None),
        P(),
        P(),
        P("dom", None, None),
        P("dom", None, None),
        P(),
    )
    return jax.shard_map(
        on_device,
        mesh=mesh,
        in_specs=placed,
        out_specs=(P(("dom", "feat"), None), P("feat", None), P("feat", None)),
        check_vma=False,
    )
```

```python
import functools

import jax
import jax.numpy as jnp
from jax import lax
from jax.experimental import pallas as pl
from jax.experimental.pallas import tpu as pltpu
from jax.sharding import PartitionSpec as P

inv_root_two = 0.7071067811865476
inv_root_two_pi = 0.3989422804014327
bf16 = jnp.bfloat16
f32 = jnp.float32
vmem_bytes = 48 * 2**20
whole_vmem = pl.BlockSpec(memory_space=pltpu.VMEM)
whole_smem = pl.BlockSpec(memory_space=pltpu.SMEM)
last_with_last = (((1,), (1,)), ((), ()))
first_with_first = (((0,), (0,)), ((), ()))


def gelu_pair(linear):
    normal_cdf = 0.5 * (1.0 + lax.erf(linear * inv_root_two))
    density = jnp.exp(-0.5 * linear * linear) * inv_root_two_pi
    return (linear * normal_cdf, normal_cdf + linear * density)


def flip(axis, bit):
    size = lax.axis_size(axis)
    return functools.partial(
        lax.ppermute, axis_name=axis, perm=[(i, i ^ bit) for i in range(size)]
    )


def bits_of(size):
    return [1 << i for i in range(size.bit_length() - 1)]


def local_call(kernel, name, outs, operands, scalars=0, scratch=(), flops=0):
    moved = sum(2 * x.size for x in operands)
    return pl.pallas_call(
        kernel,
        out_shape=outs,
        in_specs=[whole_smem] * scalars + [whole_vmem] * (len(operands) - scalars),
        out_specs=[whole_vmem] * len(outs),
        scratch_shapes=list(scratch),
        cost_estimate=pl.CostEstimate(flops=flops, bytes_accessed=moved, transcendentals=0),
        compiler_params=pltpu.CompilerParams(vmem_limit_bytes=vmem_bytes),
        name=name,
    )(*operands)


def pick_kernel(step, me_ref, columns_ref, rows_ref, picked_ref, *cut_refs):
    total = jnp.zeros(picked_ref.shape, f32)
    for at in range(0, columns_ref.shape[1], step):
        ids = lax.broadcasted_iota(jnp.int32, (step, rows_ref.shape[1]), 0) + at
        one_hot = jnp.where(ids == rows_ref[...], 1.0, 0.0).astype(bf16)
        total = total + jnp.dot(
            columns_ref[:, at : at + step], one_hot, preferred_element_type=f32
        )
    picked_ref[...] = total.astype(bf16)
    for i, cut_ref in enumerate(cut_refs):
        width = cut_ref.shape[2]
        at = pl.multiple_of((me_ref[0] ^ (i + 1)) * width, width)
        cut_ref[0] = columns_ref[:, pl.ds(at, width)]


def pick_rows(quarter, columns, rows, quarters):
    depth, width = columns.shape[0], rows.shape[1]
    cut = jax.ShapeDtypeStruct((1, depth, columns.shape[1] // quarters), bf16)
    return local_call(
        functools.partial(pick_kernel, min(256, columns.shape[1])),
        "pick_rows",
        [jax.ShapeDtypeStruct((depth, width), bf16)] + [cut] * (quarters - 1),
        (quarter, columns, rows),
        scalars=1,
    )


def mean_kernel(unroll, source_ref, kind_ref, local_ref, halo_ref, pattern_ref, mean_ref, tiles):
    depth = local_ref.shape[0]
    side = pattern_ref.shape[1]
    local_tiles, halo_tiles = local_ref.shape[1] // side, halo_ref.shape[1] // side
    for i in range(local_tiles):
        tiles[i, 0:depth, :] = local_ref[:, i * side : (i + 1) * side]
    for i in range(halo_tiles):
        tiles[local_tiles + i, 0:depth, :] = halo_ref[:, i * side : (i + 1) * side]
    tiles[:, depth:, :] = jnp.ones((tiles.shape[0], tiles.shape[1] - depth, side), bf16)
    per_block = mean_ref.shape[2] // side

    def one(t):
        rows = [tiles[source_ref[k, t]] for k in range(source_ref.shape[0])]
        weights = [pattern_ref[kind_ref[k, t]] for k in range(source_ref.shape[0])]
        summed = lax.dot_general(
            jnp.concatenate(rows, 1),
            jnp.concatenate(weights, 1),
            last_with_last,
            preferred_element_type=f32,
        )
        mean = (summed[0:depth] / summed[depth : depth + 1]).astype(bf16)
        at = lax.rem(t, per_block) * side
        mean_ref[lax.div(t, per_block), :, pl.ds(pl.multiple_of(at, side), side)] = mean

    @pl.loop(0, source_ref.shape[1] // unroll)
    def _(step):
        for u in range(unroll):
            one(step * unroll + u)


def neighbour_means(source, kind, local, halo, patterns, blocks):
    depth, count = local.shape
    side = patterns.shape[1]
    tile_count = (count + halo.shape[1]) // side
    return local_call(
        functools.partial(mean_kernel, 4 if source.shape[1] % 4 == 0 else 1),
        "neighbour_means",
        [jax.ShapeDtypeStruct((blocks, depth, count // blocks), bf16)],
        (source, kind, local, halo, patterns),
        scalars=2,
        scratch=[pltpu.VMEM((tile_count, depth + 16, side), bf16)],
        flops=2 * source.size * side * side * depth,
    )[0]


def cut_kernel(bit_ref, *refs):
    sent_ref, kept_ref = refs[-2:]
    half = sent_ref.shape[2]
    mine = pl.multiple_of(bit_ref[0] * half, half)
    theirs = pl.multiple_of((1 - bit_ref[0]) * half, half)
    at = 0
    for ref in refs[:-2]:
        for i in range(ref.shape[0]):
            sent_ref[at] = ref[i, :, pl.ds(theirs, half)]
            kept_ref[at] = ref[i, :, pl.ds(mine, half)]
            at += 1


def cut_rows(bit, parts):
    count = sum(p.shape[0] for p in parts)
    out = jax.ShapeDtypeStruct((count, parts[0].shape[1], parts[0].shape[2] // 2), bf16)
    return local_call(cut_kernel, "cut_rows", [out, out], (bit, *parts), scalars=1)


def masks_of(first, later):
    masks = list(first)
    for bit in later:
        masks = masks + [m ^ bit for m in masks]
    return masks


def own_linear_kernel(row_masks, weight_masks, me_ref, *refs):
    kept_ref, got_ref, held_ref, came_ref, features_ref, weights_ref, linear_ref, own_ref = refs
    half = kept_ref.shape[0]
    for i, mask in enumerate(row_masks):
        part = kept_ref[i] if i < half else got_ref[i - half]
        features_ref[me_ref[0] ^ mask] = part
    half = held_ref.shape[0]
    for i, mask in enumerate(weight_masks):
        part = held_ref if i < half else came_ref
        own_ref[me_ref[0] ^ mask] = part[i % half, 0]
        weights_ref[me_ref[0] ^ mask] = part[i % half, 1]
    linear_ref[...] = lax.dot_general(
        features_ref[...].reshape(-1, features_ref.shape[2]),
        own_ref[...].reshape(-1, own_ref.shape[2]),
        first_with_first,
        preferred_element_type=f32,
    )


def forward_kernel(
    core_ref, linear_ref, weight_ref, mean_ref, features_ref, cot_ref, hidden_ref, grad_ref, sent_ref
):
    rows, hid = linear_ref.shape
    step = min(256, rows)
    weight = weight_ref[...].reshape(-1, hid)
    for at in range(0, rows, step):
        mean = mean_ref[:, :, :, at : at + step].reshape(-1, step)
        linear = linear_ref[at : at + step] + lax.dot_general(
            mean, weight, first_with_first, preferred_element_type=f32
        )
        value, slope = gelu_pair(linear)
        hidden_ref[at : at + step] = value.astype(bf16)
        grad_ref[at : at + step] = (cot_ref[at : at + step].astype(f32) * slope).astype(bf16)
    partial_gradients(1 - core_ref[0], features_ref, mean_ref, grad_ref, sent_ref)


def partial_gradients(core, features_ref, mean_ref, grad_ref, out_ref):
    for i, ref in enumerate((features_ref, mean_ref)):
        part = jnp.dot(
            ref[:, core].reshape(-1, ref.shape[3]), grad_ref[...], preferred_element_type=f32
        )
        out_ref[:, i] = part.astype(out_ref.dtype).reshape(out_ref[:, i].shape)


def kept_kernel(core_ref, features_ref, mean_ref, grad_ref, kept_ref):
    partial_gradients(core_ref[0], features_ref, mean_ref, grad_ref, kept_ref)


def first_kernel(bits_ref, kept_ref, got_ref, own_ref, own_sent_ref, neigh_ref, neigh_sent_ref):
    for far in range(kept_ref.shape[0] // 4):
        for a in range(2):
            for b in range(2):
                at = far * 4 + (bits_ref[1] ^ a) * 2 + (bits_ref[0] ^ b)
                own = kept_ref[at, 0] + got_ref[at, 0].astype(f32)
                neigh = kept_ref[at, 1] + got_ref[at, 1].astype(f32)
                if b == 0:
                    own_ref[far, a] = own
                else:
                    own_sent_ref[far, a] = own.astype(bf16)
                if a == 0:
                    neigh_ref[far, b] = neigh
                else:
                    neigh_sent_ref[far, b] = neigh.astype(bf16)


def second_kernel(kept_ref, got_ref, out_ref, sent_ref):
    for far in range(kept_ref.shape[0]):
        total = kept_ref[far] + got_ref[far].astype(f32)
        out_ref[far] = total[0]
        sent_ref[far] = total[1].astype(bf16)


def third_kernel(bit_ref, own_ref, own_got_ref, neigh_ref, neigh_got_ref, out_ref, sent_ref):
    half = out_ref.shape[0]
    for i in range(half):
        for side, ref in ((bit_ref[0], out_ref), (1 - bit_ref[0], sent_ref)):
            at = side * half + i
            ref[i, 0] = (own_ref[at] + own_got_ref[at].astype(f32)).astype(ref.dtype)
            ref[i, 1] = (neigh_ref[at] + neigh_got_ref[at].astype(f32)).astype(ref.dtype)


def halving_kernel(bit_ref, kept_ref, got_ref, out_ref, sent_ref):
    half = out_ref.shape[0]
    for i in range(half):
        for side, ref in ((bit_ref[0], out_ref), (1 - bit_ref[0], sent_ref)):
            at = side * half + i
            ref[i] = (kept_ref[at] + got_ref[at].astype(f32)).astype(ref.dtype)


def round_sum_kernel(kept_ref, got_ref, out_ref):
    out_ref[...] = (kept_ref[...].astype(f32) + got_ref[...].astype(f32)).astype(out_ref.dtype)


def last_sum_kernel(kept_ref, got_ref, own_ref, neigh_ref):
    total = kept_ref[...].astype(f32) + got_ref[...].astype(f32)
    own_ref[...] = total[0, 0]
    neigh_ref[...] = total[0, 1]


def bit_of(axis, bit):
    return ((lax.axis_index(axis) // bit) % 2).astype(jnp.int32).reshape(1)


def sum_gradients(kept, got):
    feat, dom = lax.axis_size("feat"), lax.axis_size("dom")
    depth, hid = kept.shape[2:]
    far = feat // 8

    def pair(*lead):
        shape = (*lead, depth, hid)
        return [jax.ShapeDtypeStruct(shape, f32), jax.ShapeDtypeStruct(shape, bf16)]

    bits = jnp.concatenate([bit_of("feat", 2), bit_of("feat", 4)])
    own, own_sent, neigh, neigh_sent = local_call(
        first_kernel, "first_sum", pair(far, 2) + pair(far, 2), (bits, kept, got), scalars=1
    )
    own_got, neigh_got = flip("feat", 2)(own_sent), flip("feat", 4)(neigh_sent)
    own, own_sent = local_call(second_kernel, "own_sum", pair(far), (own, own_got))
    own_got = flip("feat", 4)(own_sent)
    neigh, neigh_sent = local_call(second_kernel, "neigh_sum", pair(far), (neigh, neigh_got))
    neigh_got = flip("feat", 2)(neigh_sent)
    half = far // 2
    kept, sent = local_call(
        third_kernel,
        "third_sum",
        pair(half, 2),
        (bit_of("feat", half * 8), own, own_got, neigh, neigh_got),
        scalars=1,
    )
    got = flip("feat", half * 8)(sent)
    while half > 1:
        half //= 2
        kept, sent = local_call(
            halving_kernel, "halving", pair(half, 2), (bit_of("feat", half * 8), kept, got), scalars=1
        )
        got = flip("feat", half * 8)(sent)
    rounded = jax.ShapeDtypeStruct(kept.shape, bf16)
    for bit in bits_of(dom):
        (kept,) = local_call(round_sum_kernel, "rounded_sum", [rounded], (kept, got))
        got = flip("dom", bit)(kept)
    out = jax.ShapeDtypeStruct((depth, hid), f32)
    return local_call(last_sum_kernel, "last_sum", [out, out], (kept, got))


def on_device(
    features,
    self_weight,
    neighbour_weight,
    cotangent,
    send_rows,
    send_count,
    tile_source,
    tile_kind,
    tile_patterns,
):
    feat, dom = lax.axis_size("feat"), lax.axis_size("dom")
    my_part = lax.axis_index("dom")
    me = lax.axis_index("feat").astype(jnp.int32).reshape(1)
    count, depth = features.shape
    rows = count // feat
    hid = self_weight.shape[1]
    slots = send_rows.shape[2]
    columns = features.T
    quarters, below = 4, feat // 4
    outgoing = lax.dynamic_index_in_dim(send_rows, my_part, 0, keepdims=False)
    live = lax.dynamic_index_in_dim(send_count, my_part, 0, keepdims=False)
    slot_ids = jnp.arange(slots, dtype=jnp.int32)
    outgoing = jnp.where(slot_ids[None, :] < live[:, None], outgoing, -1)
    picked, *cuts = pick_rows(
        me // below, columns, outgoing.reshape(1, dom * slots), quarters
    )
    if dom == 2:
        to_me = lax.dynamic_slice_in_dim(picked, my_part * slots, slots, 1)
        to_other = lax.dynamic_slice_in_dim(picked, (1 - my_part) * slots, slots, 1)
        got = flip("dom", 1)(to_other)
        first = my_part == 0
        halo = jnp.concatenate(
            [jnp.where(first, to_me, got), jnp.where(first, got, to_me)], axis=1
        )
    else:
        halo = lax.all_to_all(picked, "dom", 1, 1, tiled=True)
    own_cut = lax.dynamic_slice_in_dim(columns, me[0] // below * (count // quarters), count // quarters, 1)
    parts = [own_cut[None]] + [flip("feat", i * below)(cuts[i - 1]) for i in range(1, quarters)]
    weights = jnp.stack([self_weight, neighbour_weight])[None]
    weights_got = flip("feat", feat // 2)(weights)
    means = neighbour_means(
        tile_source[0].T, tile_kind[0].T, columns, halo, tile_patterns, feat
    )
    own_mean = lax.all_to_all(means, "feat", 0, 0, tiled=True)
    *parts, weights_got, _ = lax.optimization_barrier((*parts, weights_got, means))
    row_bits = list(reversed(bits_of(below)))
    for bit in row_bits:
        sent, kept = cut_rows(bit_of("feat", bit), parts)
        parts = [kept, flip("feat", bit)(sent)]
    weight_bits = [feat // 2] + [b for b in bits_of(feat)[1:-2]] + [feat // 4, 1]
    for bit in weight_bits[1:]:
        weights = jnp.concatenate([weights, weights_got])
        weights_got = flip("feat", bit)(weights)
    row_masks = masks_of([i * below for i in range(quarters)], row_bits)
    block = jax.ShapeDtypeStruct((feat, depth, rows), bf16)
    weight_block = jax.ShapeDtypeStruct((feat, depth, hid), bf16)
    own_features, neighbour_weights, linear = local_call(
        functools.partial(own_linear_kernel, row_masks, masks_of([0], weight_bits)),
        "own_linear",
        [block, weight_block, jax.ShapeDtypeStruct((rows, hid), f32)],
        (me, *parts, weights, weights_got),
        scalars=1,
        scratch=[pltpu.VMEM((feat, depth, hid), bf16)],
    )
    own_features = own_features.reshape(feat // 2, 2, depth, rows)
    own_mean = own_mean.reshape(feat // 2, 2, depth, rows)
    core = bit_of("feat", 1)
    sums = (feat // 2, 2, depth, hid)
    hidden, grad_linear, sent = local_call(
        forward_kernel,
        "forward",
        [
            jax.ShapeDtypeStruct((rows, hid), bf16),
            jax.ShapeDtypeStruct((rows, hid), bf16),
            jax.ShapeDtypeStruct(sums, bf16),
        ],
        (core, linear, neighbour_weights, own_mean, own_features, cotangent),
        scalars=1,
    )
    got = flip("feat", 1)(sent)
    (kept,) = local_call(
        kept_kernel,
        "kept_gradients",
        [jax.ShapeDtypeStruct(sums, f32)],
        (core, own_features, own_mean, grad_linear),
        scalars=1,
    )
    grad_self, grad_neighbour = sum_gradients(kept, got)
    return (hidden, grad_self, grad_neighbour)


def solution(mesh):
    placed = (
        P("dom", "feat"),
        P("feat", None),
        P("feat", None),
        P(("dom", "feat"), None),
        P(),
        P(),
        P("dom", None, None),
        P("dom", None, None),
        P(),
    )
    return jax.shard_map(
        on_device,
        mesh=mesh,
        in_specs=placed,
        out_specs=(P(("dom", "feat"), None), P("feat", None), P("feat", None)),
        check_vma=False,
    )
```

```python
import functools

import jax
import jax.numpy as jnp
from jax import lax
from jax.experimental import pallas as pl
from jax.experimental.pallas import tpu as pltpu
from jax.sharding import PartitionSpec as P

inv_root_two = 0.7071067811865476
inv_root_two_pi = 0.3989422804014327
bf16 = jnp.bfloat16
f32 = jnp.float32
vmem_bytes = 16 * 2**20
most_vmem = 60 * 2**20
whole_vmem = pl.BlockSpec(memory_space=pltpu.VMEM)
whole_smem = pl.BlockSpec(memory_space=pltpu.SMEM)
anywhere = pl.BlockSpec(memory_space=pl.ANY)
last_with_last = (((1,), (1,)), ((), ()))
first_with_first = (((0,), (0,)), ((), ()))


def gelu_pair(linear):
    normal_cdf = 0.5 * (1.0 + lax.erf(linear * inv_root_two))
    density = jnp.exp(-0.5 * linear * linear) * inv_root_two_pi
    return (linear * normal_cdf, normal_cdf + linear * density)


def flip(axis, bit):
    size = lax.axis_size(axis)
    return functools.partial(
        lax.ppermute, axis_name=axis, perm=[(i, i ^ bit) for i in range(size)]
    )


def bits_of(size):
    return [1 << i for i in range(size.bit_length() - 1)]


def with_copies(kernel, lazy, operands, outs, *refs):
    given, refs = refs[:operands], refs[operands:]
    made, refs = refs[:outs], refs[outs:]
    held, done, rest = refs[:operands], refs[operands], refs[operands + 1 :]
    copies = [pltpu.make_async_copy(g, h, done.at[i]) for i, (g, h) in enumerate(zip(given, held))]
    for copy in copies:
        copy.start()
    if lazy:

        def ready(*operands):
            for i in operands:
                copies[i].wait()

        kernel(ready, *held, *made, *rest)
        return
    for copy in copies:
        copy.wait()
    kernel(*held, *made, *rest)


def local_call(kernel, name, outs, operands, scalars=0, scratch=(), fetch=False, lazy=False):
    in_specs = [whole_smem] * scalars + [whole_vmem] * (len(operands) - scalars)
    if fetch or lazy:
        in_specs = [anywhere] * len(operands)
        held = [
            (pltpu.SMEM if i < scalars else pltpu.VMEM)(x.shape, x.dtype)
            for i, x in enumerate(operands)
        ]
        scratch = [*held, pltpu.SemaphoreType.DMA((len(operands),)), *scratch]
        kernel = functools.partial(with_copies, kernel, lazy, len(operands), len(outs))
    return pl.pallas_call(
        kernel,
        out_shape=outs,
        in_specs=in_specs,
        out_specs=[whole_vmem] * len(outs),
        scratch_shapes=list(scratch),
        cost_estimate=pl.CostEstimate(flops=0, bytes_accessed=0, transcendentals=0),
        compiler_params=pltpu.CompilerParams(vmem_limit_bytes=most_vmem if fetch or lazy else vmem_bytes),
        name=name,
    )(*operands)


def pick(columns_ref, asked):
    count = columns_ref.shape[1]
    step = min(256, count)
    total = jnp.zeros((columns_ref.shape[0], asked.shape[1]), f32)
    for at in range(0, count, step):
        ids = lax.broadcasted_iota(jnp.int32, (step, asked.shape[1]), 0) + at
        one_hot = jnp.where(ids == asked, 1.0, 0.0).astype(bf16)
        total = total + jnp.dot(
            columns_ref[:, at : at + step], one_hot, preferred_element_type=f32
        )
    return total.astype(bf16)


def asked_rows(ask_ref, count_ref, part, to):
    slot = lax.broadcasted_iota(jnp.int32, (1, ask_ref.shape[2]), 1)
    return jnp.where(slot < count_ref[part, to], ask_ref[part, pl.ds(to, 1), :], -1)


def open_kernel(
    quarters, count_ref, columns_ref, self_ref, neighbour_ref, ask_ref, picked_ref, weight_ref, across_ref, *cut_refs
):
    me, part = lax.axis_index("feat"), lax.axis_index("dom")
    below = lax.axis_size("feat") // quarters
    quarter, half = me // below, me % below // (below // 2)
    weight_ref[0] = jnp.where(part % 2 == 0, self_ref[...], neighbour_ref[...])
    width = across_ref.shape[2]
    for i, cut_ref in enumerate(cut_refs):
        at = (quarter ^ i) * 2 + half
        cut_ref[0] = columns_ref[:, pl.ds(pl.multiple_of(at * width, width), width)]
        at = (quarter ^ i) * 2 + 1 - half
        across_ref[i] = columns_ref[:, pl.ds(pl.multiple_of(at * width, width), width)]
    parts = ask_ref.shape[1]
    if parts == 2:
        asked = asked_rows(ask_ref, count_ref, part, 1 - part)
    else:
        asked = jnp.concatenate(
            [asked_rows(ask_ref, count_ref, part, to) for to in range(parts)], axis=1
        )
    picked_ref[...] = pick(columns_ref, asked)


def open_exchange(counts, columns, self_weight, neighbour_weight, asks, quarters):
    depth, count = columns.shape
    width = count // quarters // 2
    parts, slots = asks.shape[1:]
    asked = slots if parts == 2 else parts * slots
    return local_call(
        functools.partial(open_kernel, quarters),
        "open_exchange",
        [
            jax.ShapeDtypeStruct((depth, asked), bf16),
            jax.ShapeDtypeStruct((1, *self_weight.shape), bf16),
            jax.ShapeDtypeStruct((quarters, depth, width), bf16),
        ]
        + [jax.ShapeDtypeStruct((1, depth, width), bf16)] * quarters,
        (counts, columns, self_weight, neighbour_weight, asks),
        scalars=1,
        fetch=True,
    )


def mean_kernel(
    unroll, ready, source_ref, kind_ref, count_ref, local_ref, halo_ref, ask_ref, pattern_ref, mean_ref, tiles
):
    depth = local_ref.shape[0]
    side = pattern_ref.shape[1]
    local_tiles, halo_tiles = local_ref.shape[1] // side, halo_ref.shape[1] // side
    ready(2, 3, 5)
    for i in range(local_tiles):
        tiles[i, 0:depth, :] = local_ref[:, i * side : (i + 1) * side]
    first = local_tiles
    if ask_ref.shape[1] == 2:
        part = lax.axis_index("dom")
        own = pick(local_ref, asked_rows(ask_ref, count_ref, part, part))
        for i in range(halo_tiles):
            tiles[local_tiles + part * halo_tiles + i, 0:depth, :] = own[:, i * side : (i + 1) * side]
        first = local_tiles + (1 - part) * halo_tiles
    ready(4)
    for i in range(halo_tiles):
        tiles[first + i, 0:depth, :] = halo_ref[:, i * side : (i + 1) * side]
    tiles[:, depth:, :] = jnp.ones((tiles.shape[0], tiles.shape[1] - depth, side), bf16)
    per_block = mean_ref.shape[2] // side
    ready(0, 1, 6)

    def one(t):
        rows = [tiles[source_ref[k, t]] for k in range(source_ref.shape[0])]
        weights = [pattern_ref[kind_ref[k, t]] for k in range(source_ref.shape[0])]
        summed = lax.dot_general(
            jnp.concatenate(rows, 1),
            jnp.concatenate(weights, 1),
            last_with_last,
            preferred_element_type=f32,
        )
        mean = (summed[0:depth] / summed[depth : depth + 1]).astype(bf16)
        at = lax.rem(t, per_block) * side
        mean_ref[lax.div(t, per_block), :, pl.ds(pl.multiple_of(at, side), side)] = mean

    @pl.loop(0, source_ref.shape[1] // unroll)
    def _(step):
        for u in range(unroll):
            one(step * unroll + u)


def neighbour_means(source, kind, counts, local, halo, asks, patterns, blocks):
    depth, count = local.shape
    side = patterns.shape[1]
    tile_count = (count + asks.shape[1] * asks.shape[2]) // side
    return local_call(
        functools.partial(mean_kernel, 8 if source.shape[1] % 8 == 0 else 1),
        "neighbour_means",
        [jax.ShapeDtypeStruct((blocks, depth, count // blocks), bf16)],
        (source, kind, counts, local, halo, asks, patterns),
        scalars=3,
        scratch=[pltpu.VMEM((tile_count, depth + 16, side), bf16)],
        lazy=True,
    )[0]


def cut_kernel(bit, *refs):
    *held_refs, sent_ref, kept_ref = refs
    half = sent_ref.shape[2]
    bit = lax.axis_index("feat") // bit % 2
    mine = pl.multiple_of(bit * half, half)
    theirs = pl.multiple_of((1 - bit) * half, half)
    at = 0
    for ref in held_refs:
        for i in range(ref.shape[0]):
            sent_ref[at] = ref[i, :, pl.ds(theirs, half)]
            kept_ref[at] = ref[i, :, pl.ds(mine, half)]
            at += 1


def cut_rows(bit, parts, width):
    count = sum(p.shape[0] for p in parts)
    out = jax.ShapeDtypeStruct((count, parts[0].shape[1], width // 2), bf16)
    return local_call(
        functools.partial(cut_kernel, bit), "cut_rows", [out, out], parts, fetch=True
    )


def gathered(parts):
    shape = (sum(p.shape[0] for p in parts), *parts[0].shape[1:])
    return local_call(gather_kernel, "gathered", [jax.ShapeDtypeStruct(shape, bf16)], parts)[0]


def gather_kernel(*refs):
    *held_refs, out_ref = refs
    at = 0
    for ref in held_refs:
        out_ref[at : at + ref.shape[0]] = ref[...]
        at += ref.shape[0]


def flipped(masks, bit):
    return [m ^ bit for m in masks]


def features_in_order(row_masks, kept_ref, got_ref):
    half = kept_ref.shape[0]
    place = {mask: i for i, mask in enumerate(row_masks)}

    def features(mask, at=0, size=None):
        i = place[mask]
        ref = kept_ref if i < half else got_ref
        return ref[i % half, :, at : at + (size or ref.shape[2])]

    return features


def means_in_order(mean_ref):
    me = lax.axis_index("feat")

    def means(mask, at=0, size=None):
        return mean_ref[me ^ mask, :, at : at + (size or mean_ref.shape[2])]

    return means


def forward_kernel(row_masks, weight_masks, ready, *refs):
    pieces = len(weight_masks)
    kept_ref, got_ref, mean_ref, cot_ref = refs[:4]
    mine_refs, other_refs = refs[4 : 4 + pieces], refs[4 + pieces : 4 + 2 * pieces]
    hidden_ref, grad_ref, sums_ref, linear_ref = refs[4 + 2 * pieces :]
    side = lax.axis_index("dom") % 2
    features, means = features_in_order(row_masks, kept_ref, got_ref), means_in_order(mean_ref)
    rows, hid = linear_ref.shape

    def fill_linear(source, weight_refs, more):
        step = min(256, rows)
        for at in range(0, rows, step):
            total = linear_ref[at : at + step] if more else jnp.zeros((step, hid), f32)
            for masks, weight_ref in zip(weight_masks, weight_refs):
                part = jnp.concatenate([source(mask, at, step) for mask in masks], axis=0)
                total = total + lax.dot_general(
                    part,
                    weight_ref[...].reshape(-1, hid),
                    first_with_first,
                    preferred_element_type=f32,
                )
            linear_ref[at : at + step] = total

    ready(0, 1, *range(4, 4 + 2 * pieces))

    @pl.when(side == 0)
    def _():
        fill_linear(features, mine_refs, False)

    @pl.when(side != 0)
    def _():
        fill_linear(features, other_refs, False)

    ready(2)

    @pl.when(side == 0)
    def _():
        fill_linear(means, other_refs, True)

    @pl.when(side != 0)
    def _():
        fill_linear(means, mine_refs, True)

    ready(3)
    step = min(128, rows)
    for at in range(0, rows, step):
        value, slope = gelu_pair(linear_ref[at : at + step])
        hidden_ref[at : at + step] = value.astype(bf16)
        grad_ref[at : at + step] = (cot_ref[at : at + step].astype(f32) * slope).astype(bf16)
    fill_sums(1, features, means, grad_ref, sums_ref)


def fill_sums(core, features, means, grad_ref, sums_ref):
    for i, source in enumerate((features, means)):
        part = jnp.concatenate(
            [source(mask) for mask in range(core, 2 * sums_ref.shape[0], 2)], axis=0
        )
        sums = jnp.dot(part, grad_ref[...], preferred_element_type=f32)
        sums_ref[:, i] = sums.astype(sums_ref.dtype).reshape(sums_ref[:, i].shape)


def kept_kernel(row_masks, kept_ref, got_ref, mean_ref, grad_ref, sums_ref):
    features, means = features_in_order(row_masks, kept_ref, got_ref), means_in_order(mean_ref)
    fill_sums(0, features, means, grad_ref, sums_ref)


def first_kernel(kept_ref, got_ref, own_ref, own_sent_ref, neigh_ref, neigh_sent_ref):
    for at in range(kept_ref.shape[0]):
        far, a, b = at // 4, at // 2 % 2, at % 2
        own = kept_ref[at, 0] + got_ref[at, 0].astype(f32)
        neigh = kept_ref[at, 1] + got_ref[at, 1].astype(f32)
        if b == 0:
            own_ref[far, a] = own
        else:
            own_sent_ref[far, a] = own.astype(bf16)
        if a == 0:
            neigh_ref[far, b] = neigh
        else:
            neigh_sent_ref[far, b] = neigh.astype(bf16)


def second_kernel(kept_ref, got_ref, out_ref, sent_ref):
    for far in range(kept_ref.shape[0]):
        total = kept_ref[far] + got_ref[far].astype(f32)
        out_ref[far] = total[0]
        sent_ref[far] = total[1].astype(bf16)


def third_kernel(own_ref, own_got_ref, neigh_ref, neigh_got_ref, out_ref, sent_ref):
    half = out_ref.shape[0]
    for i in range(half):
        for at, ref in ((i, out_ref), (half + i, sent_ref)):
            ref[i, 0] = (own_ref[at] + own_got_ref[at].astype(f32)).astype(ref.dtype)
            ref[i, 1] = (neigh_ref[at] + neigh_got_ref[at].astype(f32)).astype(ref.dtype)


def halving_kernel(kept_ref, got_ref, out_ref, sent_ref):
    half = out_ref.shape[0]
    for i in range(half):
        for at, ref in ((i, out_ref), (half + i, sent_ref)):
            ref[i] = (kept_ref[at] + got_ref[at].astype(f32)).astype(ref.dtype)


def round_sum_kernel(kept_ref, got_ref, out_ref):
    out_ref[...] = (kept_ref[...].astype(f32) + got_ref[...].astype(f32)).astype(out_ref.dtype)


def last_sum_kernel(kept_ref, got_ref, own_ref, neigh_ref):
    total = kept_ref[...].astype(f32) + got_ref[...].astype(f32)
    own_ref[...] = total[0, 0]
    neigh_ref[...] = total[0, 1]


def sum_gradients(kept, got):
    feat, dom = lax.axis_size("feat"), lax.axis_size("dom")
    depth, hid = kept.shape[2:]
    far = feat // 8

    def pair(*lead):
        shape = (*lead, depth, hid)
        return [jax.ShapeDtypeStruct(shape, f32), jax.ShapeDtypeStruct(shape, bf16)]

    own, own_sent, neigh, neigh_sent = local_call(
        first_kernel, "first_sum", pair(far, 2) + pair(far, 2), (kept, got)
    )
    own_got, neigh_got = flip("feat", 2)(own_sent), flip("feat", 4)(neigh_sent)
    own, own_sent = local_call(second_kernel, "own_sum", pair(far), (own, own_got))
    own_got = flip("feat", 4)(own_sent)
    neigh, neigh_sent = local_call(second_kernel, "neigh_sum", pair(far), (neigh, neigh_got))
    neigh_got = flip("feat", 2)(neigh_sent)
    half = far // 2
    kept, sent = local_call(
        third_kernel, "third_sum", pair(half, 2), (own, own_got, neigh, neigh_got)
    )
    got = flip("feat", half * 8)(sent)
    while half > 1:
        half //= 2
        kept, sent = local_call(halving_kernel, "halving", pair(half, 2), (kept, got))
        got = flip("feat", half * 8)(sent)
    rounded = jax.ShapeDtypeStruct(kept.shape, bf16)
    for bit in bits_of(dom):
        (kept,) = local_call(round_sum_kernel, "rounded_sum", [rounded], (kept, got))
        got = flip("dom", bit)(kept)
    out = jax.ShapeDtypeStruct((depth, hid), f32)
    return local_call(last_sum_kernel, "last_sum", [out, out], (kept, got))


def on_device(
    features,
    self_weight,
    neighbour_weight,
    cotangent,
    send_rows,
    send_count,
    tile_source,
    tile_kind,
    tile_patterns,
):
    feat, dom = lax.axis_size("feat"), lax.axis_size("dom")
    count, depth = features.shape
    rows = count // feat
    hid = self_weight.shape[1]
    columns = features.T
    quarters, below = 4, feat // 4
    row_bits = list(reversed(bits_of(below)))
    picked, weight, across, *cuts = open_exchange(
        send_count, columns, self_weight, neighbour_weight, send_rows, quarters
    )
    came = flip("feat", row_bits[0])(across)
    weight = gathered([weight] + [flip("feat", i * below)(weight) for i in range(1, quarters)])
    near = [cuts[0]] + [flip("feat", i * below)(cuts[i]) for i in range(1, quarters)]
    far = [came[0:1]] + [flip("feat", i * below)(came[i : i + 1]) for i in range(1, quarters)]
    row_masks = [i * below for i in range(quarters)]
    pieces, weight_masks = [weight], [list(row_masks)]
    row_masks = row_masks + flipped(row_masks, row_bits[0])
    for bit in row_bits[:-1]:
        pieces = pieces + [flip("feat", bit)(p) for p in pieces]
        weight_masks = weight_masks + [flipped(m, bit) for m in weight_masks]
    if dom == 2:
        halo = flip("dom", 1)(picked)
    else:
        halo = lax.all_to_all(picked, "dom", 1, 1, tiled=True)
    halo, _, _ = lax.optimization_barrier((halo, came, pieces))
    means = neighbour_means(
        tile_source[0].T, tile_kind[0].T, send_count, columns, halo, send_rows, tile_patterns, feat
    )
    held = lax.optimization_barrier((means, near, far, pieces))
    means, near, far, pieces = held
    own_mean = lax.all_to_all(means, "feat", 0, 0, tiled=True)
    others = [flip("dom", 1)(p) for p in pieces]
    parts, width = [*near, *far], came.shape[2]
    for bit in row_bits[1:]:
        sent, kept = cut_rows(bit, parts, width)
        parts, width = [kept, flip("feat", bit)(sent)], width // 2
        row_masks = row_masks + flipped(row_masks, bit)
    pieces = pieces + [flip("feat", 1)(p) for p in pieces]
    others = others + [flip("feat", 1)(p) for p in others]
    weight_masks = weight_masks + [flipped(m, 1) for m in weight_masks]
    sums = (feat // 2, 2, depth, hid)
    square = jax.ShapeDtypeStruct((rows, hid), bf16)
    hidden, grad_linear, sent = local_call(
        functools.partial(forward_kernel, row_masks, weight_masks),
        "forward",
        [square, square, jax.ShapeDtypeStruct(sums, bf16)],
        (*parts, own_mean, cotangent, *pieces, *others),
        scratch=[pltpu.VMEM((rows, hid), f32)],
        lazy=True,
    )
    got = flip("feat", 1)(sent)
    (kept,) = local_call(
        functools.partial(kept_kernel, row_masks),
        "kept_gradients",
        [jax.ShapeDtypeStruct(sums, f32)],
        (*parts, own_mean, grad_linear),
    )
    grad_self, grad_neighbour = sum_gradients(kept, got)
    return (hidden, grad_self, grad_neighbour)


def solution(mesh):
    placed = (
        P("dom", "feat"),
        P("feat", None),
        P("feat", None),
        P(("dom", "feat"), None),
        P(),
        P(),
        P("dom", None, None),
        P("dom", None, None),
        P(),
    )
    return jax.shard_map(
        on_device,
        mesh=mesh,
        in_specs=placed,
        out_specs=(P(("dom", "feat"), None), P("feat", None), P("feat", None)),
        check_vma=False,
    )
```

```python
import functools

import jax
import jax.numpy as jnp
from jax import lax
from jax.experimental import pallas as pl
from jax.experimental.pallas import tpu as pltpu
from jax.sharding import PartitionSpec as P

inv_root_two = 0.7071067811865476
inv_root_two_pi = 0.3989422804014327
bf16 = jnp.bfloat16
f32 = jnp.float32
vmem_bytes = 16 * 2**20
most_vmem = 60 * 2**20
whole_vmem = pl.BlockSpec(memory_space=pltpu.VMEM)
whole_smem = pl.BlockSpec(memory_space=pltpu.SMEM)
anywhere = pl.BlockSpec(memory_space=pl.ANY)
whole_hbm = pl.BlockSpec(memory_space=pltpu.HBM)
last_with_last = (((1,), (1,)), ((), ()))
first_with_first = (((0,), (0,)), ((), ()))


def gelu_pair(linear):
    normal_cdf = 0.5 * (1.0 + lax.erf(linear * inv_root_two))
    density = jnp.exp(-0.5 * linear * linear) * inv_root_two_pi
    return (linear * normal_cdf, normal_cdf + linear * density)


def flip(axis, bit):
    size = lax.axis_size(axis)
    return functools.partial(
        lax.ppermute, axis_name=axis, perm=[(i, i ^ bit) for i in range(size)]
    )


def bits_of(size):
    return [1 << i for i in range(size.bit_length() - 1)]


def with_copies(kernel, lazy, still, operands, outs, *refs):
    given, refs = refs[:operands], refs[operands:]
    made, refs = refs[:outs], refs[outs:]
    moved = [i for i in range(operands) if i not in still]
    places, done, rest = refs[: len(moved)], refs[len(moved)], refs[len(moved) + 1 :]
    held = list(given)
    copies = {}
    for n, i in enumerate(moved):
        held[i] = places[n]
        copies[i] = pltpu.make_async_copy(given[i], places[n], done.at[n])
        copies[i].start()

    def ready(*which):
        for i in which:
            copies[i].wait()

    if lazy:
        kernel(ready, *held, *made, *rest)
    else:
        ready(*moved)
        kernel(*held, *made, *rest)


def local_call(
    kernel, name, outs, operands, scalars=0, scratch=(), fetch=False, lazy=False, still=(), limit=None
):
    in_specs = [whole_smem] * scalars + [whole_vmem] * (len(operands) - scalars)
    if fetch or lazy:
        limit = limit or most_vmem
        space = anywhere if limit == most_vmem else whole_hbm
        in_specs = [whole_vmem if i in still else space for i in range(len(operands))]
        held = [
            (pltpu.SMEM if i < scalars else pltpu.VMEM)(x.shape, x.dtype)
            for i, x in enumerate(operands)
            if i not in still
        ]
        scratch = [*held, pltpu.SemaphoreType.DMA((len(held),)), *scratch]
        kernel = functools.partial(with_copies, kernel, lazy, still, len(operands), len(outs))
    return pl.pallas_call(
        kernel,
        out_shape=outs,
        in_specs=in_specs,
        out_specs=[whole_vmem] * len(outs),
        scratch_shapes=list(scratch),
        cost_estimate=pl.CostEstimate(flops=0, bytes_accessed=0, transcendentals=0),
        compiler_params=pltpu.CompilerParams(vmem_limit_bytes=limit or vmem_bytes),
        name=name,
    )(*operands)


def pick(columns_ref, asked):
    count = columns_ref.shape[1]
    step = min(256, count)
    total = jnp.zeros((columns_ref.shape[0], asked.shape[1]), f32)
    for at in range(0, count, step):
        ids = lax.broadcasted_iota(jnp.int32, (step, asked.shape[1]), 0) + at
        one_hot = jnp.where(ids == asked, 1.0, 0.0).astype(bf16)
        total = total + jnp.dot(
            columns_ref[:, at : at + step], one_hot, preferred_element_type=f32
        )
    return total.astype(bf16)


def asked_rows(ask_ref, count_ref, part, to):
    slot = lax.broadcasted_iota(jnp.int32, (1, ask_ref.shape[2]), 1)
    return jnp.where(slot < count_ref[part, to], ask_ref[part, pl.ds(to, 1), :], -1)


def open_kernel(
    quarters, count_ref, columns_ref, self_ref, neighbour_ref, ask_ref, picked_ref, across_ref, *cut_refs
):
    me, part = lax.axis_index("feat"), lax.axis_index("dom")
    below = lax.axis_size("feat") // quarters
    quarter, half = me // below, me % below // (below // 2)
    weight = jnp.where(part % 2 == 0, self_ref[...], neighbour_ref[...])
    width = across_ref.shape[2]
    for i, cut_ref in enumerate(cut_refs):
        at = (quarter ^ i) * 2 + half
        cut_ref[0, :, 0:width] = columns_ref[:, pl.ds(pl.multiple_of(at * width, width), width)]
        cut_ref[0, :, width:] = weight
        at = (quarter ^ i) * 2 + 1 - half
        across_ref[i] = columns_ref[:, pl.ds(pl.multiple_of(at * width, width), width)]
    parts = ask_ref.shape[1]
    if parts == 2:
        asked = asked_rows(ask_ref, count_ref, part, 1 - part)
    else:
        asked = jnp.concatenate(
            [asked_rows(ask_ref, count_ref, part, to) for to in range(parts)], axis=1
        )
    picked_ref[...] = pick(columns_ref, asked)


def open_exchange(counts, columns, self_weight, neighbour_weight, asks, quarters):
    depth, count = columns.shape
    width = count // quarters // 2
    parts, slots = asks.shape[1:]
    asked = slots if parts == 2 else parts * slots
    return local_call(
        functools.partial(open_kernel, quarters),
        "open_exchange",
        [
            jax.ShapeDtypeStruct((depth, asked), bf16),
            jax.ShapeDtypeStruct((quarters, depth, width), bf16),
        ]
        + [jax.ShapeDtypeStruct((1, depth, width + self_weight.shape[1]), bf16)] * quarters,
        (counts, columns, self_weight, neighbour_weight, asks),
        scalars=1,
        fetch=True,
    )


def mean_kernel(
    unroll, ready, source_ref, kind_ref, count_ref, local_ref, halo_ref, ask_ref, pattern_ref, mean_ref, tiles
):
    depth = local_ref.shape[0]
    side = pattern_ref.shape[1]
    local_tiles, halo_tiles = local_ref.shape[1] // side, halo_ref.shape[1] // side
    ready(2, 3, 5)
    for i in range(local_tiles):
        tiles[i, 0:depth, :] = local_ref[:, i * side : (i + 1) * side]
    first = local_tiles
    if ask_ref.shape[1] == 2:
        part = lax.axis_index("dom")
        own = pick(local_ref, asked_rows(ask_ref, count_ref, part, part))
        for i in range(halo_tiles):
            tiles[local_tiles + part * halo_tiles + i, 0:depth, :] = own[:, i * side : (i + 1) * side]
        first = local_tiles + (1 - part) * halo_tiles
    ready(4)
    for i in range(halo_tiles):
        tiles[first + i, 0:depth, :] = halo_ref[:, i * side : (i + 1) * side]
    tiles[:, depth:, :] = jnp.ones((tiles.shape[0], tiles.shape[1] - depth, side), bf16)
    per_block = mean_ref.shape[2] // side
    ready(0, 1, 6)

    def one(t):
        rows = [tiles[source_ref[k, t]] for k in range(source_ref.shape[0])]
        weights = [pattern_ref[kind_ref[k, t]] for k in range(source_ref.shape[0])]
        summed = lax.dot_general(
            jnp.concatenate(rows, 1),
            jnp.concatenate(weights, 1),
            last_with_last,
            preferred_element_type=f32,
        )
        mean = (summed[0:depth] / summed[depth : depth + 1]).astype(bf16)
        at = lax.rem(t, per_block) * side
        mean_ref[lax.div(t, per_block), :, pl.ds(pl.multiple_of(at, side), side)] = mean

    @pl.loop(0, source_ref.shape[1] // unroll)
    def _(step):
        for u in range(unroll):
            one(step * unroll + u)


def neighbour_means(source, kind, counts, local, halo, asks, patterns, blocks):
    depth, count = local.shape
    side = patterns.shape[1]
    tile_count = (count + asks.shape[1] * asks.shape[2]) // side
    return local_call(
        functools.partial(mean_kernel, 8 if source.shape[1] % 8 == 0 else 1),
        "neighbour_means",
        [jax.ShapeDtypeStruct((blocks, depth, count // blocks), bf16)],
        (source, kind, counts, local, halo, asks, patterns),
        scalars=3,
        scratch=[pltpu.VMEM((tile_count, depth + 16, side), bf16)],
        lazy=True,
    )[0]


def cut_kernel(bit, *refs):
    *held_refs, sent_ref, kept_ref = refs
    half = sent_ref.shape[2]
    bit = lax.axis_index("feat") // bit % 2
    mine = pl.multiple_of(bit * half, half)
    theirs = pl.multiple_of((1 - bit) * half, half)
    at = 0
    for ref in held_refs:
        for i in range(ref.shape[0]):
            sent_ref[at] = ref[i, :, pl.ds(theirs, half)]
            kept_ref[at] = ref[i, :, pl.ds(mine, half)]
            at += 1


def cut_rows(bit, parts, width):
    count = sum(p.shape[0] for p in parts)
    out = jax.ShapeDtypeStruct((count, parts[0].shape[1], width // 2), bf16)
    return local_call(
        functools.partial(cut_kernel, bit), "cut_rows", [out, out], parts
    )


def weight_kernel(*refs):
    *held_refs, out_ref = refs
    for i, ref in enumerate(held_refs):
        out_ref[i] = ref[0, :, ref.shape[2] - out_ref.shape[2] :]


def weight_pieces(parts, hid):
    out = jax.ShapeDtypeStruct((len(parts), parts[0].shape[1], hid), bf16)
    return local_call(weight_kernel, "weight_pieces", [out], parts)[0]


def flipped(masks, bit):
    return [m ^ bit for m in masks]


def features_in_order(row_masks, kept_ref, got_ref):
    half = kept_ref.shape[0]
    place = {mask: i for i, mask in enumerate(row_masks)}

    def features(mask, at=0, size=None):
        i = place[mask]
        ref = kept_ref if i < half else got_ref
        return ref[i % half, :, at : at + (size or ref.shape[2])]

    return features


def means_in_order(mean_ref):
    me = lax.axis_index("feat")

    def means(mask, at=0, size=None):
        return mean_ref[me ^ mask, :, at : at + (size or mean_ref.shape[2])]

    return means


def own_linear_kernel(row_masks, weight_masks, *refs):
    pieces = len(weight_masks)
    kept_ref, got_ref = refs[:2]
    mine_refs, other_refs = refs[2 : 2 + pieces], refs[2 + pieces : 2 + 2 * pieces]
    linear_ref, weight_ref = refs[2 + 2 * pieces :]
    features = features_in_order(row_masks, kept_ref, got_ref)
    side = lax.axis_index("dom") % 2

    def fill(self_refs, neighbour_refs):
        at = 0
        for ref in neighbour_refs:
            weight_ref[at : at + ref.shape[0]] = ref[...]
            at += ref.shape[0]
        fill_linear(features, weight_masks, self_refs, linear_ref, linear_ref, False)

    @pl.when(side == 0)
    def _():
        fill(mine_refs, other_refs)

    @pl.when(side != 0)
    def _():
        fill(other_refs, mine_refs)


def fill_linear(source, weight_masks, weight_refs, base_ref, linear_ref, more):
    rows, hid = linear_ref.shape
    step = min(256, rows)
    for at in range(0, rows, step):
        total = base_ref[at : at + step] if more else jnp.zeros((step, hid), f32)
        for masks, weight_ref in zip(weight_masks, weight_refs):
            part = jnp.concatenate([source(mask, at, step) for mask in masks], axis=0)
            total = total + lax.dot_general(
                part,
                weight_ref[...].reshape(-1, hid),
                first_with_first,
                preferred_element_type=f32,
            )
        linear_ref[at : at + step] = total


def forward_kernel(row_masks, masks, ready, *refs):
    mean_ref, weight_ref, base_ref, cot_ref, kept_ref, got_ref = refs[:6]
    hidden_ref, other_sums_ref, my_sums_ref, linear_ref, grad_ref = refs[6:]
    features, means = features_in_order(row_masks, kept_ref, got_ref), means_in_order(mean_ref)
    ready(1, 2)
    fill_linear(means, [masks], [weight_ref], base_ref, linear_ref, True)
    ready(3)
    step = min(128, linear_ref.shape[0])
    for at in range(0, linear_ref.shape[0], step):
        value, slope = gelu_pair(linear_ref[at : at + step])
        hidden_ref[at : at + step] = value.astype(bf16)
        grad_ref[at : at + step] = (cot_ref[at : at + step].astype(f32) * slope).astype(bf16)
    ready(4, 5)
    fill_sums(1, features, means, grad_ref, other_sums_ref)
    fill_sums(0, features, means, grad_ref, my_sums_ref)


def fill_sums(core, features, means, grad_ref, sums_ref):
    for i, source in enumerate((features, means)):
        part = jnp.concatenate(
            [source(mask) for mask in range(core, 2 * sums_ref.shape[0], 2)], axis=0
        )
        sums = jnp.dot(part, grad_ref[...], preferred_element_type=f32)
        sums_ref[:, i] = sums.astype(sums_ref.dtype).reshape(sums_ref[:, i].shape)


def first_kernel(kept_ref, got_ref, own_ref, own_sent_ref, neigh_ref, neigh_sent_ref):
    for at in range(kept_ref.shape[0]):
        far, a, b = at // 4, at // 2 % 2, at % 2
        own = kept_ref[at, 0] + got_ref[at, 0].astype(f32)
        neigh = kept_ref[at, 1] + got_ref[at, 1].astype(f32)
        if b == 0:
            own_ref[far, a] = own
        else:
            own_sent_ref[far, a] = own.astype(bf16)
        if a == 0:
            neigh_ref[far, b] = neigh
        else:
            neigh_sent_ref[far, b] = neigh.astype(bf16)


def second_kernel(kept_ref, got_ref, out_ref, sent_ref):
    for far in range(kept_ref.shape[0]):
        total = kept_ref[far] + got_ref[far].astype(f32)
        out_ref[far] = total[0]
        sent_ref[far] = total[1].astype(bf16)


def third_kernel(own_ref, own_got_ref, neigh_ref, neigh_got_ref, out_ref, sent_ref):
    half = out_ref.shape[0]
    for i in range(half):
        for at, ref in ((i, out_ref), (half + i, sent_ref)):
            ref[i, 0] = (own_ref[at] + own_got_ref[at].astype(f32)).astype(ref.dtype)
            ref[i, 1] = (neigh_ref[at] + neigh_got_ref[at].astype(f32)).astype(ref.dtype)


def halving_kernel(kept_ref, got_ref, out_ref, sent_ref):
    half = out_ref.shape[0]
    for i in range(half):
        for at, ref in ((i, out_ref), (half + i, sent_ref)):
            ref[i] = (kept_ref[at] + got_ref[at].astype(f32)).astype(ref.dtype)


def round_sum_kernel(kept_ref, got_ref, out_ref):
    out_ref[...] = (kept_ref[...].astype(f32) + got_ref[...].astype(f32)).astype(out_ref.dtype)


def last_sum_kernel(kept_ref, got_ref, own_ref, neigh_ref):
    total = kept_ref[...].astype(f32) + got_ref[...].astype(f32)
    own_ref[...] = total[0, 0]
    neigh_ref[...] = total[0, 1]


def sum_gradients(kept, got):
    feat, dom = lax.axis_size("feat"), lax.axis_size("dom")
    depth, hid = kept.shape[2:]
    far = feat // 8

    def pair(*lead):
        shape = (*lead, depth, hid)
        return [jax.ShapeDtypeStruct(shape, f32), jax.ShapeDtypeStruct(shape, bf16)]

    own, own_sent, neigh, neigh_sent = local_call(
        first_kernel, "first_sum", pair(far, 2) + pair(far, 2), (kept, got)
    )
    own_got, neigh_got = flip("feat", 2)(own_sent), flip("feat", 4)(neigh_sent)
    own, own_sent = local_call(second_kernel, "own_sum", pair(far), (own, own_got))
    own_got = flip("feat", 4)(own_sent)
    neigh, neigh_sent = local_call(second_kernel, "neigh_sum", pair(far), (neigh, neigh_got))
    neigh_got = flip("feat", 2)(neigh_sent)
    half = far // 2
    kept, sent = local_call(
        third_kernel, "third_sum", pair(half, 2), (own, own_got, neigh, neigh_got)
    )
    got = flip("feat", half * 8)(sent)
    while half > 1:
        half //= 2
        kept, sent = local_call(halving_kernel, "halving", pair(half, 2), (kept, got))
        got = flip("feat", half * 8)(sent)
    rounded = jax.ShapeDtypeStruct(kept.shape, bf16)
    for bit in bits_of(dom):
        (kept,) = local_call(round_sum_kernel, "rounded_sum", [rounded], (kept, got))
        got = flip("dom", bit)(kept)
    out = jax.ShapeDtypeStruct((depth, hid), f32)
    return local_call(last_sum_kernel, "last_sum", [out, out], (kept, got))


def on_device(
    features,
    self_weight,
    neighbour_weight,
    cotangent,
    send_rows,
    send_count,
    tile_source,
    tile_kind,
    tile_patterns,
):
    feat, dom = lax.axis_size("feat"), lax.axis_size("dom")
    count, depth = features.shape
    rows = count // feat
    hid = self_weight.shape[1]
    columns = features.T
    quarters, below = 4, feat // 4
    row_bits = list(reversed(bits_of(below)))
    picked, across, *cuts = open_exchange(
        send_count, columns, self_weight, neighbour_weight, send_rows, quarters
    )
    came = flip("feat", row_bits[0])(across)
    near = [cuts[0]] + [flip("feat", i * below)(cuts[i]) for i in range(1, quarters)]
    if dom == 2:
        halo = flip("dom", 1)(picked)
    else:
        halo = lax.all_to_all(picked, "dom", 1, 1, tiled=True)
    means = neighbour_means(
        tile_source[0].T, tile_kind[0].T, send_count, columns, halo, send_rows, tile_patterns, feat
    )
    came, means = lax.optimization_barrier((came, means))
    far = [came[0:1]] + [flip("feat", i * below)(came[i : i + 1]) for i in range(1, quarters)]
    row_masks = [i * below for i in range(quarters)]
    pieces, weight_masks = [weight_pieces(near, hid)], [list(row_masks)]
    row_masks = row_masks + flipped(row_masks, row_bits[0])
    for bit in row_bits[:-1]:
        pieces = pieces + [flip("feat", bit)(p) for p in pieces]
        weight_masks = weight_masks + [flipped(m, bit) for m in weight_masks]
    means, near, far, pieces = lax.optimization_barrier((means, near, far, pieces))
    own_mean = lax.all_to_all(means, "feat", 0, 0, tiled=True)
    others = [flip("dom", 1)(p) for p in pieces]
    parts, width = [*near, *far], came.shape[2]
    for bit in row_bits[1:]:
        sent, kept = cut_rows(bit, parts, width)
        parts, width = [kept, flip("feat", bit)(sent)], width // 2
        row_masks = row_masks + flipped(row_masks, bit)
    pieces = pieces + [flip("feat", 1)(p) for p in pieces]
    others = others + [flip("feat", 1)(p) for p in others]
    weight_masks = weight_masks + [flipped(m, 1) for m in weight_masks]
    sums = (feat // 2, 2, depth, hid)
    linear, weights = local_call(
        functools.partial(own_linear_kernel, row_masks, weight_masks),
        "own_linear",
        [
            jax.ShapeDtypeStruct((rows, hid), f32),
            jax.ShapeDtypeStruct((feat, depth, hid), bf16),
        ],
        (*parts, *pieces, *others),

    )
    hidden, sent, kept = local_call(
        functools.partial(forward_kernel, row_masks, sum(weight_masks, [])),
        "forward",
        [
            jax.ShapeDtypeStruct((rows, hid), bf16),
            jax.ShapeDtypeStruct(sums, bf16),
            jax.ShapeDtypeStruct(sums, f32),
        ],
        (own_mean, weights, linear, cotangent, *parts),
        scratch=[pltpu.VMEM((rows, hid), f32), pltpu.VMEM((rows, hid), bf16)],
        lazy=True,
        still=(0,),
        limit=24 * 2**20,
    )
    got = flip("feat", 1)(sent)
    grad_self, grad_neighbour = sum_gradients(kept, got)
    return (hidden, grad_self, grad_neighbour)


def solution(mesh):
    placed = (
        P("dom", "feat"),
        P("feat", None),
        P("feat", None),
        P(("dom", "feat"), None),
        P(),
        P(),
        P("dom", None, None),
        P("dom", None, None),
        P(),
    )
    return jax.shard_map(
        on_device,
        mesh=mesh,
        in_specs=placed,
        out_specs=(P(("dom", "feat"), None), P("feat", None), P("feat", None)),
        check_vma=False,
    )
```

```python
import functools

import jax
import jax.numpy as jnp
from jax import lax
from jax.experimental import pallas as pl
from jax.experimental.pallas import tpu as pltpu
from jax.sharding import PartitionSpec as P

inv_root_two = 0.7071067811865476
inv_root_two_pi = 0.3989422804014327
bf16 = jnp.bfloat16
f32 = jnp.float32
vmem_bytes = 16 * 2**20
most_vmem = 60 * 2**20
whole_vmem = pl.BlockSpec(memory_space=pltpu.VMEM)
whole_smem = pl.BlockSpec(memory_space=pltpu.SMEM)
anywhere = pl.BlockSpec(memory_space=pl.ANY)
whole_hbm = pl.BlockSpec(memory_space=pltpu.HBM)
last_with_last = (((1,), (1,)), ((), ()))
first_with_first = (((0,), (0,)), ((), ()))


def gelu_pair(linear):
    normal_cdf = 0.5 * (1.0 + lax.erf(linear * inv_root_two))
    density = jnp.exp(-0.5 * linear * linear) * inv_root_two_pi
    return (linear * normal_cdf, normal_cdf + linear * density)


def flip(axis, bit):
    size = lax.axis_size(axis)
    return functools.partial(
        lax.ppermute, axis_name=axis, perm=[(i, i ^ bit) for i in range(size)]
    )


def bits_of(size):
    return [1 << i for i in range(size.bit_length() - 1)]


def with_copies(kernel, lazy, still, operands, outs, *refs):
    given, refs = refs[:operands], refs[operands:]
    made, refs = refs[:outs], refs[outs:]
    moved = [i for i in range(operands) if i not in still]
    places, done, rest = refs[: len(moved)], refs[len(moved)], refs[len(moved) + 1 :]
    held = list(given)
    copies = {}
    for n, i in enumerate(moved):
        held[i] = places[n]
        copies[i] = pltpu.make_async_copy(given[i], places[n], done.at[n])
        copies[i].start()

    def ready(*which):
        for i in which:
            copies[i].wait()

    if lazy:
        kernel(ready, *held, *made, *rest)
    else:
        ready(*moved)
        kernel(*held, *made, *rest)


def local_call(
    kernel, name, outs, operands, scalars=0, scratch=(), fetch=False, lazy=False, still=(), limit=None
):
    in_specs = [whole_smem] * scalars + [whole_vmem] * (len(operands) - scalars)
    if fetch or lazy:
        limit = limit or most_vmem
        space = anywhere if limit == most_vmem else whole_hbm
        in_specs = [whole_vmem if i in still else space for i in range(len(operands))]
        held = [
            (pltpu.SMEM if i < scalars else pltpu.VMEM)(x.shape, x.dtype)
            for i, x in enumerate(operands)
            if i not in still
        ]
        scratch = [*held, pltpu.SemaphoreType.DMA((len(held),)), *scratch]
        kernel = functools.partial(with_copies, kernel, lazy, still, len(operands), len(outs))
    return pl.pallas_call(
        kernel,
        out_shape=outs,
        in_specs=in_specs,
        out_specs=[whole_vmem] * len(outs),
        scratch_shapes=list(scratch),
        cost_estimate=pl.CostEstimate(flops=0, bytes_accessed=0, transcendentals=0),
        compiler_params=pltpu.CompilerParams(vmem_limit_bytes=limit or vmem_bytes),
        name=name,
    )(*operands)


def pick(columns_ref, asked):
    count = columns_ref.shape[1]
    step = min(256, count)
    total = jnp.zeros((columns_ref.shape[0], asked.shape[1]), f32)
    for at in range(0, count, step):
        ids = lax.broadcasted_iota(jnp.int32, (step, asked.shape[1]), 0) + at
        one_hot = jnp.where(ids == asked, 1.0, 0.0).astype(bf16)
        total = total + jnp.dot(
            columns_ref[:, at : at + step], one_hot, preferred_element_type=f32
        )
    return total.astype(bf16)


def asked_rows(ask_ref, count_ref, part, to):
    slot = lax.broadcasted_iota(jnp.int32, (1, ask_ref.shape[2]), 1)
    return jnp.where(slot < count_ref[part, to], ask_ref[part, pl.ds(to, 1), :], -1)


def open_kernel(
    quarters, count_ref, columns_ref, self_ref, neighbour_ref, ask_ref, picked_ref, across_ref, *cut_refs
):
    me, part = lax.axis_index("feat"), lax.axis_index("dom")
    below = lax.axis_size("feat") // quarters
    quarter, half = me // below, me % below // (below // 2)
    weight = jnp.where(part % 2 == 0, self_ref[...], neighbour_ref[...])
    width = across_ref.shape[2]
    for i, cut_ref in enumerate(cut_refs):
        at = (quarter ^ i) * 2 + half
        cut_ref[0, :, 0:width] = columns_ref[:, pl.ds(pl.multiple_of(at * width, width), width)]
        cut_ref[0, :, width:] = weight
        at = (quarter ^ i) * 2 + 1 - half
        across_ref[i] = columns_ref[:, pl.ds(pl.multiple_of(at * width, width), width)]
    parts = ask_ref.shape[1]
    if parts == 2:
        asked = asked_rows(ask_ref, count_ref, part, 1 - part)
    else:
        asked = jnp.concatenate(
            [asked_rows(ask_ref, count_ref, part, to) for to in range(parts)], axis=1
        )
    picked_ref[...] = pick(columns_ref, asked)


def open_exchange(counts, columns, self_weight, neighbour_weight, asks, quarters):
    depth, count = columns.shape
    width = count // quarters // 2
    parts, slots = asks.shape[1:]
    asked = slots if parts == 2 else parts * slots
    return local_call(
        functools.partial(open_kernel, quarters),
        "open_exchange",
        [
            jax.ShapeDtypeStruct((depth, asked), bf16),
            jax.ShapeDtypeStruct((quarters, depth, width), bf16),
        ]
        + [jax.ShapeDtypeStruct((1, depth, width + self_weight.shape[1]), bf16)] * quarters,
        (counts, columns, self_weight, neighbour_weight, asks),
        scalars=1,
        fetch=True,
    )


def mean_kernel(
    unroll, ready, source_ref, kind_ref, count_ref, local_ref, halo_ref, ask_ref, pattern_ref, mean_ref, tiles
):
    depth = local_ref.shape[0]
    side = pattern_ref.shape[1]
    local_tiles, halo_tiles = local_ref.shape[1] // side, halo_ref.shape[1] // side
    ready(2, 3, 5)
    for i in range(local_tiles):
        tiles[i, 0:depth, :] = local_ref[:, i * side : (i + 1) * side]
    first = local_tiles
    if ask_ref.shape[1] == 2:
        part = lax.axis_index("dom")
        own = pick(local_ref, asked_rows(ask_ref, count_ref, part, part))
        for i in range(halo_tiles):
            tiles[local_tiles + part * halo_tiles + i, 0:depth, :] = own[:, i * side : (i + 1) * side]
        first = local_tiles + (1 - part) * halo_tiles
    ready(4)
    for i in range(halo_tiles):
        tiles[first + i, 0:depth, :] = halo_ref[:, i * side : (i + 1) * side]
    tiles[:, depth:, :] = jnp.ones((tiles.shape[0], tiles.shape[1] - depth, side), bf16)
    per_block = mean_ref.shape[2] // side
    ready(0, 1, 6)

    def one(t):
        rows = [tiles[source_ref[k, t]] for k in range(source_ref.shape[0])]
        weights = [pattern_ref[kind_ref[k, t]] for k in range(source_ref.shape[0])]
        summed = lax.dot_general(
            jnp.concatenate(rows, 1),
            jnp.concatenate(weights, 1),
            last_with_last,
            preferred_element_type=f32,
        )
        mean = (summed[0:depth] / summed[depth : depth + 1]).astype(bf16)
        at = lax.rem(t, per_block) * side
        mean_ref[lax.div(t, per_block), :, pl.ds(pl.multiple_of(at, side), side)] = mean

    @pl.loop(0, source_ref.shape[1] // unroll)
    def _(step):
        for u in range(unroll):
            one(step * unroll + u)


def neighbour_means(source, kind, counts, local, halo, asks, patterns, blocks):
    depth, count = local.shape
    side = patterns.shape[1]
    tile_count = (count + asks.shape[1] * asks.shape[2]) // side
    return local_call(
        functools.partial(mean_kernel, 8 if source.shape[1] % 8 == 0 else 1),
        "neighbour_means",
        [jax.ShapeDtypeStruct((blocks, depth, count // blocks), bf16)],
        (source, kind, counts, local, halo, asks, patterns),
        scalars=3,
        scratch=[pltpu.VMEM((tile_count, depth + 16, side), bf16)],
        lazy=True,
    )[0]


def cut_kernel(bit, *refs):
    *held_refs, sent_ref, kept_ref = refs
    half = sent_ref.shape[2]
    bit = lax.axis_index("feat") // bit % 2
    mine = pl.multiple_of(bit * half, half)
    theirs = pl.multiple_of((1 - bit) * half, half)
    at = 0
    for ref in held_refs:
        for i in range(ref.shape[0]):
            sent_ref[at] = ref[i, :, pl.ds(theirs, half)]
            kept_ref[at] = ref[i, :, pl.ds(mine, half)]
            at += 1


def cut_rows(bit, parts, width):
    count = sum(p.shape[0] for p in parts)
    out = jax.ShapeDtypeStruct((count, parts[0].shape[1], width // 2), bf16)
    return local_call(
        functools.partial(cut_kernel, bit), "cut_rows", [out, out], parts
    )


def weight_kernel(*refs):
    *held_refs, out_ref = refs
    for i, ref in enumerate(held_refs):
        out_ref[i] = ref[0, :, ref.shape[2] - out_ref.shape[2] :]


def weight_pieces(parts, hid):
    out = jax.ShapeDtypeStruct((len(parts), parts[0].shape[1], hid), bf16)
    return local_call(weight_kernel, "weight_pieces", [out], parts)[0]


def flipped(masks, bit):
    return [m ^ bit for m in masks]


def features_in_order(row_masks, kept_ref, got_ref):
    half = kept_ref.shape[0]
    place = {mask: i for i, mask in enumerate(row_masks)}

    def features(mask, at=0, size=None):
        i = place[mask]
        ref = kept_ref if i < half else got_ref
        return ref[i % half, :, at : at + (size or ref.shape[2])]

    return features


def means_in_order(mean_ref):
    me = lax.axis_index("feat")

    def means(mask, at=0, size=None):
        return mean_ref[me ^ mask, :, at : at + (size or mean_ref.shape[2])]

    return means


def own_linear_kernel(row_masks, weight_masks, *refs):
    pieces = len(weight_masks)
    kept_ref, got_ref = refs[:2]
    mine_refs, other_refs = refs[2 : 2 + pieces], refs[2 + pieces : 2 + 2 * pieces]
    cot_ref, linear_ref, beside_ref = refs[2 + 2 * pieces :]
    features = features_in_order(row_masks, kept_ref, got_ref)
    side = lax.axis_index("dom") % 2

    def fill(self_refs, neighbour_refs):
        at = 0
        for ref in neighbour_refs:
            part = ref[...].reshape(-1, ref.shape[2])
            beside_ref[at : at + part.shape[0]] = part
            at += part.shape[0]
        beside_ref[at:] = cot_ref[...]
        fill_linear(features, weight_masks, self_refs, linear_ref, linear_ref, False)

    @pl.when(side == 0)
    def _():
        fill(mine_refs, other_refs)

    @pl.when(side != 0)
    def _():
        fill(other_refs, mine_refs)


def fill_linear(source, weight_masks, weight_refs, base_ref, linear_ref, more):
    rows, hid = linear_ref.shape
    step = min(256, rows)
    for at in range(0, rows, step):
        total = base_ref[at : at + step] if more else jnp.zeros((step, hid), f32)
        for masks, weight_ref in zip(weight_masks, weight_refs):
            part = jnp.concatenate([source(mask, at, step) for mask in masks], axis=0)
            total = total + lax.dot_general(
                part,
                weight_ref[...].reshape(-1, hid),
                first_with_first,
                preferred_element_type=f32,
            )
        linear_ref[at : at + step] = total


def forward_kernel(
    row_masks, masks, mean_ref, beside_ref, base_ref, kept_ref, got_ref,
    hidden_ref, grad_ref, other_sums_ref, my_sums_ref, linear_ref,
):
    features, means = features_in_order(row_masks, kept_ref, got_ref), means_in_order(mean_ref)
    rows = linear_ref.shape[0]
    depth = beside_ref.shape[0] - rows
    fill_linear(means, [masks], [beside_ref.at[0:depth]], base_ref, linear_ref, True)
    step = min(128, rows)
    for at in range(0, rows, step):
        value, slope = gelu_pair(linear_ref[at : at + step])
        hidden_ref[at : at + step] = value.astype(bf16)
        cot = beside_ref[depth + at : depth + at + step].astype(f32)
        grad_ref[at : at + step] = (cot * slope).astype(bf16)
    fill_sums(1, features, grad_ref, other_sums_ref)
    fill_sums(0, features, grad_ref, my_sums_ref)


def neighbour_sums_kernel(mean_ref, grad_ref, other_sums_ref, my_sums_ref):
    means = means_in_order(mean_ref)
    fill_sums(1, means, grad_ref, other_sums_ref)
    fill_sums(0, means, grad_ref, my_sums_ref)


def fill_sums(core, source, grad_ref, sums_ref):
    part = jnp.concatenate(
        [source(mask) for mask in range(core, 2 * sums_ref.shape[0], 2)], axis=0
    )
    sums = jnp.dot(part, grad_ref[...], preferred_element_type=f32)
    sums_ref[...] = sums.astype(sums_ref.dtype).reshape(sums_ref.shape)


def first_kernel(place, kept_ref, got_ref, out_ref, sent_ref):
    for at in range(kept_ref.shape[0]):
        far, rest = at // 4, (at // 2 % 2, at % 2)
        total = kept_ref[at] + got_ref[at].astype(f32)
        if rest[place] == 0:
            out_ref[far, rest[1 - place]] = total
        else:
            sent_ref[far, rest[1 - place]] = total.astype(bf16)


def second_kernel(kept_ref, got_ref, out_ref, sent_ref):
    for far in range(kept_ref.shape[0]):
        total = kept_ref[far] + got_ref[far].astype(f32)
        out_ref[far] = total[0]
        sent_ref[far] = total[1].astype(bf16)


def third_kernel(own_ref, own_got_ref, neigh_ref, neigh_got_ref, out_ref, sent_ref):
    half = out_ref.shape[0]
    for i in range(half):
        for at, ref in ((i, out_ref), (half + i, sent_ref)):
            ref[i, 0] = (own_ref[at] + own_got_ref[at].astype(f32)).astype(ref.dtype)
            ref[i, 1] = (neigh_ref[at] + neigh_got_ref[at].astype(f32)).astype(ref.dtype)


def halving_kernel(kept_ref, got_ref, out_ref, sent_ref):
    half = out_ref.shape[0]
    for i in range(half):
        for at, ref in ((i, out_ref), (half + i, sent_ref)):
            ref[i] = (kept_ref[at] + got_ref[at].astype(f32)).astype(ref.dtype)


def round_sum_kernel(kept_ref, got_ref, out_ref):
    out_ref[...] = (kept_ref[...].astype(f32) + got_ref[...].astype(f32)).astype(out_ref.dtype)


def last_sum_kernel(kept_ref, got_ref, own_ref, neigh_ref):
    total = kept_ref[...].astype(f32) + got_ref[...].astype(f32)
    own_ref[...] = total[0, 0]
    neigh_ref[...] = total[0, 1]


def sum_gradients(own_kept, own_got, neigh_kept, neigh_got):
    feat, dom = lax.axis_size("feat"), lax.axis_size("dom")
    depth, hid = own_kept.shape[1:]
    far = feat // 8

    def pair(*lead):
        shape = (*lead, depth, hid)
        return [jax.ShapeDtypeStruct(shape, f32), jax.ShapeDtypeStruct(shape, bf16)]

    own, own_sent = local_call(
        functools.partial(first_kernel, 1), "own_first", pair(far, 2), (own_kept, own_got)
    )
    own_got = flip("feat", 2)(own_sent)
    neigh, neigh_sent = local_call(
        functools.partial(first_kernel, 0), "neigh_first", pair(far, 2), (neigh_kept, neigh_got)
    )
    neigh_got = flip("feat", 4)(neigh_sent)
    own, own_sent = local_call(second_kernel, "own_second", pair(far), (own, own_got))
    own_got = flip("feat", 4)(own_sent)
    neigh, neigh_sent = local_call(second_kernel, "neigh_second", pair(far), (neigh, neigh_got))
    neigh_got = flip("feat", 2)(neigh_sent)
    half = far // 2
    kept, sent = local_call(
        third_kernel, "third_sum", pair(half, 2), (own, own_got, neigh, neigh_got)
    )
    got = flip("feat", half * 8)(sent)
    while half > 1:
        half //= 2
        kept, sent = local_call(halving_kernel, "halving", pair(half, 2), (kept, got))
        got = flip("feat", half * 8)(sent)
    rounded = jax.ShapeDtypeStruct(kept.shape, bf16)
    for bit in bits_of(dom):
        (kept,) = local_call(round_sum_kernel, "rounded_sum", [rounded], (kept, got))
        got = flip("dom", bit)(kept)
    out = jax.ShapeDtypeStruct((depth, hid), f32)
    return local_call(last_sum_kernel, "last_sum", [out, out], (kept, got))


def on_device(
    features,
    self_weight,
    neighbour_weight,
    cotangent,
    send_rows,
    send_count,
    tile_source,
    tile_kind,
    tile_patterns,
):
    feat, dom = lax.axis_size("feat"), lax.axis_size("dom")
    count, depth = features.shape
    rows = count // feat
    hid = self_weight.shape[1]
    columns = features.T
    quarters, below = 4, feat // 4
    row_bits = list(reversed(bits_of(below)))
    picked, across, *cuts = open_exchange(
        send_count, columns, self_weight, neighbour_weight, send_rows, quarters
    )
    came = flip("feat", row_bits[0])(across)
    near = [cuts[0]] + [flip("feat", i * below)(cuts[i]) for i in range(1, quarters)]
    if dom == 2:
        halo = flip("dom", 1)(picked)
    else:
        halo = lax.all_to_all(picked, "dom", 1, 1, tiled=True)
    means = neighbour_means(
        tile_source[0].T, tile_kind[0].T, send_count, columns, halo, send_rows, tile_patterns, feat
    )
    came, means = lax.optimization_barrier((came, means))
    far = [came[0:1]] + [flip("feat", i * below)(came[i : i + 1]) for i in range(1, quarters)]
    row_masks = [i * below for i in range(quarters)]
    pieces, weight_masks = [weight_pieces(near, hid)], [list(row_masks)]
    row_masks = row_masks + flipped(row_masks, row_bits[0])
    for bit in row_bits[:-1]:
        pieces = pieces + [flip("feat", bit)(p) for p in pieces]
        weight_masks = weight_masks + [flipped(m, bit) for m in weight_masks]
    means, near, far, pieces = lax.optimization_barrier((means, near, far, pieces))
    own_mean = lax.all_to_all(means, "feat", 0, 0, tiled=True)
    others = [flip("dom", 1)(p) for p in pieces]
    parts, width = [*near, *far], came.shape[2]
    for bit in row_bits[1:]:
        sent, kept = cut_rows(bit, parts, width)
        parts, width = [kept, flip("feat", bit)(sent)], width // 2
        row_masks = row_masks + flipped(row_masks, bit)
    pieces = pieces + [flip("feat", 1)(p) for p in pieces]
    others = others + [flip("feat", 1)(p) for p in others]
    weight_masks = weight_masks + [flipped(m, 1) for m in weight_masks]
    linear, beside = local_call(
        functools.partial(own_linear_kernel, row_masks, weight_masks),
        "own_linear",
        [
            jax.ShapeDtypeStruct((rows, hid), f32),
            jax.ShapeDtypeStruct((feat * depth + rows, hid), bf16),
        ],
        (*parts, *pieces, *others, cotangent),
    )
    square = jax.ShapeDtypeStruct((rows, hid), bf16)
    sums = (feat // 2, depth, hid)
    sums = [jax.ShapeDtypeStruct(sums, bf16), jax.ShapeDtypeStruct(sums, f32)]
    hidden, grad_linear, own_sent, own_kept = local_call(
        functools.partial(forward_kernel, row_masks, sum(weight_masks, [])),
        "forward",
        [square, square, *sums],
        (own_mean, beside, linear, *parts),
        scratch=[pltpu.VMEM((rows, hid), f32)],
    )
    own_got = flip("feat", 1)(own_sent)
    neigh_sent, neigh_kept = local_call(
        neighbour_sums_kernel, "neighbour_sums", sums, (own_mean, grad_linear)
    )
    neigh_got = flip("feat", 1)(neigh_sent)
    grad_self, grad_neighbour = sum_gradients(own_kept, own_got, neigh_kept, neigh_got)
    return (hidden, grad_self, grad_neighbour)


def solution(mesh):
    placed = (
        P("dom", "feat"),
        P("feat", None),
        P("feat", None),
        P(("dom", "feat"), None),
        P(),
        P(),
        P("dom", None, None),
        P("dom", None, None),
        P(),
    )
    return jax.shard_map(
        on_device,
        mesh=mesh,
        in_specs=placed,
        out_specs=(P(("dom", "feat"), None), P("feat", None), P("feat", None)),
        check_vma=False,
    )
```

```python
import functools

import jax
import jax.numpy as jnp
from jax import lax
from jax.experimental import pallas as pl
from jax.experimental.pallas import tpu as pltpu
from jax.sharding import PartitionSpec as P

inv_root_two = 0.7071067811865476
inv_root_two_pi = 0.3989422804014327
bf16 = jnp.bfloat16
f32 = jnp.float32
vmem_bytes = 16 * 2**20
most_vmem = 60 * 2**20
whole_vmem = pl.BlockSpec(memory_space=pltpu.VMEM)
whole_smem = pl.BlockSpec(memory_space=pltpu.SMEM)
anywhere = pl.BlockSpec(memory_space=pl.ANY)
whole_hbm = pl.BlockSpec(memory_space=pltpu.HBM)
last_with_last = (((1,), (1,)), ((), ()))
first_with_first = (((0,), (0,)), ((), ()))


def gelu_pair(linear):
    normal_cdf = 0.5 * (1.0 + lax.erf(linear * inv_root_two))
    density = jnp.exp(-0.5 * linear * linear) * inv_root_two_pi
    return (linear * normal_cdf, normal_cdf + linear * density)


def flip(axis, bit):
    size = lax.axis_size(axis)
    return functools.partial(
        lax.ppermute, axis_name=axis, perm=[(i, i ^ bit) for i in range(size)]
    )


def bits_of(size):
    return [1 << i for i in range(size.bit_length() - 1)]


def with_copies(kernel, lazy, still, operands, outs, *refs):
    given, refs = refs[:operands], refs[operands:]
    made, refs = refs[:outs], refs[outs:]
    moved = [i for i in range(operands) if i not in still]
    places, done, rest = refs[: len(moved)], refs[len(moved)], refs[len(moved) + 1 :]
    held = list(given)
    copies = {}
    for n, i in enumerate(moved):
        held[i] = places[n]
        copies[i] = pltpu.make_async_copy(given[i], places[n], done.at[n])
        copies[i].start()

    def ready(*which):
        for i in which:
            copies[i].wait()

    if lazy:
        kernel(ready, *held, *made, *rest)
    else:
        ready(*moved)
        kernel(*held, *made, *rest)


def local_call(
    kernel, name, outs, operands, scalars=0, scratch=(), fetch=False, lazy=False, still=(), limit=None
):
    in_specs = [whole_smem] * scalars + [whole_vmem] * (len(operands) - scalars)
    if fetch or lazy:
        limit = limit or most_vmem
        space = anywhere if limit == most_vmem else whole_hbm
        in_specs = [whole_vmem if i in still else space for i in range(len(operands))]
        held = [
            (pltpu.SMEM if i < scalars else pltpu.VMEM)(x.shape, x.dtype)
            for i, x in enumerate(operands)
            if i not in still
        ]
        scratch = [*held, pltpu.SemaphoreType.DMA((len(held),)), *scratch]
        kernel = functools.partial(with_copies, kernel, lazy, still, len(operands), len(outs))
    return pl.pallas_call(
        kernel,
        out_shape=outs,
        in_specs=in_specs,
        out_specs=[whole_vmem] * len(outs),
        scratch_shapes=list(scratch),
        cost_estimate=pl.CostEstimate(flops=0, bytes_accessed=0, transcendentals=0),
        compiler_params=pltpu.CompilerParams(vmem_limit_bytes=limit or vmem_bytes),
        name=name,
    )(*operands)


def pick(columns_ref, asked):
    count = columns_ref.shape[1]
    step = min(256, count)
    total = jnp.zeros((columns_ref.shape[0], asked.shape[1]), f32)
    for at in range(0, count, step):
        ids = lax.broadcasted_iota(jnp.int32, (step, asked.shape[1]), 0) + at
        one_hot = jnp.where(ids == asked, 1.0, 0.0).astype(bf16)
        total = total + jnp.dot(
            columns_ref[:, at : at + step], one_hot, preferred_element_type=f32
        )
    return total.astype(bf16)


def asked_rows(ask_ref, count_ref, part, to):
    slot = lax.broadcasted_iota(jnp.int32, (1, ask_ref.shape[2]), 1)
    return jnp.where(slot < count_ref[part, to], ask_ref[part, pl.ds(to, 1), :], -1)


def open_kernel(
    quarters, count_ref, columns_ref, self_ref, neighbour_ref, ask_ref, picked_ref, across_ref, *cut_refs
):
    me, part = lax.axis_index("feat"), lax.axis_index("dom")
    below = lax.axis_size("feat") // quarters
    quarter, half = me // below, me % below // (below // 2)
    weight = jnp.where(part % 2 == 0, self_ref[...], neighbour_ref[...])
    width = across_ref.shape[2]
    for i, cut_ref in enumerate(cut_refs):
        at = (quarter ^ i) * 2 + half
        cut_ref[0, :, 0:width] = columns_ref[:, pl.ds(pl.multiple_of(at * width, width), width)]
        cut_ref[0, :, width:] = weight
        at = (quarter ^ i) * 2 + 1 - half
        across_ref[i] = columns_ref[:, pl.ds(pl.multiple_of(at * width, width), width)]
    parts = ask_ref.shape[1]
    if parts == 2:
        asked = asked_rows(ask_ref, count_ref, part, 1 - part)
    else:
        asked = jnp.concatenate(
            [asked_rows(ask_ref, count_ref, part, to) for to in range(parts)], axis=1
        )
    picked_ref[...] = pick(columns_ref, asked)


def open_exchange(counts, columns, self_weight, neighbour_weight, asks, quarters):
    depth, count = columns.shape
    width = count // quarters // 2
    parts, slots = asks.shape[1:]
    asked = slots if parts == 2 else parts * slots
    return local_call(
        functools.partial(open_kernel, quarters),
        "open_exchange",
        [
            jax.ShapeDtypeStruct((depth, asked), bf16),
            jax.ShapeDtypeStruct((quarters, depth, width), bf16),
        ]
        + [jax.ShapeDtypeStruct((1, depth, width + self_weight.shape[1]), bf16)] * quarters,
        (counts, columns, self_weight, neighbour_weight, asks),
        scalars=1,
        fetch=True,
    )


def mean_kernel(
    unroll, ready, source_ref, kind_ref, count_ref, local_ref, halo_ref, ask_ref, pattern_ref, mean_ref, tiles, turned
):
    depth = local_ref.shape[0]
    side = pattern_ref.shape[1]
    local_tiles, halo_tiles = local_ref.shape[1] // side, halo_ref.shape[1] // side
    ready(2, 3, 5)
    for i in range(local_tiles):
        tiles[i, 0:depth, :] = local_ref[:, i * side : (i + 1) * side]
    first = local_tiles
    if ask_ref.shape[1] == 2:
        part = lax.axis_index("dom")
        own = pick(local_ref, asked_rows(ask_ref, count_ref, part, part))
        for i in range(halo_tiles):
            tiles[local_tiles + part * halo_tiles + i, 0:depth, :] = own[:, i * side : (i + 1) * side]
        first = local_tiles + (1 - part) * halo_tiles
    ready(4)
    for i in range(halo_tiles):
        tiles[first + i, 0:depth, :] = halo_ref[:, i * side : (i + 1) * side]
    tiles[:, depth:, :] = jnp.ones((tiles.shape[0], tiles.shape[1] - depth, side), bf16)
    per_block = mean_ref.shape[2] // side
    ready(0, 1, 6)
    for i in range(pattern_ref.shape[0]):
        turned[i] = pattern_ref[i].T

    def one(t):
        rows = [tiles[source_ref[k, t]] for k in range(source_ref.shape[0])]
        weights = [turned[kind_ref[k, t]] for k in range(source_ref.shape[0])]
        summed = lax.dot_general(
            jnp.concatenate(rows, 1),
            jnp.concatenate(weights, 0),
            (((1,), (0,)), ((), ())),
            preferred_element_type=f32,
        )
        mean = (summed[0:depth] / summed[depth : depth + 1]).astype(bf16)
        at = lax.rem(t, per_block) * side
        mean_ref[lax.div(t, per_block), :, pl.ds(pl.multiple_of(at, side), side)] = mean

    @pl.loop(0, source_ref.shape[1] // unroll)
    def _(step):
        for u in range(unroll):
            one(step * unroll + u)


def neighbour_means(source, kind, counts, local, halo, asks, patterns, blocks):
    depth, count = local.shape
    side = patterns.shape[1]
    tile_count = (count + asks.shape[1] * asks.shape[2]) // side
    return local_call(
        functools.partial(mean_kernel, 16 if source.shape[1] % 16 == 0 else 1),
        "neighbour_means",
        [jax.ShapeDtypeStruct((blocks, depth, count // blocks), bf16)],
        (source, kind, counts, local, halo, asks, patterns),
        scalars=3,
        scratch=[pltpu.VMEM((tile_count, depth + 16, side), bf16), pltpu.VMEM(patterns.shape, bf16)],
        lazy=True,
    )[0]


def cut_kernel(bit, *refs):
    *held_refs, sent_ref, kept_ref = refs
    half = sent_ref.shape[2]
    bit = lax.axis_index("feat") // bit % 2
    mine = pl.multiple_of(bit * half, half)
    theirs = pl.multiple_of((1 - bit) * half, half)
    at = 0
    for ref in held_refs:
        for i in range(ref.shape[0]):
            sent_ref[at] = ref[i, :, pl.ds(theirs, half)]
            kept_ref[at] = ref[i, :, pl.ds(mine, half)]
            at += 1


def cut_rows(bit, parts, width):
    count = sum(p.shape[0] for p in parts)
    out = jax.ShapeDtypeStruct((count, parts[0].shape[1], width // 2), bf16)
    return local_call(
        functools.partial(cut_kernel, bit), "cut_rows", [out, out], parts
    )


def weight_kernel(*refs):
    *held_refs, out_ref = refs
    for i, ref in enumerate(held_refs):
        out_ref[i] = ref[0, :, ref.shape[2] - out_ref.shape[2] :]


def weight_pieces(parts, hid):
    out = jax.ShapeDtypeStruct((len(parts), parts[0].shape[1], hid), bf16)
    return local_call(weight_kernel, "weight_pieces", [out], parts)[0]


def flipped(masks, bit):
    return [m ^ bit for m in masks]


def features_in_order(row_masks, kept_ref, got_ref):
    half = kept_ref.shape[0]
    place = {mask: i for i, mask in enumerate(row_masks)}

    def features(mask, at=0, size=None):
        i = place[mask]
        ref = kept_ref if i < half else got_ref
        return ref[i % half, :, at : at + (size or ref.shape[2])]

    return features


def means_in_order(mean_ref):
    me = lax.axis_index("feat")

    def means(mask, at=0, size=None):
        return mean_ref[me ^ mask, :, at : at + (size or mean_ref.shape[2])]

    return means


def own_linear_kernel(row_masks, weight_masks, *refs):
    pieces = len(weight_masks)
    kept_ref, got_ref = refs[:2]
    mine_refs, other_refs = refs[2 : 2 + pieces], refs[2 + pieces : 2 + 2 * pieces]
    cot_ref, linear_ref, beside_ref = refs[2 + 2 * pieces :]
    features = features_in_order(row_masks, kept_ref, got_ref)
    side = lax.axis_index("dom") % 2

    def fill(self_refs, neighbour_refs):
        at = 0
        for ref in neighbour_refs:
            part = ref[...].reshape(-1, ref.shape[2])
            beside_ref[at : at + part.shape[0]] = part
            at += part.shape[0]
        beside_ref[at:] = cot_ref[...]
        fill_linear(features, weight_masks, self_refs, linear_ref, linear_ref, False)

    @pl.when(side == 0)
    def _():
        fill(mine_refs, other_refs)

    @pl.when(side != 0)
    def _():
        fill(other_refs, mine_refs)


def fill_linear(source, weight_masks, weight_refs, base_ref, linear_ref, more):
    rows, hid = linear_ref.shape
    step = min(256, rows)
    for at in range(0, rows, step):
        total = base_ref[at : at + step] if more else jnp.zeros((step, hid), f32)
        for masks, weight_ref in zip(weight_masks, weight_refs):
            part = jnp.concatenate([source(mask, at, step) for mask in masks], axis=0)
            total = total + lax.dot_general(
                part,
                weight_ref[...].reshape(-1, hid),
                first_with_first,
                preferred_element_type=f32,
            )
        linear_ref[at : at + step] = total


def forward_kernel(
    row_masks, masks, mean_ref, beside_ref, base_ref, kept_ref, got_ref,
    hidden_ref, grad_ref, other_sums_ref, my_sums_ref, linear_ref,
):
    features, means = features_in_order(row_masks, kept_ref, got_ref), means_in_order(mean_ref)
    rows = linear_ref.shape[0]
    depth = beside_ref.shape[0] - rows
    fill_linear(means, [masks], [beside_ref.at[0:depth]], base_ref, linear_ref, True)
    step = min(128, rows)
    for at in range(0, rows, step):
        value, slope = gelu_pair(linear_ref[at : at + step])
        hidden_ref[at : at + step] = value.astype(bf16)
        cot = beside_ref[depth + at : depth + at + step].astype(f32)
        grad_ref[at : at + step] = (cot * slope).astype(bf16)
    fill_sums(1, features, grad_ref, other_sums_ref)
    fill_sums(0, features, grad_ref, my_sums_ref)


def neighbour_sums_kernel(mean_ref, grad_ref, other_sums_ref, my_sums_ref):
    means = means_in_order(mean_ref)
    fill_sums(1, means, grad_ref, other_sums_ref)
    fill_sums(0, means, grad_ref, my_sums_ref)


def fill_sums(core, source, grad_ref, sums_ref):
    part = jnp.concatenate(
        [source(mask) for mask in range(core, 2 * sums_ref.shape[0], 2)], axis=0
    )
    sums = jnp.dot(part, grad_ref[...], preferred_element_type=f32)
    sums_ref[...] = sums.astype(sums_ref.dtype).reshape(sums_ref.shape)


def first_kernel(place, kept_ref, got_ref, out_ref, sent_ref):
    for at in range(kept_ref.shape[0]):
        far, rest = at // 4, (at // 2 % 2, at % 2)
        total = kept_ref[at] + got_ref[at].astype(f32)
        if rest[place] == 0:
            out_ref[far, rest[1 - place]] = total
        else:
            sent_ref[far, rest[1 - place]] = total.astype(bf16)


def second_kernel(kept_ref, got_ref, out_ref, sent_ref):
    for far in range(kept_ref.shape[0]):
        total = kept_ref[far] + got_ref[far].astype(f32)
        out_ref[far] = total[0]
        sent_ref[far] = total[1].astype(bf16)


def third_kernel(own_ref, own_got_ref, neigh_ref, neigh_got_ref, out_ref, sent_ref):
    half = out_ref.shape[0]
    for i in range(half):
        for at, ref in ((i, out_ref), (half + i, sent_ref)):
            ref[i, 0] = (own_ref[at] + own_got_ref[at].astype(f32)).astype(ref.dtype)
            ref[i, 1] = (neigh_ref[at] + neigh_got_ref[at].astype(f32)).astype(ref.dtype)


def halving_kernel(kept_ref, got_ref, out_ref, sent_ref):
    half = out_ref.shape[0]
    for i in range(half):
        for at, ref in ((i, out_ref), (half + i, sent_ref)):
            ref[i] = (kept_ref[at] + got_ref[at].astype(f32)).astype(ref.dtype)


def round_sum_kernel(kept_ref, got_ref, out_ref):
    out_ref[...] = (kept_ref[...].astype(f32) + got_ref[...].astype(f32)).astype(out_ref.dtype)


def last_sum_kernel(kept_ref, got_ref, own_ref, neigh_ref):
    total = kept_ref[...].astype(f32) + got_ref[...].astype(f32)
    own_ref[...] = total[0, 0]
    neigh_ref[...] = total[0, 1]


def sum_gradients(own_kept, own_got, neigh_kept, neigh_got):
    feat, dom = lax.axis_size("feat"), lax.axis_size("dom")
    depth, hid = own_kept.shape[1:]
    far = feat // 8

    def pair(*lead):
        shape = (*lead, depth, hid)
        return [jax.ShapeDtypeStruct(shape, f32), jax.ShapeDtypeStruct(shape, bf16)]

    own, own_sent = local_call(
        functools.partial(first_kernel, 1), "own_first", pair(far, 2), (own_kept, own_got)
    )
    own_got = flip("feat", 2)(own_sent)
    neigh, neigh_sent = local_call(
        functools.partial(first_kernel, 0), "neigh_first", pair(far, 2), (neigh_kept, neigh_got)
    )
    neigh_got = flip("feat", 4)(neigh_sent)
    own, own_sent = local_call(second_kernel, "own_second", pair(far), (own, own_got))
    own_got = flip("feat", 4)(own_sent)
    neigh, neigh_sent = local_call(second_kernel, "neigh_second", pair(far), (neigh, neigh_got))
    neigh_got = flip("feat", 2)(neigh_sent)
    half = far // 2
    kept, sent = local_call(
        third_kernel, "third_sum", pair(half, 2), (own, own_got, neigh, neigh_got)
    )
    got = flip("feat", half * 8)(sent)
    while half > 1:
        half //= 2
        kept, sent = local_call(halving_kernel, "halving", pair(half, 2), (kept, got))
        got = flip("feat", half * 8)(sent)
    rounded = jax.ShapeDtypeStruct(kept.shape, bf16)
    for bit in bits_of(dom):
        (kept,) = local_call(round_sum_kernel, "rounded_sum", [rounded], (kept, got))
        got = flip("dom", bit)(kept)
    out = jax.ShapeDtypeStruct((depth, hid), f32)
    return local_call(last_sum_kernel, "last_sum", [out, out], (kept, got))


def on_device(
    features,
    self_weight,
    neighbour_weight,
    cotangent,
    send_rows,
    send_count,
    tile_source,
    tile_kind,
    tile_patterns,
):
    feat, dom = lax.axis_size("feat"), lax.axis_size("dom")
    count, depth = features.shape
    rows = count // feat
    hid = self_weight.shape[1]
    columns = features.T
    quarters, below = 4, feat // 4
    row_bits = list(reversed(bits_of(below)))
    picked, across, *cuts = open_exchange(
        send_count, columns, self_weight, neighbour_weight, send_rows, quarters
    )
    came = flip("feat", row_bits[0])(across)
    near = [cuts[0]] + [flip("feat", i * below)(cuts[i]) for i in range(1, quarters)]
    if dom == 2:
        halo = flip("dom", 1)(picked)
    else:
        halo = lax.all_to_all(picked, "dom", 1, 1, tiled=True)
    means = neighbour_means(
        tile_source[0].T, tile_kind[0].T, send_count, columns, halo, send_rows, tile_patterns, feat
    )
    came, means = lax.optimization_barrier((came, means))
    far = [came[0:1]] + [flip("feat", i * below)(came[i : i + 1]) for i in range(1, quarters)]
    row_masks = [i * below for i in range(quarters)]
    pieces, weight_masks = [weight_pieces(near, hid)], [list(row_masks)]
    row_masks = row_masks + flipped(row_masks, row_bits[0])
    for bit in row_bits[:-1]:
        pieces = pieces + [flip("feat", bit)(p) for p in pieces]
        weight_masks = weight_masks + [flipped(m, bit) for m in weight_masks]
    means, near, far, pieces = lax.optimization_barrier((means, near, far, pieces))
    own_mean = lax.all_to_all(means, "feat", 0, 0, tiled=True)
    others = [flip("dom", 1)(p) for p in pieces]
    parts, width = [*near, *far], came.shape[2]
    for bit in row_bits[1:]:
        sent, kept = cut_rows(bit, parts, width)
        parts, width = [kept, flip("feat", bit)(sent)], width // 2
        row_masks = row_masks + flipped(row_masks, bit)
    pieces = pieces + [flip("feat", 1)(p) for p in pieces]
    others = others + [flip("feat", 1)(p) for p in others]
    weight_masks = weight_masks + [flipped(m, 1) for m in weight_masks]
    linear, beside = local_call(
        functools.partial(own_linear_kernel, row_masks, weight_masks),
        "own_linear",
        [
            jax.ShapeDtypeStruct((rows, hid), f32),
            jax.ShapeDtypeStruct((feat * depth + rows, hid), bf16),
        ],
        (*parts, *pieces, *others, cotangent),
    )
    square = jax.ShapeDtypeStruct((rows, hid), bf16)
    sums = (feat // 2, depth, hid)
    sums = [jax.ShapeDtypeStruct(sums, bf16), jax.ShapeDtypeStruct(sums, f32)]
    hidden, grad_linear, own_sent, own_kept = local_call(
        functools.partial(forward_kernel, row_masks, sum(weight_masks, [])),
        "forward",
        [square, square, *sums],
        (own_mean, beside, linear, *parts),
        scratch=[pltpu.VMEM((rows, hid), f32)],
    )
    own_got = flip("feat", 1)(own_sent)
    neigh_sent, neigh_kept = local_call(
        neighbour_sums_kernel, "neighbour_sums", sums, (own_mean, grad_linear)
    )
    neigh_got = flip("feat", 1)(neigh_sent)
    grad_self, grad_neighbour = sum_gradients(own_kept, own_got, neigh_kept, neigh_got)
    return (hidden, grad_self, grad_neighbour)


def solution(mesh):
    placed = (
        P("dom", "feat"),
        P("feat", None),
        P("feat", None),
        P(("dom", "feat"), None),
        P(),
        P(),
        P("dom", None, None),
        P("dom", None, None),
        P(),
    )
    return jax.shard_map(
        on_device,
        mesh=mesh,
        in_specs=placed,
        out_specs=(P(("dom", "feat"), None), P("feat", None), P("feat", None)),
        check_vma=False,
    )
```

```python
import functools

import jax
import jax.numpy as jnp
from jax import lax
from jax.experimental import pallas as pl
from jax.experimental.pallas import tpu as pltpu
from jax.sharding import PartitionSpec as P

inv_root_two = 0.7071067811865476
inv_root_two_pi = 0.3989422804014327
bf16 = jnp.bfloat16
f32 = jnp.float32
vmem_bytes = 16 * 2**20
most_vmem = 60 * 2**20
whole_vmem = pl.BlockSpec(memory_space=pltpu.VMEM)
whole_smem = pl.BlockSpec(memory_space=pltpu.SMEM)
anywhere = pl.BlockSpec(memory_space=pl.ANY)
whole_hbm = pl.BlockSpec(memory_space=pltpu.HBM)
last_with_last = (((1,), (1,)), ((), ()))
first_with_first = (((0,), (0,)), ((), ()))


def gelu_pair(linear):
    normal_cdf = 0.5 * (1.0 + lax.erf(linear * inv_root_two))
    density = jnp.exp(-0.5 * linear * linear) * inv_root_two_pi
    return (linear * normal_cdf, normal_cdf + linear * density)


def flip(axis, bit):
    size = lax.axis_size(axis)
    return functools.partial(
        lax.ppermute, axis_name=axis, perm=[(i, i ^ bit) for i in range(size)]
    )


def bits_of(size):
    return [1 << i for i in range(size.bit_length() - 1)]


def with_copies(kernel, lazy, still, operands, outs, *refs):
    given, refs = refs[:operands], refs[operands:]
    made, refs = refs[:outs], refs[outs:]
    moved = [i for i in range(operands) if i not in still]
    places, done, rest = refs[: len(moved)], refs[len(moved)], refs[len(moved) + 1 :]
    held = list(given)
    copies = {}
    for n, i in enumerate(moved):
        held[i] = places[n]
        copies[i] = pltpu.make_async_copy(given[i], places[n], done.at[n])
        copies[i].start()

    def ready(*which):
        for i in which:
            copies[i].wait()

    if lazy:
        kernel(ready, *held, *made, *rest)
    else:
        ready(*moved)
        kernel(*held, *made, *rest)


def local_call(
    kernel, name, outs, operands, scalars=0, scratch=(), fetch=False, lazy=False, still=(), limit=None
):
    in_specs = [whole_smem] * scalars + [whole_vmem] * (len(operands) - scalars)
    if fetch or lazy:
        limit = limit or most_vmem
        space = anywhere if limit == most_vmem else whole_hbm
        in_specs = [whole_vmem if i in still else space for i in range(len(operands))]
        held = [
            (pltpu.SMEM if i < scalars else pltpu.VMEM)(x.shape, x.dtype)
            for i, x in enumerate(operands)
            if i not in still
        ]
        scratch = [*held, pltpu.SemaphoreType.DMA((len(held),)), *scratch]
        kernel = functools.partial(with_copies, kernel, lazy, still, len(operands), len(outs))
    return pl.pallas_call(
        kernel,
        out_shape=outs,
        in_specs=in_specs,
        out_specs=[whole_vmem] * len(outs),
        scratch_shapes=list(scratch),
        cost_estimate=pl.CostEstimate(flops=0, bytes_accessed=0, transcendentals=0),
        compiler_params=pltpu.CompilerParams(vmem_limit_bytes=limit or vmem_bytes),
        name=name,
    )(*operands)


def pick(columns_ref, asked):
    count = columns_ref.shape[1]
    step = min(256, count)
    total = jnp.zeros((columns_ref.shape[0], asked.shape[1]), f32)
    for at in range(0, count, step):
        ids = lax.broadcasted_iota(jnp.int32, (step, asked.shape[1]), 0) + at
        one_hot = jnp.where(ids == asked, 1.0, 0.0).astype(bf16)
        total = total + jnp.dot(
            columns_ref[:, at : at + step], one_hot, preferred_element_type=f32
        )
    return total.astype(bf16)


def asked_rows(ask_ref, count_ref, part, to):
    slot = lax.broadcasted_iota(jnp.int32, (1, ask_ref.shape[2]), 1)
    return jnp.where(slot < count_ref[part, to], ask_ref[part, pl.ds(to, 1), :], -1)


def open_kernel(
    quarters, count_ref, columns_ref, self_ref, neighbour_ref, ask_ref, picked_ref, across_ref, *cut_refs
):
    me, part = lax.axis_index("feat"), lax.axis_index("dom")
    below = lax.axis_size("feat") // quarters
    quarter, half = me // below, me % below // (below // 2)
    weight = jnp.where(part % 2 == 0, self_ref[...], neighbour_ref[...])
    width = across_ref.shape[2]
    for i, cut_ref in enumerate(cut_refs):
        at = (quarter ^ i) * 2 + half
        cut_ref[0, :, 0:width] = columns_ref[:, pl.ds(pl.multiple_of(at * width, width), width)]
        if cut_ref.shape[2] > width:
            cut_ref[0, :, width:] = weight
        at = (quarter ^ i) * 2 + 1 - half
        across_ref[i] = columns_ref[:, pl.ds(pl.multiple_of(at * width, width), width)]
    parts = ask_ref.shape[1]
    if parts == 2:
        asked = asked_rows(ask_ref, count_ref, part, 1 - part)
    else:
        asked = jnp.concatenate(
            [asked_rows(ask_ref, count_ref, part, to) for to in range(parts)], axis=1
        )
    picked_ref[...] = pick(columns_ref, asked)


def open_exchange(counts, columns, self_weight, neighbour_weight, asks, quarters):
    depth, count = columns.shape
    width = count // quarters // 2
    parts, slots = asks.shape[1:]
    asked = slots if parts == 2 else parts * slots
    return local_call(
        functools.partial(open_kernel, quarters),
        "open_exchange",
        [
            jax.ShapeDtypeStruct((depth, asked), bf16),
            jax.ShapeDtypeStruct((quarters, depth, width), bf16),
        ]
        + [jax.ShapeDtypeStruct((1, depth, width + self_weight.shape[1]), bf16)] * (quarters - 1)
        + [jax.ShapeDtypeStruct((1, depth, width), bf16)],
        (counts, columns, self_weight, neighbour_weight, asks),
        scalars=1,
        fetch=True,
    )


def mean_kernel(
    unroll, ready, source_ref, kind_ref, count_ref, local_ref, halo_ref, ask_ref, pattern_ref, mean_ref, tiles, turned
):
    depth = local_ref.shape[0]
    side = pattern_ref.shape[1]
    local_tiles, halo_tiles = local_ref.shape[1] // side, halo_ref.shape[1] // side
    ready(2, 3, 5)
    for i in range(local_tiles):
        tiles[i, 0:depth, :] = local_ref[:, i * side : (i + 1) * side]
    first = local_tiles
    if ask_ref.shape[1] == 2:
        part = lax.axis_index("dom")
        own = pick(local_ref, asked_rows(ask_ref, count_ref, part, part))
        for i in range(halo_tiles):
            tiles[local_tiles + part * halo_tiles + i, 0:depth, :] = own[:, i * side : (i + 1) * side]
        first = local_tiles + (1 - part) * halo_tiles
    ready(4)
    for i in range(halo_tiles):
        tiles[first + i, 0:depth, :] = halo_ref[:, i * side : (i + 1) * side]
    tiles[:, depth:, :] = jnp.ones((tiles.shape[0], tiles.shape[1] - depth, side), bf16)
    per_block = mean_ref.shape[2] // side
    ready(0, 1, 6)
    for i in range(pattern_ref.shape[0]):
        turned[i] = pattern_ref[i].T

    def one(t):
        rows = [tiles[source_ref[k, t]] for k in range(source_ref.shape[0])]
        weights = [turned[kind_ref[k, t]] for k in range(source_ref.shape[0])]
        summed = lax.dot_general(
            jnp.concatenate(rows, 1),
            jnp.concatenate(weights, 0),
            (((1,), (0,)), ((), ())),
            preferred_element_type=f32,
        )
        mean = (summed[0:depth] / summed[depth : depth + 1]).astype(bf16)
        at = lax.rem(t, per_block) * side
        mean_ref[lax.div(t, per_block), :, pl.ds(pl.multiple_of(at, side), side)] = mean

    @pl.loop(0, source_ref.shape[1] // unroll)
    def _(step):
        for u in range(unroll):
            one(step * unroll + u)


def neighbour_means(source, kind, counts, local, halo, asks, patterns, blocks):
    depth, count = local.shape
    side = patterns.shape[1]
    tile_count = (count + asks.shape[1] * asks.shape[2]) // side
    return local_call(
        functools.partial(mean_kernel, 16 if source.shape[1] % 16 == 0 else 1),
        "neighbour_means",
        [jax.ShapeDtypeStruct((blocks, depth, count // blocks), bf16)],
        (source, kind, counts, local, halo, asks, patterns),
        scalars=3,
        scratch=[pltpu.VMEM((tile_count, depth + 16, side), bf16), pltpu.VMEM(patterns.shape, bf16)],
        lazy=True,
    )[0]


def cut_kernel(bit, *refs):
    *held_refs, sent_ref, kept_ref = refs
    half = sent_ref.shape[2]
    bit = lax.axis_index("feat") // bit % 2
    mine = pl.multiple_of(bit * half, half)
    theirs = pl.multiple_of((1 - bit) * half, half)
    at = 0
    for ref in held_refs:
        for i in range(ref.shape[0]):
            sent_ref[at] = ref[i, :, pl.ds(theirs, half)]
            kept_ref[at] = ref[i, :, pl.ds(mine, half)]
            at += 1


def cut_rows(bit, parts, width):
    count = sum(p.shape[0] for p in parts)
    out = jax.ShapeDtypeStruct((count, parts[0].shape[1], width // 2), bf16)
    return local_call(
        functools.partial(cut_kernel, bit), "cut_rows", [out, out], parts
    )


def weight_kernel(*refs):
    *held_refs, out_ref = refs
    for i, ref in enumerate(held_refs):
        out_ref[i] = ref[0, :, ref.shape[2] - out_ref.shape[2] :]


def weight_pieces(parts, hid):
    out = jax.ShapeDtypeStruct((len(parts), parts[0].shape[1], hid), bf16)
    return local_call(weight_kernel, "weight_pieces", [out], parts)[0]


def relay_kernel(came_ref, near_ref, out_ref):
    width = came_ref.shape[2]
    out_ref[0, :, 0:width] = came_ref[1]
    out_ref[0, :, width:] = near_ref[0, :, near_ref.shape[2] - (out_ref.shape[2] - width) :]


def relayed(came, near):
    out = jax.ShapeDtypeStruct((1, came.shape[1], near.shape[2]), bf16)
    return local_call(relay_kernel, "relayed", [out], (came, near))[0]


def gather_kernel(*refs):
    *held_refs, out_ref = refs
    at = 0
    for ref in held_refs:
        out_ref[at : at + ref.shape[0]] = ref[...]
        at += ref.shape[0]


def gathered(parts):
    shape = (sum(p.shape[0] for p in parts), *parts[0].shape[1:])
    return local_call(gather_kernel, "gathered", [jax.ShapeDtypeStruct(shape, bf16)], parts)[0]


def flipped(masks, bit):
    return [m ^ bit for m in masks]


def features_in_order(row_masks, kept_ref, got_ref):
    half = kept_ref.shape[0]
    place = {mask: i for i, mask in enumerate(row_masks)}

    def features(mask, at=0, size=None):
        i = place[mask]
        ref = kept_ref if i < half else got_ref
        return ref[i % half, :, at : at + (size or ref.shape[2])]

    return features


def means_in_order(mean_ref):
    me = lax.axis_index("feat")

    def means(mask, at=0, size=None):
        return mean_ref[me ^ mask, :, at : at + (size or mean_ref.shape[2])]

    return means


def own_linear_kernel(row_masks, weight_masks, *refs):
    pieces = len(weight_masks)
    kept_ref, got_ref = refs[:2]
    mine_refs, other_refs = refs[2 : 2 + pieces], refs[2 + pieces : 2 + 2 * pieces]
    cot_ref, linear_ref, beside_ref = refs[2 + 2 * pieces :]
    features = features_in_order(row_masks, kept_ref, got_ref)
    side = lax.axis_index("dom") % 2

    def fill(self_refs, neighbour_refs):
        at = 0
        for ref in neighbour_refs:
            part = ref[...].reshape(-1, ref.shape[2])
            beside_ref[at : at + part.shape[0]] = part
            at += part.shape[0]
        beside_ref[at:] = cot_ref[...]
        fill_linear(features, weight_masks, self_refs, linear_ref, linear_ref, False)

    @pl.when(side == 0)
    def _():
        fill(mine_refs, other_refs)

    @pl.when(side != 0)
    def _():
        fill(other_refs, mine_refs)


def fill_linear(source, weight_masks, weight_refs, base_ref, linear_ref, more):
    rows, hid = linear_ref.shape
    step = min(256, rows)
    for at in range(0, rows, step):
        total = base_ref[at : at + step] if more else jnp.zeros((step, hid), f32)
        for masks, weight_ref in zip(weight_masks, weight_refs):
            part = jnp.concatenate([source(mask, at, step) for mask in masks], axis=0)
            total = total + lax.dot_general(
                part,
                weight_ref[...].reshape(-1, hid),
                first_with_first,
                preferred_element_type=f32,
            )
        linear_ref[at : at + step] = total


def forward_kernel(
    row_masks, masks, mean_ref, beside_ref, base_ref, kept_ref, got_ref,
    hidden_ref, grad_ref, other_sums_ref, my_sums_ref, linear_ref,
):
    features, means = features_in_order(row_masks, kept_ref, got_ref), means_in_order(mean_ref)
    rows = linear_ref.shape[0]
    depth = beside_ref.shape[0] - rows
    fill_linear(means, [masks], [beside_ref.at[0:depth]], base_ref, linear_ref, True)
    step = min(128, rows)
    for at in range(0, rows, step):
        value, slope = gelu_pair(linear_ref[at : at + step])
        hidden_ref[at : at + step] = value.astype(bf16)
        cot = beside_ref[depth + at : depth + at + step].astype(f32)
        grad_ref[at : at + step] = (cot * slope).astype(bf16)
    fill_sums(1, features, grad_ref, other_sums_ref)
    fill_sums(0, features, grad_ref, my_sums_ref)


def neighbour_sums_kernel(mean_ref, grad_ref, other_sums_ref, my_sums_ref):
    means = means_in_order(mean_ref)
    fill_sums(1, means, grad_ref, other_sums_ref)
    fill_sums(0, means, grad_ref, my_sums_ref)


def fill_sums(core, source, grad_ref, sums_ref):
    part = jnp.concatenate(
        [source(mask) for mask in range(core, 2 * sums_ref.shape[0], 2)], axis=0
    )
    sums = jnp.dot(part, grad_ref[...], preferred_element_type=f32)
    sums_ref[...] = sums.astype(sums_ref.dtype).reshape(sums_ref.shape)


def first_kernel(place, kept_ref, got_ref, out_ref, sent_ref):
    for at in range(kept_ref.shape[0]):
        far, rest = at // 4, (at // 2 % 2, at % 2)
        total = kept_ref[at] + got_ref[at].astype(f32)
        if rest[place] == 0:
            out_ref[far, rest[1 - place]] = total
        else:
            sent_ref[far, rest[1 - place]] = total.astype(bf16)


def second_kernel(kept_ref, got_ref, out_ref, sent_ref):
    for far in range(kept_ref.shape[0]):
        total = kept_ref[far] + got_ref[far].astype(f32)
        out_ref[far] = total[0]
        sent_ref[far] = total[1].astype(bf16)


def third_kernel(own_ref, own_got_ref, neigh_ref, neigh_got_ref, out_ref, sent_ref):
    half = out_ref.shape[0]
    for i in range(half):
        for at, ref in ((i, out_ref), (half + i, sent_ref)):
            ref[i, 0] = (own_ref[at] + own_got_ref[at].astype(f32)).astype(ref.dtype)
            ref[i, 1] = (neigh_ref[at] + neigh_got_ref[at].astype(f32)).astype(ref.dtype)


def halving_kernel(kept_ref, got_ref, out_ref, sent_ref):
    half = out_ref.shape[0]
    for i in range(half):
        for at, ref in ((i, out_ref), (half + i, sent_ref)):
            ref[i] = (kept_ref[at] + got_ref[at].astype(f32)).astype(ref.dtype)


def round_sum_kernel(kept_ref, got_ref, out_ref):
    out_ref[...] = (kept_ref[...].astype(f32) + got_ref[...].astype(f32)).astype(out_ref.dtype)


def last_sum_kernel(kept_ref, got_ref, own_ref, neigh_ref):
    total = kept_ref[...].astype(f32) + got_ref[...].astype(f32)
    own_ref[...] = total[0, 0]
    neigh_ref[...] = total[0, 1]


def sum_gradients(own_kept, own_got, neigh_kept, neigh_got):
    feat, dom = lax.axis_size("feat"), lax.axis_size("dom")
    depth, hid = own_kept.shape[1:]
    far = feat // 8

    def pair(*lead):
        shape = (*lead, depth, hid)
        return [jax.ShapeDtypeStruct(shape, f32), jax.ShapeDtypeStruct(shape, bf16)]

    own, own_sent = local_call(
        functools.partial(first_kernel, 1), "own_first", pair(far, 2), (own_kept, own_got)
    )
    own_got = flip("feat", 2)(own_sent)
    neigh, neigh_sent = local_call(
        functools.partial(first_kernel, 0), "neigh_first", pair(far, 2), (neigh_kept, neigh_got)
    )
    neigh_got = flip("feat", 4)(neigh_sent)
    own, own_sent = local_call(second_kernel, "own_second", pair(far), (own, own_got))
    own_got = flip("feat", 4)(own_sent)
    neigh, neigh_sent = local_call(second_kernel, "neigh_second", pair(far), (neigh, neigh_got))
    neigh_got = flip("feat", 2)(neigh_sent)
    half = far // 2
    kept, sent = local_call(
        third_kernel, "third_sum", pair(half, 2), (own, own_got, neigh, neigh_got)
    )
    got = flip("feat", half * 8)(sent)
    while half > 1:
        half //= 2
        kept, sent = local_call(halving_kernel, "halving", pair(half, 2), (kept, got))
        got = flip("feat", half * 8)(sent)
    rounded = jax.ShapeDtypeStruct(kept.shape, bf16)
    for bit in bits_of(dom):
        (kept,) = local_call(round_sum_kernel, "rounded_sum", [rounded], (kept, got))
        got = flip("dom", bit)(kept)
    out = jax.ShapeDtypeStruct((depth, hid), f32)
    return local_call(last_sum_kernel, "last_sum", [out, out], (kept, got))


def on_device(
    features,
    self_weight,
    neighbour_weight,
    cotangent,
    send_rows,
    send_count,
    tile_source,
    tile_kind,
    tile_patterns,
):
    feat, dom = lax.axis_size("feat"), lax.axis_size("dom")
    count, depth = features.shape
    rows = count // feat
    hid = self_weight.shape[1]
    columns = features.T
    quarters, below = 4, feat // 4
    row_bits = list(reversed(bits_of(below)))
    picked, across, *cuts = open_exchange(
        send_count, columns, self_weight, neighbour_weight, send_rows, quarters
    )
    came = flip("feat", row_bits[0])(across)
    near = [cuts[0]] + [flip("feat", i * below)(cuts[i]) for i in range(1, quarters)]
    if dom == 2:
        halo = flip("dom", 1)(picked)
    else:
        halo = lax.all_to_all(picked, "dom", 1, 1, tiled=True)
    means = neighbour_means(
        tile_source[0].T, tile_kind[0].T, send_count, columns, halo, send_rows, tile_patterns, feat
    )
    came, means = lax.optimization_barrier((came, means))
    leaving = [came[0:1], relayed(came, near[2]), came[2:3], came[3:4]]
    far = leaving[:1] + [flip("feat", i * below)(leaving[i]) for i in range(1, quarters)]
    row_masks = [i * below for i in range(quarters)]
    pieces = [weight_pieces(near[:3], hid), weight_pieces(far[1:2], hid)]
    weight_masks = list(row_masks)
    row_masks = row_masks + flipped(row_masks, row_bits[0])
    for bit in row_bits[:-1]:
        pieces = pieces + [flip("feat", bit)(p) for p in pieces]
        weight_masks = weight_masks + flipped(weight_masks, bit)
    means, near, far, pieces = lax.optimization_barrier((means, near, far, pieces))
    own_mean = lax.all_to_all(means, "feat", 0, 0, tiled=True)
    pieces, weight_masks = [gathered(pieces)], [weight_masks]
    others = [flip("dom", 1)(p) for p in pieces]
    parts, width = [*near, *far], came.shape[2]
    for bit in row_bits[1:]:
        sent, kept = cut_rows(bit, parts, width)
        parts, width = [kept, flip("feat", bit)(sent)], width // 2
        row_masks = row_masks + flipped(row_masks, bit)
    pieces = pieces + [flip("feat", 1)(p) for p in pieces]
    others = others + [flip("feat", 1)(p) for p in others]
    weight_masks = weight_masks + [flipped(m, 1) for m in weight_masks]
    linear, beside = local_call(
        functools.partial(own_linear_kernel, row_masks, weight_masks),
        "own_linear",
        [
            jax.ShapeDtypeStruct((rows, hid), f32),
            jax.ShapeDtypeStruct((feat * depth + rows, hid), bf16),
        ],
        (*parts, *pieces, *others, cotangent),
    )
    square = jax.ShapeDtypeStruct((rows, hid), bf16)
    sums = (feat // 2, depth, hid)
    sums = [jax.ShapeDtypeStruct(sums, bf16), jax.ShapeDtypeStruct(sums, f32)]
    hidden, grad_linear, own_sent, own_kept = local_call(
        functools.partial(forward_kernel, row_masks, sum(weight_masks, [])),
        "forward",
        [square, square, *sums],
        (own_mean, beside, linear, *parts),
        scratch=[pltpu.VMEM((rows, hid), f32)],
    )
    own_got = flip("feat", 1)(own_sent)
    neigh_sent, neigh_kept = local_call(
        neighbour_sums_kernel, "neighbour_sums", sums, (own_mean, grad_linear)
    )
    neigh_got = flip("feat", 1)(neigh_sent)
    grad_self, grad_neighbour = sum_gradients(own_kept, own_got, neigh_kept, neigh_got)
    return (hidden, grad_self, grad_neighbour)


def solution(mesh):
    placed = (
        P("dom", "feat"),
        P("feat", None),
        P("feat", None),
        P(("dom", "feat"), None),
        P(),
        P(),
        P("dom", None, None),
        P("dom", None, None),
        P(),
    )
    return jax.shard_map(
        on_device,
        mesh=mesh,
        in_specs=placed,
        out_specs=(P(("dom", "feat"), None), P("feat", None), P("feat", None)),
        check_vma=False,
    )
```

```python
import functools

import jax
import jax.numpy as jnp
from jax import lax
from jax.experimental import pallas as pl
from jax.experimental.pallas import tpu as pltpu
from jax.sharding import PartitionSpec as P

inv_root_two = 0.7071067811865476
inv_root_two_pi = 0.3989422804014327
bf16 = jnp.bfloat16
f32 = jnp.float32
vmem_bytes = 16 * 2**20
most_vmem = 60 * 2**20
whole_vmem = pl.BlockSpec(memory_space=pltpu.VMEM)
whole_smem = pl.BlockSpec(memory_space=pltpu.SMEM)
anywhere = pl.BlockSpec(memory_space=pl.ANY)
whole_hbm = pl.BlockSpec(memory_space=pltpu.HBM)
last_with_last = (((1,), (1,)), ((), ()))
first_with_first = (((0,), (0,)), ((), ()))


def gelu_pair(linear):
    normal_cdf = 0.5 * (1.0 + lax.erf(linear * inv_root_two))
    density = jnp.exp(-0.5 * linear * linear) * inv_root_two_pi
    return (linear * normal_cdf, normal_cdf + linear * density)


def flip(axis, bit):
    size = lax.axis_size(axis)
    return functools.partial(
        lax.ppermute, axis_name=axis, perm=[(i, i ^ bit) for i in range(size)]
    )


def bits_of(size):
    return [1 << i for i in range(size.bit_length() - 1)]


def with_copies(kernel, lazy, still, operands, outs, *refs):
    given, refs = refs[:operands], refs[operands:]
    made, refs = refs[:outs], refs[outs:]
    moved = [i for i in range(operands) if i not in still]
    places, done, rest = refs[: len(moved)], refs[len(moved)], refs[len(moved) + 1 :]
    held = list(given)
    copies = {}
    for n, i in enumerate(moved):
        held[i] = places[n]
        copies[i] = pltpu.make_async_copy(given[i], places[n], done.at[n])
        copies[i].start()

    def ready(*which):
        for i in which:
            copies[i].wait()

    if lazy:
        kernel(ready, *held, *made, *rest)
    else:
        ready(*moved)
        kernel(*held, *made, *rest)


def local_call(
    kernel, name, outs, operands, scalars=0, scratch=(), fetch=False, lazy=False, still=(), limit=None
):
    in_specs = [whole_smem] * scalars + [whole_vmem] * (len(operands) - scalars)
    if fetch or lazy:
        limit = limit or most_vmem
        space = anywhere if limit == most_vmem else whole_hbm
        in_specs = [whole_vmem if i in still else space for i in range(len(operands))]
        held = [
            (pltpu.SMEM if i < scalars else pltpu.VMEM)(x.shape, x.dtype)
            for i, x in enumerate(operands)
            if i not in still
        ]
        scratch = [*held, pltpu.SemaphoreType.DMA((len(held),)), *scratch]
        kernel = functools.partial(with_copies, kernel, lazy, still, len(operands), len(outs))
    return pl.pallas_call(
        kernel,
        out_shape=outs,
        in_specs=in_specs,
        out_specs=[whole_vmem] * len(outs),
        scratch_shapes=list(scratch),
        cost_estimate=pl.CostEstimate(flops=0, bytes_accessed=0, transcendentals=0),
        compiler_params=pltpu.CompilerParams(vmem_limit_bytes=limit or vmem_bytes),
        name=name,
    )(*operands)


def pick(columns_ref, asked):
    count = columns_ref.shape[1]
    step = min(256, count)
    total = jnp.zeros((columns_ref.shape[0], asked.shape[1]), f32)
    for at in range(0, count, step):
        ids = lax.broadcasted_iota(jnp.int32, (step, asked.shape[1]), 0) + at
        one_hot = jnp.where(ids == asked, 1.0, 0.0).astype(bf16)
        total = total + jnp.dot(
            columns_ref[:, at : at + step], one_hot, preferred_element_type=f32
        )
    return total.astype(bf16)


def asked_rows(ask_ref, count_ref, part, to):
    slot = lax.broadcasted_iota(jnp.int32, (1, ask_ref.shape[2]), 1)
    return jnp.where(slot < count_ref[part, to], ask_ref[part, pl.ds(to, 1), :], -1)


def open_kernel(
    quarters, count_ref, columns_ref, self_ref, neighbour_ref, ask_ref, picked_ref, across_ref, *cut_refs
):
    me, part = lax.axis_index("feat"), lax.axis_index("dom")
    below = lax.axis_size("feat") // quarters
    quarter, half = me // below, me % below // (below // 2)
    weight = jnp.where(part % 2 == 0, self_ref[...], neighbour_ref[...])
    width = across_ref.shape[2]
    for i, cut_ref in enumerate(cut_refs):
        at = (quarter ^ i) * 2 + half
        cut_ref[0, :, 0:width] = columns_ref[:, pl.ds(pl.multiple_of(at * width, width), width)]
        if cut_ref.shape[2] > width:
            cut_ref[0, :, width:] = weight
        at = (quarter ^ i) * 2 + 1 - half
        across_ref[i] = columns_ref[:, pl.ds(pl.multiple_of(at * width, width), width)]
    parts = ask_ref.shape[1]
    if parts == 2:
        asked = asked_rows(ask_ref, count_ref, part, 1 - part)
    else:
        asked = jnp.concatenate(
            [asked_rows(ask_ref, count_ref, part, to) for to in range(parts)], axis=1
        )
    picked_ref[...] = pick(columns_ref, asked)


def open_exchange(counts, columns, self_weight, neighbour_weight, asks, quarters):
    depth, count = columns.shape
    width = count // quarters // 2
    parts, slots = asks.shape[1:]
    asked = slots if parts == 2 else parts * slots
    return local_call(
        functools.partial(open_kernel, quarters),
        "open_exchange",
        [
            jax.ShapeDtypeStruct((depth, asked), bf16),
            jax.ShapeDtypeStruct((quarters, depth, width), bf16),
        ]
        + [jax.ShapeDtypeStruct((1, depth, width + self_weight.shape[1]), bf16)] * (quarters - 1)
        + [jax.ShapeDtypeStruct((1, depth, width), bf16)],
        (counts, columns, self_weight, neighbour_weight, asks),
        scalars=1,
        fetch=True,
    )


def mean_kernel(
    unroll, ready, source_ref, kind_ref, count_ref, local_ref, halo_ref, ask_ref, pattern_ref, mean_ref, tiles, turned
):
    depth = local_ref.shape[0]
    side = pattern_ref.shape[1]
    local_tiles, halo_tiles = local_ref.shape[1] // side, halo_ref.shape[1] // side
    ready(2, 3, 5)
    for i in range(local_tiles):
        tiles[i, 0:depth, :] = local_ref[:, i * side : (i + 1) * side]
    first = local_tiles
    if ask_ref.shape[1] == 2:
        part = lax.axis_index("dom")
        own = pick(local_ref, asked_rows(ask_ref, count_ref, part, part))
        for i in range(halo_tiles):
            tiles[local_tiles + part * halo_tiles + i, 0:depth, :] = own[:, i * side : (i + 1) * side]
        first = local_tiles + (1 - part) * halo_tiles
    ready(4)
    for i in range(halo_tiles):
        tiles[first + i, 0:depth, :] = halo_ref[:, i * side : (i + 1) * side]
    tiles[:, depth:, :] = jnp.ones((tiles.shape[0], tiles.shape[1] - depth, side), bf16)
    per_block = mean_ref.shape[2] // side
    ready(0, 1, 6)
    for i in range(pattern_ref.shape[0]):
        turned[i] = pattern_ref[i].T

    def one(t):
        rows = [tiles[source_ref[k, t]] for k in range(source_ref.shape[0])]
        weights = [turned[kind_ref[k, t]] for k in range(source_ref.shape[0])]
        summed = lax.dot_general(
            jnp.concatenate(rows, 1),
            jnp.concatenate(weights, 0),
            (((1,), (0,)), ((), ())),
            preferred_element_type=f32,
        )
        mean = (summed[0:depth] / summed[depth : depth + 1]).astype(bf16)
        at = lax.rem(t, per_block) * side
        mean_ref[lax.div(t, per_block), :, pl.ds(pl.multiple_of(at, side), side)] = mean

    @pl.loop(0, source_ref.shape[1] // unroll)
    def _(step):
        for u in range(unroll):
            one(step * unroll + u)


def neighbour_means(source, kind, counts, local, halo, asks, patterns, blocks):
    depth, count = local.shape
    side = patterns.shape[1]
    tile_count = (count + asks.shape[1] * asks.shape[2]) // side
    return local_call(
        functools.partial(mean_kernel, 16 if source.shape[1] % 16 == 0 else 1),
        "neighbour_means",
        [jax.ShapeDtypeStruct((blocks, depth, count // blocks), bf16)],
        (source, kind, counts, local, halo, asks, patterns),
        scalars=3,
        scratch=[pltpu.VMEM((tile_count, depth + 16, side), bf16), pltpu.VMEM(patterns.shape, bf16)],
        lazy=True,
    )[0]


def cut_kernel(bit, *refs):
    *held_refs, sent_ref, kept_ref = refs
    half = sent_ref.shape[2]
    bit = lax.axis_index("feat") // bit % 2
    mine = pl.multiple_of(bit * half, half)
    theirs = pl.multiple_of((1 - bit) * half, half)
    at = 0
    for ref in held_refs:
        for i in range(ref.shape[0]):
            sent_ref[at] = ref[i, :, pl.ds(theirs, half)]
            kept_ref[at] = ref[i, :, pl.ds(mine, half)]
            at += 1


def cut_rows(bit, parts, width):
    count = sum(p.shape[0] for p in parts)
    out = jax.ShapeDtypeStruct((count, parts[0].shape[1], width // 2), bf16)
    return local_call(
        functools.partial(cut_kernel, bit), "cut_rows", [out, out], parts
    )


def weight_kernel(*refs):
    *held_refs, out_ref = refs
    for i, ref in enumerate(held_refs):
        out_ref[i] = ref[0, :, ref.shape[2] - out_ref.shape[2] :]


def weight_pieces(parts, hid):
    out = jax.ShapeDtypeStruct((len(parts), parts[0].shape[1], hid), bf16)
    return local_call(weight_kernel, "weight_pieces", [out], parts)[0]


def relay_kernel(came_ref, near_ref, out_ref):
    width = came_ref.shape[2]
    out_ref[0, :, 0:width] = came_ref[1]
    out_ref[0, :, width:] = near_ref[0, :, near_ref.shape[2] - (out_ref.shape[2] - width) :]


def relayed(came, near):
    out = jax.ShapeDtypeStruct((1, came.shape[1], near.shape[2]), bf16)
    return local_call(relay_kernel, "relayed", [out], (came, near))[0]


def gather_kernel(*refs):
    *held_refs, out_ref = refs
    at = 0
    for ref in held_refs:
        out_ref[at : at + ref.shape[0]] = ref[...]
        at += ref.shape[0]


def gathered(parts):
    shape = (sum(p.shape[0] for p in parts), *parts[0].shape[1:])
    return local_call(gather_kernel, "gathered", [jax.ShapeDtypeStruct(shape, bf16)], parts)[0]


def flipped(masks, bit):
    return [m ^ bit for m in masks]


def features_in_order(row_masks, kept_ref, got_ref):
    half = kept_ref.shape[0]
    place = {mask: i for i, mask in enumerate(row_masks)}

    def features(mask, at=0, size=None):
        i = place[mask]
        ref = kept_ref if i < half else got_ref
        return ref[i % half, :, at : at + (size or ref.shape[2])]

    return features


def means_in_order(mean_ref):
    me = lax.axis_index("feat")

    def means(mask, at=0, size=None):
        return mean_ref[me ^ mask, :, at : at + (size or mean_ref.shape[2])]

    return means


def own_linear_kernel(row_masks, weight_masks, *refs):
    pieces = len(weight_masks)
    kept_ref, got_ref = refs[:2]
    mine_refs, other_refs = refs[2 : 2 + pieces], refs[2 + pieces : 2 + 2 * pieces]
    cot_ref, linear_ref, beside_ref = refs[2 + 2 * pieces :]
    features = features_in_order(row_masks, kept_ref, got_ref)
    side = lax.axis_index("dom") % 2

    def fill(self_refs, neighbour_refs):
        at = 0
        for ref in neighbour_refs:
            part = ref[...].reshape(-1, ref.shape[2])
            beside_ref[at : at + part.shape[0]] = part
            at += part.shape[0]
        beside_ref[at:] = cot_ref[...]
        fill_linear(features, weight_masks, self_refs, linear_ref, linear_ref, False)

    @pl.when(side == 0)
    def _():
        fill(mine_refs, other_refs)

    @pl.when(side != 0)
    def _():
        fill(other_refs, mine_refs)


def fill_linear(source, weight_masks, weight_refs, base_ref, linear_ref, more):
    rows, hid = linear_ref.shape
    step = min(256, rows)
    for at in range(0, rows, step):
        total = base_ref[at : at + step] if more else jnp.zeros((step, hid), f32)
        for masks, weight_ref in zip(weight_masks, weight_refs):
            part = jnp.concatenate([source(mask, at, step) for mask in masks], axis=0)
            total = total + lax.dot_general(
                part,
                weight_ref[...].reshape(-1, hid),
                first_with_first,
                preferred_element_type=f32,
            )
        linear_ref[at : at + step] = total


def forward_kernel(
    row_masks, masks, mean_ref, beside_ref, base_ref, kept_ref, got_ref,
    hidden_ref, grad_ref, other_sums_ref, my_sums_ref, linear_ref,
):
    features, means = features_in_order(row_masks, kept_ref, got_ref), means_in_order(mean_ref)
    rows = linear_ref.shape[0]
    depth = beside_ref.shape[0] - rows
    fill_linear(means, [masks], [beside_ref.at[0:depth]], base_ref, linear_ref, True)
    step = min(128, rows)
    for at in range(0, rows, step):
        value, slope = gelu_pair(linear_ref[at : at + step])
        hidden_ref[at : at + step] = value.astype(bf16)
        cot = beside_ref[depth + at : depth + at + step].astype(f32)
        grad_ref[at : at + step] = (cot * slope).astype(bf16)
    fill_sums(1, features, grad_ref, other_sums_ref)
    fill_sums(0, features, grad_ref, my_sums_ref)


def neighbour_sums_kernel(mean_ref, grad_ref, other_sums_ref, my_sums_ref):
    means = means_in_order(mean_ref)
    fill_sums(1, means, grad_ref, other_sums_ref)
    fill_sums(0, means, grad_ref, my_sums_ref)


def fill_sums(core, source, grad_ref, sums_ref):
    part = jnp.concatenate(
        [source(mask) for mask in range(core, 2 * sums_ref.shape[0], 2)], axis=0
    )
    sums = jnp.dot(part, grad_ref[...], preferred_element_type=f32)
    sums_ref[...] = sums.astype(sums_ref.dtype).reshape(sums_ref.shape)


def first_kernel(place, kept_ref, got_ref, out_ref, sent_ref):
    for at in range(kept_ref.shape[0]):
        far, rest = at // 4, (at // 2 % 2, at % 2)
        total = kept_ref[at] + got_ref[at].astype(f32)
        if rest[place] == 0:
            out_ref[far, rest[1 - place]] = total
        else:
            sent_ref[far, rest[1 - place]] = total.astype(bf16)


def second_kernel(kept_ref, got_ref, out_ref, sent_ref):
    for far in range(kept_ref.shape[0]):
        total = kept_ref[far] + got_ref[far].astype(f32)
        out_ref[far] = total[0]
        sent_ref[far] = total[1].astype(bf16)


def halving_kernel(kept_ref, got_ref, out_ref, sent_ref):
    half = out_ref.shape[0]
    for i in range(half):
        for at, ref in ((i, out_ref), (half + i, sent_ref)):
            ref[i] = (kept_ref[at] + got_ref[at].astype(f32)).astype(ref.dtype)


def round_sum_kernel(kept_ref, got_ref, out_ref):
    out_ref[...] = (kept_ref[...].astype(f32) + got_ref[...].astype(f32)).astype(out_ref.dtype)


def last_sum_kernel(*refs):
    for i, out_ref in enumerate(refs[4:]):
        kept_ref, got_ref = refs[2 * i : 2 * i + 2]
        out_ref[...] = (kept_ref[...].astype(f32) + got_ref[...].astype(f32))[0]


def finish_sum(kept, got):
    count, depth, hid = kept.shape
    while count > 1:
        count //= 2
        shape = (count, depth, hid)
        outs = [jax.ShapeDtypeStruct(shape, f32), jax.ShapeDtypeStruct(shape, bf16)]
        kept, sent = local_call(halving_kernel, "halving", outs, (kept, got))
        got = flip("feat", count * 8)(sent)
    rounded = jax.ShapeDtypeStruct(kept.shape, bf16)
    for bit in bits_of(lax.axis_size("dom")):
        (kept,) = local_call(round_sum_kernel, "rounded_sum", [rounded], (kept, got))
        got = flip("dom", bit)(kept)
    return kept, got


def sum_gradients(own_kept, own_got, neigh_kept, neigh_got):
    depth, hid = own_kept.shape[1:]
    far = lax.axis_size("feat") // 8

    def pair(*lead):
        shape = (*lead, depth, hid)
        return [jax.ShapeDtypeStruct(shape, f32), jax.ShapeDtypeStruct(shape, bf16)]

    own, own_sent = local_call(
        functools.partial(first_kernel, 1), "own_first", pair(far, 2), (own_kept, own_got)
    )
    own_got = flip("feat", 2)(own_sent)
    neigh, neigh_sent = local_call(
        functools.partial(first_kernel, 0), "neigh_first", pair(far, 2), (neigh_kept, neigh_got)
    )
    neigh_got = flip("feat", 4)(neigh_sent)
    own, own_sent = local_call(second_kernel, "own_second", pair(far), (own, own_got))
    own_got = flip("feat", 4)(own_sent)
    neigh, neigh_sent = local_call(second_kernel, "neigh_second", pair(far), (neigh, neigh_got))
    neigh_got = flip("feat", 2)(neigh_sent)
    out = jax.ShapeDtypeStruct((depth, hid), f32)
    last = (*finish_sum(own, own_got), *finish_sum(neigh, neigh_got))
    return local_call(last_sum_kernel, "last_sum", [out, out], last)


def on_device(
    features,
    self_weight,
    neighbour_weight,
    cotangent,
    send_rows,
    send_count,
    tile_source,
    tile_kind,
    tile_patterns,
):
    feat, dom = lax.axis_size("feat"), lax.axis_size("dom")
    count, depth = features.shape
    rows = count // feat
    hid = self_weight.shape[1]
    columns = features.T
    quarters, below = 4, feat // 4
    row_bits = list(reversed(bits_of(below)))
    picked, across, *cuts = open_exchange(
        send_count, columns, self_weight, neighbour_weight, send_rows, quarters
    )
    came = flip("feat", row_bits[0])(across)
    near = {i: flip("feat", i * below)(cuts[i]) for i in (3, 2, 1)}
    near = [cuts[0], near[1], near[2], near[3]]
    if dom == 2:
        halo = flip("dom", 1)(picked)
    else:
        halo = lax.all_to_all(picked, "dom", 1, 1, tiled=True)
    means = neighbour_means(
        tile_source[0].T, tile_kind[0].T, send_count, columns, halo, send_rows, tile_patterns, feat
    )
    came, means = lax.optimization_barrier((came, means))
    leaving = [came[0:1], relayed(came, near[2]), came[2:3], came[3:4]]
    far = leaving[:1] + [flip("feat", i * below)(leaving[i]) for i in range(1, quarters)]
    row_masks = [i * below for i in range(quarters)]
    pieces = [weight_pieces(near[:3], hid), weight_pieces(far[1:2], hid)]
    weight_masks = list(row_masks)
    row_masks = row_masks + flipped(row_masks, row_bits[0])
    for bit in row_bits[:-1]:
        pieces = pieces + [flip("feat", bit)(p) for p in pieces]
        weight_masks = weight_masks + flipped(weight_masks, bit)
    means, near, far, pieces = lax.optimization_barrier((means, near, far, pieces))
    own_mean = lax.all_to_all(means, "feat", 0, 0, tiled=True)
    pieces, weight_masks = [gathered(pieces)], [weight_masks]
    others = [flip("dom", 1)(p) for p in pieces]
    parts, width = [*near, *far], came.shape[2]
    for bit in row_bits[1:]:
        sent, kept = cut_rows(bit, parts, width)
        parts, width = [kept, flip("feat", bit)(sent)], width // 2
        row_masks = row_masks + flipped(row_masks, bit)
    pieces = pieces + [flip("feat", 1)(p) for p in pieces]
    others = others + [flip("feat", 1)(p) for p in others]
    weight_masks = weight_masks + [flipped(m, 1) for m in weight_masks]
    linear, beside = local_call(
        functools.partial(own_linear_kernel, row_masks, weight_masks),
        "own_linear",
        [
            jax.ShapeDtypeStruct((rows, hid), f32),
            jax.ShapeDtypeStruct((feat * depth + rows, hid), bf16),
        ],
        (*parts, *pieces, *others, cotangent),
    )
    square = jax.ShapeDtypeStruct((rows, hid), bf16)
    sums = (feat // 2, depth, hid)
    sums = [jax.ShapeDtypeStruct(sums, bf16), jax.ShapeDtypeStruct(sums, f32)]
    hidden, grad_linear, own_sent, own_kept = local_call(
        functools.partial(forward_kernel, row_masks, sum(weight_masks, [])),
        "forward",
        [square, square, *sums],
        (own_mean, beside, linear, *parts),
        scratch=[pltpu.VMEM((rows, hid), f32)],
    )
    own_got = flip("feat", 1)(own_sent)
    neigh_sent, neigh_kept = local_call(
        neighbour_sums_kernel, "neighbour_sums", sums, (own_mean, grad_linear)
    )
    neigh_got = flip("feat", 1)(neigh_sent)
    grad_self, grad_neighbour = sum_gradients(own_kept, own_got, neigh_kept, neigh_got)
    return (hidden, grad_self, grad_neighbour)


def solution(mesh):
    placed = (
        P("dom", "feat"),
        P("feat", None),
        P("feat", None),
        P(("dom", "feat"), None),
        P(),
        P(),
        P("dom", None, None),
        P("dom", None, None),
        P(),
    )
    return jax.shard_map(
        on_device,
        mesh=mesh,
        in_specs=placed,
        out_specs=(P(("dom", "feat"), None), P("feat", None), P("feat", None)),
        check_vma=False,
    )
```

```python
import functools

import jax
import jax.numpy as jnp
from jax import lax
from jax.experimental import pallas as pl
from jax.experimental.pallas import tpu as pltpu
from jax.sharding import PartitionSpec as P

inv_root_two = 0.7071067811865476
inv_root_two_pi = 0.3989422804014327
bf16 = jnp.bfloat16
f32 = jnp.float32
vmem_bytes = 16 * 2**20
most_vmem = 60 * 2**20
whole_vmem = pl.BlockSpec(memory_space=pltpu.VMEM)
whole_smem = pl.BlockSpec(memory_space=pltpu.SMEM)
anywhere = pl.BlockSpec(memory_space=pl.ANY)
whole_hbm = pl.BlockSpec(memory_space=pltpu.HBM)
last_with_last = (((1,), (1,)), ((), ()))
first_with_first = (((0,), (0,)), ((), ()))


def gelu_pair(linear):
    normal_cdf = 0.5 * (1.0 + lax.erf(linear * inv_root_two))
    density = jnp.exp(-0.5 * linear * linear) * inv_root_two_pi
    return (linear * normal_cdf, normal_cdf + linear * density)


def flip(axis, bit):
    size = lax.axis_size(axis)
    return functools.partial(
        lax.ppermute, axis_name=axis, perm=[(i, i ^ bit) for i in range(size)]
    )


def bits_of(size):
    return [1 << i for i in range(size.bit_length() - 1)]


def with_copies(kernel, lazy, still, operands, outs, *refs):
    given, refs = refs[:operands], refs[operands:]
    made, refs = refs[:outs], refs[outs:]
    moved = [i for i in range(operands) if i not in still]
    places, done, rest = refs[: len(moved)], refs[len(moved)], refs[len(moved) + 1 :]
    held = list(given)
    copies = {}
    for n, i in enumerate(moved):
        held[i] = places[n]
        copies[i] = pltpu.make_async_copy(given[i], places[n], done.at[n])
        copies[i].start()

    def ready(*which):
        for i in which:
            copies[i].wait()

    if lazy:
        kernel(ready, *held, *made, *rest)
    else:
        ready(*moved)
        kernel(*held, *made, *rest)


def local_call(
    kernel, name, outs, operands, scalars=0, scratch=(), fetch=False, lazy=False, still=(), limit=None
):
    in_specs = [whole_smem] * scalars + [whole_vmem] * (len(operands) - scalars)
    if fetch or lazy:
        limit = limit or most_vmem
        space = anywhere if limit == most_vmem else whole_hbm
        in_specs = [whole_vmem if i in still else space for i in range(len(operands))]
        held = [
            (pltpu.SMEM if i < scalars else pltpu.VMEM)(x.shape, x.dtype)
            for i, x in enumerate(operands)
            if i not in still
        ]
        scratch = [*held, pltpu.SemaphoreType.DMA((len(held),)), *scratch]
        kernel = functools.partial(with_copies, kernel, lazy, still, len(operands), len(outs))
    return pl.pallas_call(
        kernel,
        out_shape=outs,
        in_specs=in_specs,
        out_specs=[whole_vmem] * len(outs),
        scratch_shapes=list(scratch),
        cost_estimate=pl.CostEstimate(flops=0, bytes_accessed=0, transcendentals=0),
        compiler_params=pltpu.CompilerParams(vmem_limit_bytes=limit or vmem_bytes),
        name=name,
    )(*operands)


def pick(columns_ref, asked):
    count = columns_ref.shape[1]
    step = min(256, count)
    total = jnp.zeros((columns_ref.shape[0], asked.shape[1]), f32)
    for at in range(0, count, step):
        ids = lax.broadcasted_iota(jnp.int32, (step, asked.shape[1]), 0) + at
        one_hot = jnp.where(ids == asked, 1.0, 0.0).astype(bf16)
        total = total + jnp.dot(
            columns_ref[:, at : at + step], one_hot, preferred_element_type=f32
        )
    return total.astype(bf16)


def asked_rows(ask_ref, count_ref, part, to):
    slot = lax.broadcasted_iota(jnp.int32, (1, ask_ref.shape[2]), 1)
    return jnp.where(slot < count_ref[part, to], ask_ref[part, pl.ds(to, 1), :], -1)


def open_kernel(
    quarters, count_ref, columns_ref, self_ref, neighbour_ref, ask_ref, picked_ref, across_ref, *cut_refs
):
    me, part = lax.axis_index("feat"), lax.axis_index("dom")
    below = lax.axis_size("feat") // quarters
    quarter, half = me // below, me % below // (below // 2)
    weight = jnp.where(part % 2 == 0, self_ref[...], neighbour_ref[...])
    width = across_ref.shape[2]
    for i, cut_ref in enumerate(cut_refs):
        at = (quarter ^ i) * 2 + half
        cut_ref[0, :, 0:width] = columns_ref[:, pl.ds(pl.multiple_of(at * width, width), width)]
        if cut_ref.shape[2] > width:
            cut_ref[0, :, width:] = weight
        at = (quarter ^ i) * 2 + 1 - half
        across_ref[i] = columns_ref[:, pl.ds(pl.multiple_of(at * width, width), width)]
    parts = ask_ref.shape[1]
    if parts == 2:
        asked = asked_rows(ask_ref, count_ref, part, 1 - part)
    else:
        asked = jnp.concatenate(
            [asked_rows(ask_ref, count_ref, part, to) for to in range(parts)], axis=1
        )
    picked_ref[...] = pick(columns_ref, asked)


def open_exchange(counts, columns, self_weight, neighbour_weight, asks, quarters):
    depth, count = columns.shape
    width = count // quarters // 2
    parts, slots = asks.shape[1:]
    asked = slots if parts == 2 else parts * slots
    return local_call(
        functools.partial(open_kernel, quarters),
        "open_exchange",
        [
            jax.ShapeDtypeStruct((depth, asked), bf16),
            jax.ShapeDtypeStruct((quarters, depth, width), bf16),
        ]
        + [jax.ShapeDtypeStruct((1, depth, width + self_weight.shape[1]), bf16)] * (quarters - 1)
        + [jax.ShapeDtypeStruct((1, depth, width), bf16)],
        (counts, columns, self_weight, neighbour_weight, asks),
        scalars=1,
        fetch=True,
    )


def mean_kernel(
    unroll, ready, source_ref, kind_ref, count_ref, local_ref, halo_ref, ask_ref, pattern_ref, mean_ref, tiles, turned
):
    depth = local_ref.shape[0]
    side = pattern_ref.shape[1]
    local_tiles, halo_tiles = local_ref.shape[1] // side, halo_ref.shape[1] // side
    ready(2, 3, 5)
    for i in range(local_tiles):
        tiles[i, 0:depth, :] = local_ref[:, i * side : (i + 1) * side]
    first = local_tiles
    if ask_ref.shape[1] == 2:
        part = lax.axis_index("dom")
        own = pick(local_ref, asked_rows(ask_ref, count_ref, part, part))
        for i in range(halo_tiles):
            tiles[local_tiles + part * halo_tiles + i, 0:depth, :] = own[:, i * side : (i + 1) * side]
        first = local_tiles + (1 - part) * halo_tiles
    ready(4)
    for i in range(halo_tiles):
        tiles[first + i, 0:depth, :] = halo_ref[:, i * side : (i + 1) * side]
    tiles[:, depth:, :] = jnp.ones((tiles.shape[0], tiles.shape[1] - depth, side), bf16)
    per_block = mean_ref.shape[2] // side
    ready(0, 1, 6)
    for i in range(pattern_ref.shape[0]):
        turned[i] = pattern_ref[i].T

    def one(t):
        rows = [tiles[source_ref[k, t]] for k in range(source_ref.shape[0])]
        weights = [turned[kind_ref[k, t]] for k in range(source_ref.shape[0])]
        summed = lax.dot_general(
            jnp.concatenate(rows, 1),
            jnp.concatenate(weights, 0),
            (((1,), (0,)), ((), ())),
            preferred_element_type=f32,
        )
        mean = (summed[0:depth] / summed[depth : depth + 1]).astype(bf16)
        at = lax.rem(t, per_block) * side
        mean_ref[lax.div(t, per_block), :, pl.ds(pl.multiple_of(at, side), side)] = mean

    @pl.loop(0, source_ref.shape[1] // unroll)
    def _(step):
        for u in range(unroll):
            one(step * unroll + u)


def neighbour_means(source, kind, counts, local, halo, asks, patterns, blocks):
    depth, count = local.shape
    side = patterns.shape[1]
    tile_count = (count + asks.shape[1] * asks.shape[2]) // side
    return local_call(
        functools.partial(mean_kernel, 16 if source.shape[1] % 16 == 0 else 1),
        "neighbour_means",
        [jax.ShapeDtypeStruct((blocks, depth, count // blocks), bf16)],
        (source, kind, counts, local, halo, asks, patterns),
        scalars=3,
        scratch=[pltpu.VMEM((tile_count, depth + 16, side), bf16), pltpu.VMEM(patterns.shape, bf16)],
        lazy=True,
    )[0]


def cut_kernel(bit, *refs):
    *held_refs, sent_ref, kept_ref = refs
    half = sent_ref.shape[2]
    bit = lax.axis_index("feat") // bit % 2
    mine = pl.multiple_of(bit * half, half)
    theirs = pl.multiple_of((1 - bit) * half, half)
    at = 0
    for ref in held_refs:
        for i in range(ref.shape[0]):
            sent_ref[at] = ref[i, :, pl.ds(theirs, half)]
            kept_ref[at] = ref[i, :, pl.ds(mine, half)]
            at += 1


def cut_rows(bit, parts, width):
    count = sum(p.shape[0] for p in parts)
    out = jax.ShapeDtypeStruct((count, parts[0].shape[1], width // 2), bf16)
    return local_call(
        functools.partial(cut_kernel, bit), "cut_rows", [out, out], parts
    )


def weight_kernel(*refs):
    *held_refs, out_ref = refs
    for i, ref in enumerate(held_refs):
        out_ref[i] = ref[0, :, ref.shape[2] - out_ref.shape[2] :]


def weight_pieces(parts, hid):
    out = jax.ShapeDtypeStruct((len(parts), parts[0].shape[1], hid), bf16)
    return local_call(weight_kernel, "weight_pieces", [out], parts)[0]


def relay_kernel(came_ref, near_ref, out_ref):
    width = came_ref.shape[2]
    out_ref[0, :, 0:width] = came_ref[1]
    out_ref[0, :, width:] = near_ref[0, :, near_ref.shape[2] - (out_ref.shape[2] - width) :]


def relayed(came, near):
    out = jax.ShapeDtypeStruct((1, came.shape[1], near.shape[2]), bf16)
    return local_call(relay_kernel, "relayed", [out], (came, near))[0]


def gather_kernel(*refs):
    *held_refs, out_ref = refs
    at = 0
    for ref in held_refs:
        out_ref[at : at + ref.shape[0]] = ref[...]
        at += ref.shape[0]


def gathered(parts):
    shape = (sum(p.shape[0] for p in parts), *parts[0].shape[1:])
    return local_call(gather_kernel, "gathered", [jax.ShapeDtypeStruct(shape, bf16)], parts)[0]


def flipped(masks, bit):
    return [m ^ bit for m in masks]


def features_in_order(row_masks, kept_ref, got_ref):
    half = kept_ref.shape[0]
    place = {mask: i for i, mask in enumerate(row_masks)}

    def features(mask, at=0, size=None):
        i = place[mask]
        ref = kept_ref if i < half else got_ref
        return ref[i % half, :, at : at + (size or ref.shape[2])]

    return features


def means_in_order(mean_ref):
    me = lax.axis_index("feat")

    def means(mask, at=0, size=None):
        return mean_ref[me ^ mask, :, at : at + (size or mean_ref.shape[2])]

    return means


def own_linear_kernel(row_masks, weight_masks, *refs):
    pieces = len(weight_masks)
    kept_ref, got_ref = refs[:2]
    mine_refs, other_refs = refs[2 : 2 + pieces], refs[2 + pieces : 2 + 2 * pieces]
    cot_ref, linear_ref, beside_ref = refs[2 + 2 * pieces :]
    features = features_in_order(row_masks, kept_ref, got_ref)
    side = lax.axis_index("dom") % 2

    def fill(self_refs, neighbour_refs):
        at = 0
        for ref in neighbour_refs:
            part = ref[...].reshape(-1, ref.shape[2])
            beside_ref[at : at + part.shape[0]] = part
            at += part.shape[0]
        beside_ref[at:] = cot_ref[...]
        fill_linear(features, weight_masks, self_refs, linear_ref, linear_ref, False)

    @pl.when(side == 0)
    def _():
        fill(mine_refs, other_refs)

    @pl.when(side != 0)
    def _():
        fill(other_refs, mine_refs)


def fill_linear(source, weight_masks, weight_refs, base_ref, linear_ref, more):
    rows, hid = linear_ref.shape
    step = min(256, rows)
    for at in range(0, rows, step):
        total = base_ref[at : at + step] if more else jnp.zeros((step, hid), f32)
        for masks, weight_ref in zip(weight_masks, weight_refs):
            part = jnp.concatenate([source(mask, at, step) for mask in masks], axis=0)
            total = total + lax.dot_general(
                part,
                weight_ref[...].reshape(-1, hid),
                first_with_first,
                preferred_element_type=f32,
            )
        linear_ref[at : at + step] = total


def forward_kernel(
    row_masks, masks, mean_ref, beside_ref, base_ref, kept_ref, got_ref,
    hidden_ref, other_own_ref, my_own_ref, other_neigh_ref, my_neigh_ref, linear_ref, grad_ref,
):
    features, means = features_in_order(row_masks, kept_ref, got_ref), means_in_order(mean_ref)
    rows = linear_ref.shape[0]
    depth = beside_ref.shape[0] - rows
    fill_linear(means, [masks], [beside_ref.at[0:depth]], base_ref, linear_ref, True)
    step = min(128, rows)
    for at in range(0, rows, step):
        value, slope = gelu_pair(linear_ref[at : at + step])
        hidden_ref[at : at + step] = value.astype(bf16)
        cot = beside_ref[depth + at : depth + at + step].astype(f32)
        grad_ref[at : at + step] = (cot * slope).astype(bf16)
    fill_sums(1, features, grad_ref, other_own_ref)
    fill_sums(1, means, grad_ref, other_neigh_ref)
    fill_sums(0, features, grad_ref, my_own_ref)
    fill_sums(0, means, grad_ref, my_neigh_ref)


def fill_sums(core, source, grad_ref, sums_ref):
    part = jnp.concatenate(
        [source(mask) for mask in range(core, 2 * sums_ref.shape[0], 2)], axis=0
    )
    sums = jnp.dot(part, grad_ref[...], preferred_element_type=f32)
    sums_ref[...] = sums.astype(sums_ref.dtype).reshape(sums_ref.shape)


def first_kernel(place, kept_ref, got_ref, out_ref, sent_ref):
    for at in range(kept_ref.shape[0]):
        far, rest = at // 4, (at // 2 % 2, at % 2)
        total = kept_ref[at] + got_ref[at].astype(f32)
        if rest[place] == 0:
            out_ref[far, rest[1 - place]] = total
        else:
            sent_ref[far, rest[1 - place]] = total.astype(bf16)


def second_kernel(kept_ref, got_ref, out_ref, sent_ref):
    for far in range(kept_ref.shape[0]):
        total = kept_ref[far] + got_ref[far].astype(f32)
        out_ref[far] = total[0]
        sent_ref[far] = total[1].astype(bf16)


def halving_kernel(kept_ref, got_ref, out_ref, sent_ref):
    half = out_ref.shape[0]
    for i in range(half):
        for at, ref in ((i, out_ref), (half + i, sent_ref)):
            ref[i] = (kept_ref[at] + got_ref[at].astype(f32)).astype(ref.dtype)


def round_sum_kernel(kept_ref, got_ref, out_ref):
    out_ref[...] = (kept_ref[...].astype(f32) + got_ref[...].astype(f32)).astype(out_ref.dtype)


def last_sum_kernel(*refs):
    for i, out_ref in enumerate(refs[4:]):
        kept_ref, got_ref = refs[2 * i : 2 * i + 2]
        out_ref[...] = (kept_ref[...].astype(f32) + got_ref[...].astype(f32))[0]


def finish_sum(kept, got):
    count, depth, hid = kept.shape
    while count > 1:
        count //= 2
        shape = (count, depth, hid)
        outs = [jax.ShapeDtypeStruct(shape, f32), jax.ShapeDtypeStruct(shape, bf16)]
        kept, sent = local_call(halving_kernel, "halving", outs, (kept, got))
        got = flip("feat", count * 8)(sent)
    rounded = jax.ShapeDtypeStruct(kept.shape, bf16)
    for bit in bits_of(lax.axis_size("dom")):
        (kept,) = local_call(round_sum_kernel, "rounded_sum", [rounded], (kept, got))
        got = flip("dom", bit)(kept)
    return kept, got


def sum_gradients(own_kept, own_got, neigh_kept, neigh_got):
    depth, hid = own_kept.shape[1:]
    far = lax.axis_size("feat") // 8

    def pair(*lead):
        shape = (*lead, depth, hid)
        return [jax.ShapeDtypeStruct(shape, f32), jax.ShapeDtypeStruct(shape, bf16)]

    own, own_sent = local_call(
        functools.partial(first_kernel, 1), "own_first", pair(far, 2), (own_kept, own_got)
    )
    own_got = flip("feat", 2)(own_sent)
    neigh, neigh_sent = local_call(
        functools.partial(first_kernel, 0), "neigh_first", pair(far, 2), (neigh_kept, neigh_got)
    )
    neigh_got = flip("feat", 4)(neigh_sent)
    own, own_sent = local_call(second_kernel, "own_second", pair(far), (own, own_got))
    own_got = flip("feat", 4)(own_sent)
    neigh, neigh_sent = local_call(second_kernel, "neigh_second", pair(far), (neigh, neigh_got))
    neigh_got = flip("feat", 2)(neigh_sent)
    out = jax.ShapeDtypeStruct((depth, hid), f32)
    last = (*finish_sum(own, own_got), *finish_sum(neigh, neigh_got))
    return local_call(last_sum_kernel, "last_sum", [out, out], last)


def on_device(
    features,
    self_weight,
    neighbour_weight,
    cotangent,
    send_rows,
    send_count,
    tile_source,
    tile_kind,
    tile_patterns,
):
    feat, dom = lax.axis_size("feat"), lax.axis_size("dom")
    count, depth = features.shape
    rows = count // feat
    hid = self_weight.shape[1]
    columns = features.T
    quarters, below = 4, feat // 4
    row_bits = list(reversed(bits_of(below)))
    picked, across, *cuts = open_exchange(
        send_count, columns, self_weight, neighbour_weight, send_rows, quarters
    )
    came = flip("feat", row_bits[0])(across)
    near = {i: flip("feat", i * below)(cuts[i]) for i in (3, 2, 1)}
    near = [cuts[0], near[1], near[2], near[3]]
    if dom == 2:
        halo = flip("dom", 1)(picked)
    else:
        halo = lax.all_to_all(picked, "dom", 1, 1, tiled=True)
    means = neighbour_means(
        tile_source[0].T, tile_kind[0].T, send_count, columns, halo, send_rows, tile_patterns, feat
    )
    came, means = lax.optimization_barrier((came, means))
    leaving = [came[0:1], relayed(came, near[2]), came[2:3], came[3:4]]
    far = leaving[:1] + [flip("feat", i * below)(leaving[i]) for i in range(1, quarters)]
    row_masks = [i * below for i in range(quarters)]
    pieces = [weight_pieces(near[:3], hid), weight_pieces(far[1:2], hid)]
    weight_masks = list(row_masks)
    row_masks = row_masks + flipped(row_masks, row_bits[0])
    for bit in row_bits[:-1]:
        pieces = pieces + [flip("feat", bit)(p) for p in pieces]
        weight_masks = weight_masks + flipped(weight_masks, bit)
    means, near, far, pieces = lax.optimization_barrier((means, near, far, pieces))
    own_mean = lax.all_to_all(means, "feat", 0, 0, tiled=True)
    pieces, weight_masks = [gathered(pieces)], [weight_masks]
    others = [flip("dom", 1)(p) for p in pieces]
    parts, width = [*near, *far], came.shape[2]
    for bit in row_bits[1:]:
        sent, kept = cut_rows(bit, parts, width)
        parts, width = [kept, flip("feat", bit)(sent)], width // 2
        row_masks = row_masks + flipped(row_masks, bit)
    pieces = pieces + [flip("feat", 1)(p) for p in pieces]
    others = others + [flip("feat", 1)(p) for p in others]
    weight_masks = weight_masks + [flipped(m, 1) for m in weight_masks]
    linear, beside = local_call(
        functools.partial(own_linear_kernel, row_masks, weight_masks),
        "own_linear",
        [
            jax.ShapeDtypeStruct((rows, hid), f32),
            jax.ShapeDtypeStruct((feat * depth + rows, hid), bf16),
        ],
        (*parts, *pieces, *others, cotangent),
    )
    square = jax.ShapeDtypeStruct((rows, hid), bf16)
    sums = (feat // 2, depth, hid)
    sums = [jax.ShapeDtypeStruct(sums, bf16), jax.ShapeDtypeStruct(sums, f32)]
    hidden, own_sent, own_kept, neigh_sent, neigh_kept = local_call(
        functools.partial(forward_kernel, row_masks, sum(weight_masks, [])),
        "forward",
        [square, *sums, *sums],
        (own_mean, beside, linear, *parts),
        scratch=[pltpu.VMEM((rows, hid), f32), pltpu.VMEM((rows, hid), bf16)],
    )
    own_got, neigh_got = flip("feat", 1)(own_sent), flip("feat", 1)(neigh_sent)
    grad_self, grad_neighbour = sum_gradients(own_kept, own_got, neigh_kept, neigh_got)
    return (hidden, grad_self, grad_neighbour)


def solution(mesh):
    placed = (
        P("dom", "feat"),
        P("feat", None),
        P("feat", None),
        P(("dom", "feat"), None),
        P(),
        P(),
        P("dom", None, None),
        P("dom", None, None),
        P(),
    )
    return jax.shard_map(
        on_device,
        mesh=mesh,
        in_specs=placed,
        out_specs=(P(("dom", "feat"), None), P("feat", None), P("feat", None)),
        check_vma=False,
    )
```

```python
import functools

import jax
import jax.numpy as jnp
from jax import lax
from jax.experimental import pallas as pl
from jax.experimental.pallas import tpu as pltpu
from jax.sharding import PartitionSpec as P

inv_root_two = 0.7071067811865476
inv_root_two_pi = 0.3989422804014327
bf16 = jnp.bfloat16
f32 = jnp.float32
vmem_bytes = 16 * 2**20
most_vmem = 54 * 2**20
whole_vmem = pl.BlockSpec(memory_space=pltpu.VMEM)
whole_smem = pl.BlockSpec(memory_space=pltpu.SMEM)
anywhere = pl.BlockSpec(memory_space=pl.ANY)
whole_hbm = pl.BlockSpec(memory_space=pltpu.HBM)
last_with_last = (((1,), (1,)), ((), ()))
first_with_first = (((0,), (0,)), ((), ()))


def gelu_pair(linear):
    normal_cdf = 0.5 * (1.0 + lax.erf(linear * inv_root_two))
    density = jnp.exp(-0.5 * linear * linear) * inv_root_two_pi
    return (linear * normal_cdf, normal_cdf + linear * density)


def flip(axis, bit):
    size = lax.axis_size(axis)
    return functools.partial(
        lax.ppermute, axis_name=axis, perm=[(i, i ^ bit) for i in range(size)]
    )


def bits_of(size):
    return [1 << i for i in range(size.bit_length() - 1)]


def with_copies(kernel, lazy, still, operands, outs, *refs):
    given, refs = refs[:operands], refs[operands:]
    made, refs = refs[:outs], refs[outs:]
    moved = [i for i in range(operands) if i not in still]
    places, done, rest = refs[: len(moved)], refs[len(moved)], refs[len(moved) + 1 :]
    held = list(given)
    copies = {}
    for n, i in enumerate(moved):
        held[i] = places[n]
        copies[i] = pltpu.make_async_copy(given[i], places[n], done.at[n])
        copies[i].start()

    def ready(*which):
        for i in which:
            copies[i].wait()

    if lazy:
        kernel(ready, *held, *made, *rest)
    else:
        ready(*moved)
        kernel(*held, *made, *rest)


def local_call(
    kernel, name, outs, operands, scalars=0, scratch=(), fetch=False, lazy=False, still=(), limit=None
):
    in_specs = [whole_smem] * scalars + [whole_vmem] * (len(operands) - scalars)
    if fetch or lazy:
        limit = limit or most_vmem
        space = anywhere if limit == most_vmem else whole_hbm
        in_specs = [whole_vmem if i in still else space for i in range(len(operands))]
        held = [
            (pltpu.SMEM if i < scalars else pltpu.VMEM)(x.shape, x.dtype)
            for i, x in enumerate(operands)
            if i not in still
        ]
        scratch = [*held, pltpu.SemaphoreType.DMA((len(held),)), *scratch]
        kernel = functools.partial(with_copies, kernel, lazy, still, len(operands), len(outs))
    return pl.pallas_call(
        kernel,
        out_shape=outs,
        in_specs=in_specs,
        out_specs=[whole_vmem] * len(outs),
        scratch_shapes=list(scratch),
        cost_estimate=pl.CostEstimate(flops=0, bytes_accessed=0, transcendentals=0),
        compiler_params=pltpu.CompilerParams(vmem_limit_bytes=limit or vmem_bytes),
        name=name,
    )(*operands)


def pick(columns_ref, asked):
    depth, count = columns_ref.shape
    span = 256 if count % 256 == 0 else count
    spans = count // span
    low = lax.rem(asked + span, span)
    high = lax.div(asked + span, span) - 1
    ids = lax.broadcasted_iota(jnp.int32, (span, asked.shape[1]), 0)
    one_hot = jnp.where(ids == low, 1.0, 0.0).astype(bf16)
    total = jnp.zeros((depth, asked.shape[1]), f32)
    group = 8 if spans % 8 == 0 else 1
    for first in range(0, spans, group):
        rows = [columns_ref[:, i * span : (i + 1) * span] for i in range(first, first + group)]
        found = jnp.dot(jnp.concatenate(rows, 0), one_hot, preferred_element_type=f32)
        for i in range(group):
            total = total + jnp.where(high == first + i, found[i * depth : (i + 1) * depth], 0.0)
    return total.astype(bf16)


def asked_rows(ask_ref, count_ref, part, to):
    slot = lax.broadcasted_iota(jnp.int32, (1, ask_ref.shape[2]), 1)
    return jnp.where(slot < count_ref[part, to], ask_ref[part, pl.ds(to, 1), :], -1)


def open_kernel(
    quarters, count_ref, columns_ref, self_ref, neighbour_ref, ask_ref, picked_ref, across_ref, *cut_refs
):
    me, part = lax.axis_index("feat"), lax.axis_index("dom")
    below = lax.axis_size("feat") // quarters
    quarter, half = me // below, me % below // (below // 2)
    weight = jnp.where(part % 2 == 0, self_ref[...], neighbour_ref[...])
    width = across_ref.shape[2]
    for i, cut_ref in enumerate(cut_refs):
        at = (quarter ^ i) * 2 + half
        cut_ref[0, :, 0:width] = columns_ref[:, pl.ds(pl.multiple_of(at * width, width), width)]
        if cut_ref.shape[2] > width:
            cut_ref[0, :, width:] = weight
        at = (quarter ^ i) * 2 + 1 - half
        across_ref[i] = columns_ref[:, pl.ds(pl.multiple_of(at * width, width), width)]
    parts = ask_ref.shape[1]
    if parts == 2:
        asked = asked_rows(ask_ref, count_ref, part, 1 - part)
    else:
        asked = jnp.concatenate(
            [asked_rows(ask_ref, count_ref, part, to) for to in range(parts)], axis=1
        )
    picked_ref[...] = pick(columns_ref, asked)


def open_exchange(counts, columns, self_weight, neighbour_weight, asks, quarters):
    depth, count = columns.shape
    width = count // quarters // 2
    parts, slots = asks.shape[1:]
    asked = slots if parts == 2 else parts * slots
    return local_call(
        functools.partial(open_kernel, quarters),
        "open_exchange",
        [
            jax.ShapeDtypeStruct((depth, asked), bf16),
            jax.ShapeDtypeStruct((quarters, depth, width), bf16),
        ]
        + [jax.ShapeDtypeStruct((1, depth, width + self_weight.shape[1]), bf16)] * (quarters - 1)
        + [jax.ShapeDtypeStruct((1, depth, width), bf16)],
        (counts, columns, self_weight, neighbour_weight, asks),
        scalars=1,
        fetch=True,
    )


def mean_kernel(
    unroll, ready, source_ref, kind_ref, count_ref, local_ref, halo_ref, ask_ref, pattern_ref, mean_ref, tiles, turned
):
    depth = local_ref.shape[0]
    side = pattern_ref.shape[1]
    local_tiles, halo_tiles = local_ref.shape[1] // side, halo_ref.shape[1] // side
    ready(2, 3, 5)
    for i in range(local_tiles):
        tiles[i, 0:depth, :] = local_ref[:, i * side : (i + 1) * side]
    first = local_tiles
    if ask_ref.shape[1] == 2:
        part = lax.axis_index("dom")
        own = pick(local_ref, asked_rows(ask_ref, count_ref, part, part))
        for i in range(halo_tiles):
            tiles[local_tiles + part * halo_tiles + i, 0:depth, :] = own[:, i * side : (i + 1) * side]
        first = local_tiles + (1 - part) * halo_tiles
    ready(4)
    for i in range(halo_tiles):
        tiles[first + i, 0:depth, :] = halo_ref[:, i * side : (i + 1) * side]
    tiles[:, depth:, :] = jnp.ones((tiles.shape[0], tiles.shape[1] - depth, side), bf16)
    per_block = mean_ref.shape[2] // side
    ready(0, 1, 6)
    for i in range(pattern_ref.shape[0]):
        turned[i] = pattern_ref[i].T

    def one(t):
        rows = [tiles[source_ref[k, t]] for k in range(source_ref.shape[0])]
        weights = [turned[kind_ref[k, t]] for k in range(source_ref.shape[0])]
        summed = lax.dot_general(
            jnp.concatenate(rows, 1),
            jnp.concatenate(weights, 0),
            (((1,), (0,)), ((), ())),
            preferred_element_type=f32,
        )
        mean = (summed[0:depth] / summed[depth : depth + 1]).astype(bf16)
        at = lax.rem(t, per_block) * side
        mean_ref[lax.div(t, per_block), :, pl.ds(pl.multiple_of(at, side), side)] = mean

    @pl.loop(0, source_ref.shape[1] // unroll)
    def _(step):
        for u in range(unroll):
            one(step * unroll + u)


def neighbour_means(source, kind, counts, local, halo, asks, patterns, blocks):
    depth, count = local.shape
    side = patterns.shape[1]
    tile_count = (count + asks.shape[1] * asks.shape[2]) // side
    return local_call(
        functools.partial(mean_kernel, 16 if source.shape[1] % 16 == 0 else 1),
        "neighbour_means",
        [jax.ShapeDtypeStruct((blocks, depth, count // blocks), bf16)],
        (source, kind, counts, local, halo, asks, patterns),
        scalars=3,
        scratch=[pltpu.VMEM((tile_count, depth + 16, side), bf16), pltpu.VMEM(patterns.shape, bf16)],
        lazy=True,
    )[0]


def cut_kernel(bit, *refs):
    *held_refs, sent_ref, kept_ref = refs
    half = sent_ref.shape[2]
    bit = lax.axis_index("feat") // bit % 2
    mine = pl.multiple_of(bit * half, half)
    theirs = pl.multiple_of((1 - bit) * half, half)
    at = 0
    for ref in held_refs:
        for i in range(ref.shape[0]):
            sent_ref[at] = ref[i, :, pl.ds(theirs, half)]
            kept_ref[at] = ref[i, :, pl.ds(mine, half)]
            at += 1


def cut_rows(bit, parts, width):
    count = sum(p.shape[0] for p in parts)
    out = jax.ShapeDtypeStruct((count, parts[0].shape[1], width // 2), bf16)
    return local_call(
        functools.partial(cut_kernel, bit), "cut_rows", [out, out], parts
    )


def weight_kernel(*refs):
    *held_refs, out_ref = refs
    for i, ref in enumerate(held_refs):
        out_ref[i] = ref[0, :, ref.shape[2] - out_ref.shape[2] :]


def weight_pieces(parts, hid):
    out = jax.ShapeDtypeStruct((len(parts), parts[0].shape[1], hid), bf16)
    return local_call(weight_kernel, "weight_pieces", [out], parts)[0]


def relay_kernel(came_ref, near_ref, out_ref):
    width = came_ref.shape[2]
    out_ref[0, :, 0:width] = came_ref[1]
    out_ref[0, :, width:] = near_ref[0, :, near_ref.shape[2] - (out_ref.shape[2] - width) :]


def relayed(came, near):
    out = jax.ShapeDtypeStruct((1, came.shape[1], near.shape[2]), bf16)
    return local_call(relay_kernel, "relayed", [out], (came, near))[0]


def gather_kernel(*refs):
    *held_refs, out_ref = refs
    at = 0
    for ref in held_refs:
        out_ref[at : at + ref.shape[0]] = ref[...]
        at += ref.shape[0]


def gathered(parts):
    shape = (sum(p.shape[0] for p in parts), *parts[0].shape[1:])
    return local_call(gather_kernel, "gathered", [jax.ShapeDtypeStruct(shape, bf16)], parts)[0]


def flipped(masks, bit):
    return [m ^ bit for m in masks]


def features_in_order(row_masks, kept_ref, got_ref):
    half = kept_ref.shape[0]
    place = {mask: i for i, mask in enumerate(row_masks)}

    def features(mask, at=0, size=None):
        i = place[mask]
        ref = kept_ref if i < half else got_ref
        return ref[i % half, :, at : at + (size or ref.shape[2])]

    return features


def means_in_order(mean_ref):
    me = lax.axis_index("feat")

    def means(mask, at=0, size=None):
        return mean_ref[me ^ mask, :, at : at + (size or mean_ref.shape[2])]

    return means


def own_linear_kernel(row_masks, weight_masks, *refs):
    pieces = len(weight_masks)
    kept_ref, got_ref = refs[:2]
    mine_refs, other_refs = refs[2 : 2 + pieces], refs[2 + pieces : 2 + 2 * pieces]
    cot_ref, linear_ref, beside_ref = refs[2 + 2 * pieces :]
    features = features_in_order(row_masks, kept_ref, got_ref)
    side = lax.axis_index("dom") % 2

    def fill(self_refs, neighbour_refs):
        at = 0
        for ref in neighbour_refs:
            part = ref[...].reshape(-1, ref.shape[2])
            beside_ref[at : at + part.shape[0]] = part
            at += part.shape[0]
        beside_ref[at:] = cot_ref[...]
        fill_linear(features, weight_masks, self_refs, linear_ref, linear_ref, False)

    @pl.when(side == 0)
    def _():
        fill(mine_refs, other_refs)

    @pl.when(side != 0)
    def _():
        fill(other_refs, mine_refs)


def fill_linear(source, weight_masks, weight_refs, base_ref, linear_ref, more):
    rows, hid = linear_ref.shape
    step = min(512, rows)
    for at in range(0, rows, step):
        total = base_ref[at : at + step] if more else jnp.zeros((step, hid), f32)
        for masks, weight_ref in zip(weight_masks, weight_refs):
            part = jnp.concatenate([source(mask, at, step) for mask in masks], axis=0)
            total = total + lax.dot_general(
                part,
                weight_ref[...].reshape(-1, hid),
                first_with_first,
                preferred_element_type=f32,
            )
        linear_ref[at : at + step] = total


def forward_kernel(
    row_masks, masks, mean_ref, beside_ref, base_ref, kept_ref, got_ref,
    hidden_ref, grad_ref, other_sums_ref, my_sums_ref, linear_ref,
):
    features, means = features_in_order(row_masks, kept_ref, got_ref), means_in_order(mean_ref)
    rows = linear_ref.shape[0]
    depth = beside_ref.shape[0] - rows
    fill_linear(means, [masks], [beside_ref.at[0:depth]], base_ref, linear_ref, True)
    step = min(128, rows)
    for at in range(0, rows, step):
        value, slope = gelu_pair(linear_ref[at : at + step])
        hidden_ref[at : at + step] = value.astype(bf16)
        cot = beside_ref[depth + at : depth + at + step].astype(f32)
        grad_ref[at : at + step] = (cot * slope).astype(bf16)
    fill_sums(1, features, grad_ref, other_sums_ref)
    fill_sums(0, features, grad_ref, my_sums_ref)


def neighbour_sums_kernel(mean_ref, grad_ref, other_sums_ref, my_sums_ref):
    means = means_in_order(mean_ref)
    fill_sums(1, means, grad_ref, other_sums_ref)
    fill_sums(0, means, grad_ref, my_sums_ref)


def fill_sums(core, source, grad_ref, sums_ref):
    part = jnp.concatenate(
        [source(mask) for mask in range(core, 2 * sums_ref.shape[0], 2)], axis=0
    )
    sums = jnp.dot(part, grad_ref[...], preferred_element_type=f32)
    sums_ref[...] = sums.astype(sums_ref.dtype).reshape(sums_ref.shape)


def first_kernel(place, kept_ref, got_ref, out_ref, sent_ref):
    for at in range(kept_ref.shape[0]):
        far, rest = at // 4, (at // 2 % 2, at % 2)
        total = kept_ref[at] + got_ref[at].astype(f32)
        if rest[place] == 0:
            out_ref[far, rest[1 - place]] = total
        else:
            sent_ref[far, rest[1 - place]] = total.astype(bf16)


def second_kernel(kept_ref, got_ref, out_ref, sent_ref):
    for far in range(kept_ref.shape[0]):
        total = kept_ref[far] + got_ref[far].astype(f32)
        out_ref[far] = total[0]
        sent_ref[far] = total[1].astype(bf16)


def halving_kernel(kept_ref, got_ref, out_ref, sent_ref):
    half = out_ref.shape[0]
    for i in range(half):
        for at, ref in ((i, out_ref), (half + i, sent_ref)):
            ref[i] = (kept_ref[at] + got_ref[at].astype(f32)).astype(ref.dtype)


def round_sum_kernel(kept_ref, got_ref, out_ref):
    out_ref[...] = (kept_ref[...].astype(f32) + got_ref[...].astype(f32)).astype(out_ref.dtype)


def last_sum_kernel(*refs):
    for i, out_ref in enumerate(refs[4:]):
        kept_ref, got_ref = refs[2 * i : 2 * i + 2]
        out_ref[...] = (kept_ref[...].astype(f32) + got_ref[...].astype(f32))[0]


def finish_sum(kept, got):
    count, depth, hid = kept.shape
    while count > 1:
        count //= 2
        shape = (count, depth, hid)
        outs = [jax.ShapeDtypeStruct(shape, f32), jax.ShapeDtypeStruct(shape, bf16)]
        kept, sent = local_call(halving_kernel, "halving", outs, (kept, got))
        got = flip("feat", count * 8)(sent)
    rounded = jax.ShapeDtypeStruct(kept.shape, bf16)
    for bit in bits_of(lax.axis_size("dom")):
        (kept,) = local_call(round_sum_kernel, "rounded_sum", [rounded], (kept, got))
        got = flip("dom", bit)(kept)
    return kept, got


def sum_gradients(own_kept, own_got, neigh_kept, neigh_got):
    depth, hid = own_kept.shape[1:]
    far = lax.axis_size("feat") // 8

    def pair(*lead):
        shape = (*lead, depth, hid)
        return [jax.ShapeDtypeStruct(shape, f32), jax.ShapeDtypeStruct(shape, bf16)]

    own, own_sent = local_call(
        functools.partial(first_kernel, 1), "own_first", pair(far, 2), (own_kept, own_got)
    )
    own_got = flip("feat", 2)(own_sent)
    neigh, neigh_sent = local_call(
        functools.partial(first_kernel, 0), "neigh_first", pair(far, 2), (neigh_kept, neigh_got)
    )
    neigh_got = flip("feat", 4)(neigh_sent)
    own, own_sent = local_call(second_kernel, "own_second", pair(far), (own, own_got))
    own_got = flip("feat", 4)(own_sent)
    neigh, neigh_sent = local_call(second_kernel, "neigh_second", pair(far), (neigh, neigh_got))
    neigh_got = flip("feat", 2)(neigh_sent)
    out = jax.ShapeDtypeStruct((depth, hid), f32)
    last = (*finish_sum(own, own_got), *finish_sum(neigh, neigh_got))
    return local_call(last_sum_kernel, "last_sum", [out, out], last)


def on_device(
    features,
    self_weight,
    neighbour_weight,
    cotangent,
    send_rows,
    send_count,
    tile_source,
    tile_kind,
    tile_patterns,
):
    feat, dom = lax.axis_size("feat"), lax.axis_size("dom")
    count, depth = features.shape
    rows = count // feat
    hid = self_weight.shape[1]
    columns = features.T
    quarters, below = 4, feat // 4
    row_bits = list(reversed(bits_of(below)))
    picked, across, *cuts = open_exchange(
        send_count, columns, self_weight, neighbour_weight, send_rows, quarters
    )
    came = flip("feat", row_bits[0])(across)
    near = {i: flip("feat", i * below)(cuts[i]) for i in (3, 2, 1)}
    near = [cuts[0], near[1], near[2], near[3]]
    if dom == 2:
        halo = flip("dom", 1)(picked)
    else:
        halo = lax.all_to_all(picked, "dom", 1, 1, tiled=True)
    means = neighbour_means(
        tile_source[0].T, tile_kind[0].T, send_count, columns, halo, send_rows, tile_patterns, feat
    )
    came, means = lax.optimization_barrier((came, means))
    leaving = [came[0:1], relayed(came, near[2]), came[2:3], came[3:4]]
    far = leaving[:1] + [flip("feat", i * below)(leaving[i]) for i in range(1, quarters)]
    row_masks = [i * below for i in range(quarters)]
    pieces = [weight_pieces(near[:3], hid), weight_pieces(far[1:2], hid)]
    weight_masks = list(row_masks)
    row_masks = row_masks + flipped(row_masks, row_bits[0])
    for bit in row_bits[:-1]:
        pieces = pieces + [flip("feat", bit)(p) for p in pieces]
        weight_masks = weight_masks + flipped(weight_masks, bit)
    means, near, far, pieces = lax.optimization_barrier((means, near, far, pieces))
    own_mean = lax.all_to_all(means, "feat", 0, 0, tiled=True)
    pieces, weight_masks = [gathered(pieces)], [weight_masks]
    others = [flip("dom", 1)(p) for p in pieces]
    parts, width = [*near, *far], came.shape[2]
    for bit in row_bits[1:]:
        sent, kept = cut_rows(bit, parts, width)
        parts, width = [kept, flip("feat", bit)(sent)], width // 2
        row_masks = row_masks + flipped(row_masks, bit)
    pieces = pieces + [flip("feat", 1)(p) for p in pieces]
    others = others + [flip("feat", 1)(p) for p in others]
    weight_masks = weight_masks + [flipped(m, 1) for m in weight_masks]
    linear, beside = local_call(
        functools.partial(own_linear_kernel, row_masks, weight_masks),
        "own_linear",
        [
            jax.ShapeDtypeStruct((rows, hid), f32),
            jax.ShapeDtypeStruct((feat * depth + rows, hid), bf16),
        ],
        (*parts, *pieces, *others, cotangent),
    )
    square = jax.ShapeDtypeStruct((rows, hid), bf16)
    sums = (feat // 2, depth, hid)
    sums = [jax.ShapeDtypeStruct(sums, bf16), jax.ShapeDtypeStruct(sums, f32)]
    hidden, grad_linear, own_sent, own_kept = local_call(
        functools.partial(forward_kernel, row_masks, sum(weight_masks, [])),
        "forward",
        [square, square, *sums],
        (own_mean, beside, linear, *parts),
        scratch=[pltpu.VMEM((rows, hid), f32)],
    )
    own_got = flip("feat", 1)(own_sent)
    neigh_sent, neigh_kept = local_call(
        neighbour_sums_kernel, "neighbour_sums", sums, (own_mean, grad_linear)
    )
    neigh_got = flip("feat", 1)(neigh_sent)
    grad_self, grad_neighbour = sum_gradients(own_kept, own_got, neigh_kept, neigh_got)
    return (hidden, grad_self, grad_neighbour)


def solution(mesh):
    placed = (
        P("dom", "feat"),
        P("feat", None),
        P("feat", None),
        P(("dom", "feat"), None),
        P(),
        P(),
        P("dom", None, None),
        P("dom", None, None),
        P(),
    )
    return jax.shard_map(
        on_device,
        mesh=mesh,
        in_specs=placed,
        out_specs=(P(("dom", "feat"), None), P("feat", None), P("feat", None)),
        check_vma=False,
    )
```
